256 devices in a mesh: tri: 256 (over y, z, x, core).
Axes of the slice: x: 4, y: 4, z: 8, core: 2. Of those that a mesh axis runs over, the one named last changes fastest.
Arguments:
- tiles: float32 [8192, 128, 128], P('tri')
- tile_rows: int32 [8192], P('tri'), may hold values from 0 to 1023, as said below
- tile_cols: int32 [8192], P('tri'), may hold values from 0 to 1023, as said below
- counts: int32 [256], P('tri'), may hold values from 0 to 32, as said below
- block_vectors: float32 [1024, 8, 128], P('tri'), may hold values from -6 to 6
Outputs:
- image: float32 [1024, 8, 128], P('tri')
- gram_mixed: float32 [8, 8], replicated
- gram_image: float32 [8, 8], replicated
The draws below stay inside these ranges and needn't reach their ends.
Inputs may be any that keep to these rules, and one draw needn't show every extreme that they name: `tile_rows`: the states are cut into 22 segments, segment i spanning tiles i * 1024 // 22 to (i + 1) * 1024 // 22 - 1. Device d below 253 holds block (i, j), i >= j, of the lower triangle taken row by row (d = i * (i + 1) // 2 + j): its slots name row tiles of segment i and column tiles of segment j, no (row tile, column tile) pair twice; the slots of the remaining devices name tile 0. `tile_cols`: the column tile of a slot is at most its row tile. `counts`: devices past the triangle use no slot; the last block uses all 32.
All inputs are finite; a program needn't handle non-finite values.
Results may differ from the reference program's by a relative error of at most 0.0003.
Values sent between devices are 32-bit elements; how exact they have to be, the bound alone decides.
A program may use at most 64 MiB of HBM per device.

```python
import jax
import jax.numpy as jnp
from jax import lax

TILE = 128
VEC = 8
MAXT = 32
ROWB = 22
NT = 1024
DIM = 131072
N_TRI = 256


def block_of(device_ids):
    marks = jnp.arange(1, ROWB, dtype=jnp.int32)
    bounds = marks * (marks + 1) // 2
    row_block = jnp.sum((bounds[None, :] <= device_ids[:, None]).astype(jnp.int32), axis=1)
    col_block = device_ids - row_block * (row_block + 1) // 2
    return (row_block, col_block)


def placement(key):
    key = jax.random.fold_in(key, 11)
    device_ids = jnp.arange(N_TRI, dtype=jnp.int32)
    blocks = ROWB * (ROWB + 1) // 2
    used = device_ids < blocks
    row_block, col_block = block_of(jnp.minimum(device_ids, blocks - 1))
    row_low = row_block * NT // ROWB
    col_low = col_block * NT // ROWB
    row_size = (row_block + 1) * NT // ROWB - row_low
    col_size = (col_block + 1) * NT // ROWB - col_low
    widest = (NT + ROWB - 1) // ROWB
    positions = jnp.arange(widest * widest, dtype=jnp.int32)
    down = positions // widest
    across = positions % widest
    valid = (down[None, :] < row_size[:, None]) & (across[None, :] < col_size[:, None])
    valid = valid & ((row_block > col_block)[:, None] | (down[None, :] >= across[None, :]))
    scores = jax.random.randint(key, (N_TRI, widest * widest), 0, 4096, dtype=jnp.int32) * (widest * widest)
    scores = scores + positions[None, :] + jnp.where(valid, 0, 2 ** 30).astype(jnp.int32)
    chosen = jnp.argsort(scores, axis=1)[:, :MAXT].astype(jnp.int32)
    rows = jnp.where(used[:, None], row_low[:, None] + chosen // widest, 0)
    cols = jnp.where(used[:, None], col_low[:, None] + chosen % widest, 0)
    return (rows.reshape(-1).astype(jnp.int32), cols.reshape(-1).astype(jnp.int32))


def draw_tile_rows(key, part):
    return placement(key)[0]


def draw_tile_cols(key, part):
    return placement(key)[1]


def draw_counts(key, part):
    key = jax.random.fold_in(key, 5)
    device_ids = jnp.arange(N_TRI, dtype=jnp.int32)
    blocks = ROWB * (ROWB + 1) // 2
    base = MAXT // 4 + 3 * MAXT // 4 * device_ids // max(blocks - 1, 1)
    jitter = jax.random.randint(key, (N_TRI,), 0, MAXT // 4 + 1, dtype=jnp.int32)
    filled = jnp.clip(base - jitter, 1, MAXT)
    filled = jnp.where(device_ids == blocks - 1, MAXT, filled)
    return jnp.where(device_ids < blocks, filled, 0).astype(jnp.int32)


def draw_tiles(key, part):
    key = jax.random.fold_in(key, 7)
    blocks = ROWB * (ROWB + 1) // 2
    device_ids = jnp.arange(N_TRI * MAXT, dtype=jnp.int32) // MAXT
    owner = jnp.minimum(device_ids, blocks - 1).astype(jnp.float32)
    rising = 1.0 + 2.0 * owner / max(blocks - 1, 1)
    spread = (TILE * max(1, MAXT * ROWB * ROWB // NT)) ** (-0.5)
    scale = (rising * spread)[:, None, None]
    shape = (N_TRI * MAXT, TILE, TILE)
    values = jax.random.normal(key, shape, jnp.float32)
    return (values * scale).astype(jnp.float32)


def levels(rng, extent, shards, smallest, high):
    level = 1.0
    for axis_at, shards_of in shards:
        heights = jax.random.uniform(jax.random.fold_in(jax.random.fold_in(rng, 6), axis_at), (shards_of,), jnp.float32, smallest / len(shards), high / len(shards))
        level = level * jnp.repeat(jnp.exp(heights), extent[axis_at] // shards_of).reshape((-1,) + (1,) * (len(extent) - 1 - axis_at))
    return level


def bell_draw(rng, extent, scale, reach, cuts=(), kind=jnp.bfloat16):
    entries = scale * jax.random.normal(rng, extent, jnp.float32)
    if cuts:
        entries = entries * levels(rng, extent, cuts, -0.22, 0.18)
    return jnp.clip(entries, -reach, reach).astype(kind)


def setup_inputs(seed: int = 0) -> dict:
    streams_of = jax.random.split(jax.random.key(seed), 6)
    return {
        "tiles": draw_tiles(jax.random.fold_in(streams_of[5], 71), 0),
        "tile_rows": draw_tile_rows(jax.random.fold_in(streams_of[5], 71), 0),
        "tile_cols": draw_tile_cols(jax.random.fold_in(streams_of[5], 71), 0),
        "counts": draw_counts(jax.random.fold_in(streams_of[5], 71), 0),
        "block_vectors": bell_draw(streams_of[4], (NT, VEC, TILE), 1.0, 6.0, ((0, 256),), jnp.float32),
    }


def reference(tiles, tile_rows, tile_cols, counts, block_vectors):
    highest = lax.Precision.HIGHEST

    def one_device(totals, owner):
        first = owner * MAXT
        tile_list = lax.dynamic_slice_in_dim(tiles, first, MAXT, 0)
        row_ids = lax.dynamic_slice_in_dim(tile_rows, first, MAXT, 0)
        col_ids = lax.dynamic_slice_in_dim(tile_cols, first, MAXT, 0)
        live = (jnp.arange(MAXT, dtype=jnp.int32) < counts[owner]).astype(tiles.dtype)[:, None, None]
        col_vectors = block_vectors[col_ids]
        row_vectors = block_vectors[row_ids]
        row_terms = jnp.einsum('kab,kvb->kva', tile_list, col_vectors, precision=highest) * live
        col_terms = jnp.einsum('kab,kva->kvb', tile_list, row_vectors, precision=highest) * live
        totals = totals.at[row_ids].add(row_terms).at[col_ids].add(col_terms)
        return totals, None

    start = jnp.zeros(block_vectors.shape, block_vectors.dtype)
    image, _ = lax.scan(one_device, start, jnp.arange(N_TRI, dtype=jnp.int32))
    scale = 1.0 / DIM
    gram_mixed = jnp.einsum('tva,twa->vw', block_vectors, image, precision=highest) * scale
    gram_image = jnp.einsum('tva,twa->vw', image, image, precision=highest) * scale
    return image, gram_mixed, gram_image
```

```python
import jax
import jax.numpy as jnp
from jax import lax
from jax.experimental import pallas as pl
from jax.experimental.pallas import tpu as pltpu
from jax.sharding import PartitionSpec as P

MESH = pl.DeviceIdType.MESH
SEGS = 22
TILES = 1024
SHARE = 4
VEC = 8
WIDTH = 128
ROWS = SHARE * VEC
SLOTS = 32
WINDOW = 13
PAD = 64
BLOCKS = SEGS * (SEGS + 1) // 2
DEVICES = 256
NT_DIMS = (((1,), (1,)), ((), ()))
NN_DIMS = (((1,), (0,)), ((), ()))


def seg_low(s):
    return (s * TILES) // SEGS


def seg_of(t):
    return ((t + 1) * SEGS - 1) // TILES


def first_share(s):
    return seg_low(s) // SHARE


def shares(s):
    return (seg_low(s + 1) - 1) // SHARE - first_share(s) + 1


def block_of(d):
    row = 0
    for m in range(1, SEGS):
        row = row + jnp.where(d >= m * (m + 1) // 2, 1, 0)
    col = d - (row * (row + 1)) // 2
    return row, jnp.minimum(col, row)


def member(s, m):
    is_row = m <= s
    dev = jnp.where(is_row, (s * (s + 1)) // 2 + m, (m * (m + 1)) // 2 + s)
    return dev, is_row


def split(a):
    hi = a.astype(jnp.bfloat16)
    lo = (a - hi.astype(jnp.float32)).astype(jnp.bfloat16)
    return hi, lo


def kernel(
    tiles_ref, rows_ref, cols_ref, count_ref, rows_vec, cols_vec, x_ref,
    image_ref, grams_ref,
    tile_buf, hi_buf, lo_buf, xb, row_terms, col_terms, contrib, arrived,
    gram_own, gram_a, gram_b, gram_c,
    tile_sem, gather_send, gather_recv, scatter_send, scatter_recv, gram_send, gram_recv,
):
    me = lax.axis_index("tri")
    row, col = block_of(me)
    works = me < BLOCKS
    diagonal = row == col
    seg_a = seg_of(SHARE * me)
    seg_b = seg_of(SHARE * me + SHARE - 1)
    two = seg_b > seg_a

    tile_copy = pltpu.make_async_copy(tiles_ref, tile_buf, tile_sem)
    tile_copy.start()

    barrier = pltpu.get_barrier_semaphore()

    def greet(dev):
        pl.semaphore_signal(barrier, inc=1, device_id=(dev,), device_id_type=MESH)

    def greet_segment(s):
        def body(p, _):
            dev = first_share(s) + p

            @pl.when(dev != me)
            def _():
                greet(dev)

            return 0

        lax.fori_loop(0, shares(s), body, 0)

    @pl.when(works)
    def _():
        greet_segment(row)

        @pl.when(jnp.logical_not(diagonal))
        def _():
            greet_segment(col)

    base_a = (me // 8) * 8
    base_b = (me // 64) * 64 + me % 8
    base_c = me % 64
    groups = ((base_a, 1, 8), (base_b, 8, 8), (base_c, 64, 4))
    for base, stride, size in groups:
        for q in range(size):
            dev = base + q * stride

            @pl.when(dev != me)
            def _():
                greet(dev)

    def is_member(s):
        return jnp.logical_and(works, jnp.logical_or(row == s, col == s))

    expected = 17 + SEGS - jnp.where(is_member(seg_a), 1, 0)
    expected = expected + jnp.where(two, SEGS - jnp.where(is_member(seg_b), 1, 0), 0)
    pl.semaphore_wait(barrier, expected)

    def gather_copy(s, m, w):
        dev, is_row = member(s, m)
        which = jnp.where(is_row, 0, 1)
        dst = xb.at[which, pl.ds((me - first_share(s)) * SHARE, SHARE)]
        remote = pltpu.make_async_remote_copy(
            src_ref=x_ref, dst_ref=dst, send_sem=gather_send.at[w * SEGS + m],
            recv_sem=gather_recv.at[which], device_id=(dev,), device_id_type=MESH,
        )
        local = pltpu.make_async_copy(x_ref, dst, gather_recv.at[which])
        return dev, remote, local

    def gather_segment(s, w):
        def body(m, _):
            dev, remote, local = gather_copy(s, m, w)

            @pl.when(dev != me)
            def _():
                remote.start()

            @pl.when(dev == me)
            def _():
                local.start()

            return 0

        lax.fori_loop(0, SEGS, body, 0)

    gather_segment(seg_a, 0)

    @pl.when(two)
    def _():
        gather_segment(seg_b, 1)

    tile_copy.wait()

    def split_tile(k, _):
        hi, lo = split(tile_buf[k])
        hi_buf[k] = hi
        lo_buf[k] = lo
        return 0

    lax.fori_loop(0, SLOTS, split_tile, 0)

    def wait_rows(s, which):
        for n in (WINDOW - 1, WINDOW):
            @pl.when(shares(s) == n)
            def _():
                view = xb.at[which, pl.ds(0, n * SHARE)]
                pltpu.make_async_copy(view, view, gather_recv.at[which]).wait()

    @pl.when(works)
    def _():
        wait_rows(row, 0)

        @pl.when(jnp.logical_not(diagonal))
        def _():
            wait_rows(col, 1)

        row_base = SHARE * first_share(row)
        col_base = SHARE * first_share(col)
        col_which = jnp.where(diagonal, 0, 1)

        def operand(which, tile, base):
            hi, lo = split(xb[which, jnp.clip(tile - base, 0, WINDOW * SHARE - 1)])
            both = jnp.concatenate([hi, lo], axis=0)
            return jnp.concatenate([both, both], axis=1)

        def one_slot(k):
            x_col = operand(col_which, cols_ref[k], col_base)
            x_row = operand(0, rows_ref[k], row_base)
            hi, lo = hi_buf[k], lo_buf[k]
            by_row = lax.dot_general(
                x_col, jnp.concatenate([hi, lo], axis=1), NT_DIMS,
                preferred_element_type=jnp.float32,
            )
            by_col = lax.dot_general(
                x_row, jnp.concatenate([hi, lo], axis=0), NN_DIMS,
                preferred_element_type=jnp.float32,
            )
            at = pl.ds(pl.multiple_of(k * VEC, VEC), VEC)
            row_terms[at, :] = by_row[:VEC] + by_row[VEC:]
            col_terms[at, :] = by_col[:VEC] + by_col[VEC:]

        def four_slots(n, _):
            for u in range(4):
                one_slot(4 * n + u)
            return 0

        lax.fori_loop(0, SLOTS // 4, four_slots, 0)

        live = lax.broadcasted_iota(jnp.int32, (PAD, SLOTS), 1) < count_ref[0]
        place = lax.broadcasted_iota(jnp.int32, (PAD, SLOTS), 0)

        def chooser(vec, base):
            hit = jnp.logical_and(place == vec[...] - base, live)
            hot = hit.astype(jnp.float32).astype(jnp.bfloat16)
            return jnp.concatenate([hot, hot], axis=1)

        row_hot = chooser(rows_vec, row_base)
        col_hot = chooser(cols_vec, col_base)

        def reduced(hot, terms, v):
            hi, lo = split(terms[pl.ds(v, SLOTS, stride=VEC), :])
            return lax.dot_general(
                hot, jnp.concatenate([hi, lo], axis=0), NN_DIMS,
                preferred_element_type=jnp.float32,
            )

        for v in range(VEC):
            to_row = reduced(row_hot, row_terms, v)
            to_col = reduced(col_hot, col_terms, v)
            contrib[0, pl.ds(v, PAD, stride=VEC), :] = to_row + jnp.where(diagonal, to_col, 0.0)
            contrib[1, pl.ds(v, PAD, stride=VEC), :] = to_col

        def scatter_segment(s, which, m, start):
            def body(p, _):
                owner = first_share(s) + p
                second = jnp.where(seg_of(SHARE * owner) == s, 0, 1)
                src = contrib.at[which, pl.ds(pl.multiple_of(p * ROWS, ROWS), ROWS), :]
                dst = arrived.at[second, m]
                sem = scatter_recv.at[second]
                remote = pltpu.make_async_remote_copy(
                    src_ref=src, dst_ref=dst, send_sem=scatter_send.at[which * WINDOW + p],
                    recv_sem=sem, device_id=(owner,), device_id_type=MESH,
                )
                local = pltpu.make_async_copy(src, dst, sem)

                @pl.when(owner != me)
                def _():
                    if start:
                        remote.start()
                    else:
                        remote.wait_send()

                if start:
                    @pl.when(owner == me)
                    def _():
                        local.start()

                return 0

            lax.fori_loop(0, shares(s), body, 0)

        scatter_segment(row, 0, col, True)

        @pl.when(jnp.logical_not(diagonal))
        def _():
            scatter_segment(col, 1, row, True)

        scatter_segment(row, 0, col, False)

        @pl.when(jnp.logical_not(diagonal))
        def _():
            scatter_segment(col, 1, row, False)

    def collect(second, start):
        view = arrived.at[second]
        pltpu.make_async_copy(view, view, scatter_recv.at[second]).wait()
        return lax.fori_loop(0, SEGS, lambda m, acc: acc + arrived[second, m], start)

    def put(total):
        for t in range(SHARE):
            image_ref[t] = total[t * VEC:(t + 1) * VEC]

    put(collect(0, jnp.zeros((ROWS, WIDTH), jnp.float32)))

    @pl.when(two)
    def _():
        put(collect(1, jnp.concatenate([image_ref[t] for t in range(SHARE)], axis=0)))

    def flat(ref):
        return jnp.concatenate([ref[t] for t in range(SHARE)], axis=1)

    image = flat(image_ref)
    both = jnp.concatenate([flat(x_ref), image], axis=0)
    gram_own[0] = jnp.zeros((2 * VEC, WIDTH), jnp.float32)
    gram_own[0, :, 0:VEC] = lax.dot_general(
        both, image, NT_DIMS, precision=lax.Precision.HIGHEST, preferred_element_type=jnp.float32
    )

    for n, (buf, (base, stride, size)) in enumerate(zip((gram_a, gram_b, gram_c), groups)):
        rank = (me - base) // stride
        buf[rank] = gram_own[n]

        def swap(q, n=n, buf=buf, base=base, stride=stride, rank=rank):
            dev = base + q * stride
            return dev, pltpu.make_async_remote_copy(
                src_ref=gram_own.at[n], dst_ref=buf.at[rank], send_sem=gram_send.at[n * 8 + q],
                recv_sem=gram_recv.at[n], device_id=(dev,), device_id_type=MESH,
            )

        for q in range(size):
            dev, copy = swap(q)

            @pl.when(dev != me)
            def _():
                copy.start()

        view = buf.at[pl.ds(0, size - 1)]
        pltpu.make_async_copy(view, view, gram_recv.at[n]).wait()
        total = buf[0]
        for q in range(1, size):
            total = total + buf[q]
        if n < 2:
            gram_own[n + 1] = total
        else:
            grams_ref[...] = total * (1.0 / (TILES * WIDTH))
        for q in range(size):
            dev, copy = swap(q)

            @pl.when(dev != me)
            def _():
                copy.wait_send()

    def finish_segment(s, w):
        def body(m, _):
            dev, remote, _local = gather_copy(s, m, w)

            @pl.when(dev != me)
            def _():
                remote.wait_send()

            return 0

        lax.fori_loop(0, SEGS, body, 0)

    finish_segment(seg_a, 0)

    @pl.when(two)
    def _():
        finish_segment(seg_b, 1)


def per_device(tiles, tile_rows, tile_cols, counts, block_vectors):
    f32 = jnp.float32
    vmem = pl.BlockSpec(memory_space=pltpu.VMEM)
    smem = pl.BlockSpec(memory_space=pltpu.SMEM)
    image, grams = pl.pallas_call(
        kernel,
        out_shape=(
            jax.ShapeDtypeStruct((SHARE, VEC, WIDTH), f32),
            jax.ShapeDtypeStruct((2 * VEC, WIDTH), f32),
        ),
        in_specs=[pl.BlockSpec(memory_space=pl.ANY), smem, smem, smem, vmem, vmem, vmem],
        out_specs=(vmem, vmem),
        scratch_shapes=[
            pltpu.VMEM((SLOTS, WIDTH, WIDTH), f32),
            pltpu.VMEM((SLOTS, WIDTH, WIDTH), jnp.bfloat16),
            pltpu.VMEM((SLOTS, WIDTH, WIDTH), jnp.bfloat16),
            pltpu.VMEM((2, WINDOW * SHARE, VEC, WIDTH), f32),
            pltpu.VMEM((SLOTS * VEC, WIDTH), f32),
            pltpu.VMEM((SLOTS * VEC, WIDTH), f32),
            pltpu.VMEM((2, PAD * VEC, WIDTH), f32),
            pltpu.VMEM((2, SEGS, ROWS, WIDTH), f32),
            pltpu.VMEM((3, 2 * VEC, WIDTH), f32),
            pltpu.VMEM((8, 2 * VEC, WIDTH), f32),
            pltpu.VMEM((8, 2 * VEC, WIDTH), f32),
            pltpu.VMEM((4, 2 * VEC, WIDTH), f32),
            pltpu.SemaphoreType.DMA,
            pltpu.SemaphoreType.DMA((2 * SEGS,)),
            pltpu.SemaphoreType.DMA((2,)),
            pltpu.SemaphoreType.DMA((2 * WINDOW,)),
            pltpu.SemaphoreType.DMA((2,)),
            pltpu.SemaphoreType.DMA((24,)),
            pltpu.SemaphoreType.DMA((3,)),
        ],
        compiler_params=pltpu.CompilerParams(
            collective_id=0, has_side_effects=True, vmem_limit_bytes=32 * 1024 * 1024
        ),
    )(
        tiles, tile_rows, tile_cols, counts, tile_rows.reshape(1, SLOTS),
        tile_cols.reshape(1, SLOTS), block_vectors,
    )
    return image, grams[:VEC, :VEC], grams[VEC:, :VEC]


def solution(mesh):
    placed = (P("tri", None, None), P("tri"), P("tri"), P("tri"), P("tri", None, None))
    return jax.shard_map(
        per_device,
        mesh=mesh,
        in_specs=placed,
        out_specs=(P("tri", None, None), P(), P()),
        check_vma=False,
    )
```

```python
import jax
import jax.numpy as jnp
from jax import lax
from jax.experimental import pallas as pl
from jax.experimental.pallas import tpu as pltpu
from jax.sharding import PartitionSpec as P

MESH = pl.DeviceIdType.MESH
SEGS = 22
TILES = 1024
SHARE = 4
VEC = 8
WIDTH = 128
ROWS = SHARE * VEC
SLOTS = 32
WINDOW = 13
PAD = 64
BLOCKS = SEGS * (SEGS + 1) // 2
GROUP = 8
CIRCLE = 16
KEYS = 4
NT_DIMS = (((1,), (1,)), ((), ()))
NN_DIMS = (((1,), (0,)), ((), ()))


def seg_low(s):
    return (s * TILES) // SEGS


def seg_of(t):
    return ((t + 1) * SEGS - 1) // TILES


def first_share(s):
    return seg_low(s) // SHARE


def shares(s):
    return (seg_low(s + 1) - 1) // SHARE - first_share(s) + 1


def tri(s):
    return (s * (s + 1)) // 2


def row_of(d):
    row = 0
    for m in range(1, SEGS):
        row = row + jnp.where(d >= m * (m + 1) // 2, 1, 0)
    return row


def first_group(s):
    return tri(s) // GROUP


def groups_of(s):
    return (tri(s) + s) // GROUP - first_group(s) + 1


def split(a):
    hi = a.astype(jnp.bfloat16)
    lo = (a - hi.astype(jnp.float32)).astype(jnp.bfloat16)
    return hi, lo


def kernel(
    tiles_ref, rows_hbm, cols_hbm, rows_hbm2, cols_hbm2, count_hbm, x_hbm,
    image_ref, grams_ref,
    tile_buf, hi_buf, lo_buf, x_ref, rows_ref, cols_ref, rows_vec, cols_vec, count_ref,
    x_row, x_col, relay_buf, row_terms, col_terms, contrib, part_buf, part_sum, arrived,
    gram_own, gram_a, gram_b,
    in_sem, relay_send, relay_recv, pass_send, gather_send, gather_recv,
    part_send, part_recv, sum_send, col_send, arrive_recv, gram_send, gram_recv,
):
    me = lax.axis_index("tri")
    residue = me % GROUP
    group = me // GROUP
    base = group * GROUP
    works = me < BLOCKS
    row = row_of(me)
    col = jnp.minimum(me - tri(row), row)
    off_diagonal = jnp.logical_and(works, row > col)
    on_diagonal = jnp.logical_and(works, row == col)
    top = row_of(base)
    rows_here = row_of(jnp.minimum(base + GROUP - 1, BLOCKS - 1)) - top + 1
    seg_a = seg_of(SHARE * me)
    seg_b = seg_of(SHARE * me + SHARE - 1)
    two = seg_b > seg_a

    loads = [
        pltpu.make_async_copy(src, dst, in_sem.at[n])
        for n, (src, dst) in enumerate((
            (x_hbm, x_ref), (tiles_ref, tile_buf), (rows_hbm, rows_ref), (cols_hbm, cols_ref),
            (rows_hbm2, rows_vec), (cols_hbm2, cols_vec), (count_hbm, count_ref),
        ))
    ]
    for load in loads:
        load.start()

    def loop(n, body):
        def step(i, _):
            body(i)
            return 0

        lax.fori_loop(0, n, step, 0)

    def owned(body):
        body(seg_a, 0)

        @pl.when(two)
        def _():
            body(seg_b, 1)

    def relayed(body):
        def each(n):
            s = top + n
            start = (residue - first_share(s) % GROUP + GROUP) % GROUP
            for turn in range(2):
                p = start + GROUP * turn

                @pl.when(p < shares(s))
                def _():
                    body(s, p, s % KEYS, turn)

        loop(rows_here, each)

    def members(s, body):
        low = jnp.maximum(tri(s), base)
        high = jnp.minimum(tri(s) + s, base + GROUP - 1)
        loop(high - low + 1, lambda i: body(low + i))

    def send(src, dst, send_sem, recv_sem, dev):
        @pl.when(dev != me)
        def _():
            pltpu.make_async_remote_copy(
                src_ref=src, dst_ref=dst, send_sem=send_sem, recv_sem=recv_sem,
                device_id=(dev,), device_id_type=MESH,
            ).start()

        @pl.when(dev == me)
        def _():
            pltpu.make_async_copy(src, dst, recv_sem).start()

    def sent(src, send_sem, dev):
        @pl.when(dev != me)
        def _():
            pltpu.make_async_copy(src, src, send_sem).wait()

    def landed(dst, recv_sem):
        pltpu.make_async_copy(dst, dst, recv_sem).wait()

    barrier = pltpu.get_barrier_semaphore()

    def greet(dev):
        @pl.when(dev != me)
        def _():
            pl.semaphore_signal(barrier, inc=1, device_id=(dev,), device_id_type=MESH)

    @pl.when(off_diagonal)
    def _():
        loop(shares(col), lambda p: greet(first_share(col) + p))

    relayed(lambda s, p, key, turn: greet(first_share(s) + p))

    core, x, z, y = me % 2, residue // 2, group % 8, me // 64

    def device(y, z, x, core):
        return ((y * 8 + z) * 4 + x) * 2 + core

    for q in range(GROUP):
        greet(base + q)
    for dz in range(1, 8):
        for q in range(2):
            greet(device(y, (z + dz) % 8, x, q))
    for dy in range(1, 4):
        for q in range(4):
            greet(device((y + dy) % 4, z, q, core))

    def greeters(s):
        mine = jnp.logical_and(group >= first_group(s), group < first_group(s) + groups_of(s))
        n = groups_of(s) - jnp.where(mine, 1, 0)
        return n + SEGS - 1 - s - jnp.where(jnp.logical_and(off_diagonal, col == s), 1, 0)

    pl.semaphore_wait(barrier, 33 + greeters(seg_a) + jnp.where(two, greeters(seg_b), 0))
    loads[0].wait()

    def to_relays(start):
        def body(s, w):
            turn = (me - first_share(s)) // GROUP
            dst, sem = relay_buf.at[s % KEYS, turn], relay_recv.at[s % KEYS, turn]

            def each(n):
                dev = (first_group(s) + n) * GROUP + residue
                if start:
                    send(x_ref, dst, relay_send.at[w * KEYS + n], sem, dev)
                else:
                    sent(x_ref, relay_send.at[w * KEYS + n], dev)

            loop(groups_of(s), each)

        return body

    def to_columns(start):
        def body(s, w):
            dst = x_col.at[pl.ds((me - first_share(s)) * SHARE, SHARE)]

            def each(n):
                dev = tri(s + 1 + n) + s
                if start:
                    send(x_ref, dst, gather_send.at[w * SEGS + n], gather_recv.at[1], dev)
                else:
                    sent(x_ref, gather_send.at[w * SEGS + n], dev)

            loop(SEGS - 1 - s, each)

        return body

    owned(to_relays(True))
    owned(to_columns(True))

    for load in loads[1:]:
        load.wait()

    def split_tile(k):
        hi, lo = split(tile_buf[k])
        hi_buf[k] = hi
        lo_buf[k] = lo

    loop(SLOTS, split_tile)

    def pass_on(start):
        def body(s, p, key, turn):
            src = relay_buf.at[key, turn]
            dst = x_row.at[pl.ds(p * SHARE, SHARE)]
            if start:
                landed(src, relay_recv.at[key, turn])

            def each(dev):
                sem = pass_send.at[key, turn, dev % GROUP]
                if start:
                    send(src, dst, sem, gather_recv.at[0], dev)
                else:
                    sent(src, sem, dev)

            members(s, each)

        return body

    relayed(pass_on(True))

    def wait_rows(s, held, recv_sem):
        for n in (WINDOW - 1, WINDOW):
            @pl.when(shares(s) == n)
            def _():
                landed(held.at[pl.ds(0, n * SHARE)], recv_sem)

    def wait_row():
        wait_rows(row, x_row, gather_recv.at[0])

    row_base = SHARE * first_share(row)
    col_base = SHARE * first_share(col)

    def multiply(held, ids, origin, terms, axis, dims):
        def one(k):
            hi, lo = split(held[jnp.clip(ids[k] - origin, 0, WINDOW * SHARE - 1)])
            both = jnp.concatenate([hi, lo], axis=0)
            out = lax.dot_general(
                jnp.concatenate([both, both], axis=1),
                jnp.concatenate([hi_buf[k], lo_buf[k]], axis=axis), dims,
                preferred_element_type=jnp.float32,
            )
            terms[pl.ds(pl.multiple_of(k * VEC, VEC), VEC), :] = out[:VEC] + out[VEC:]

        def several(n):
            for u in range(8):
                one(8 * n + u)

        loop(SLOTS // 8, several)

    def reduce(vec, origin, terms, which):
        live = lax.broadcasted_iota(jnp.int32, (PAD, SLOTS), 1) < count_ref[0]
        place = lax.broadcasted_iota(jnp.int32, (PAD, SLOTS), 0)
        hit = jnp.logical_and(place == vec[...] - origin, live)
        hot = hit.astype(jnp.float32).astype(jnp.bfloat16)
        hot = jnp.concatenate([hot, hot], axis=1)
        for v in range(VEC):
            hi, lo = split(terms[pl.ds(v, SLOTS, stride=VEC), :])
            contrib[which, pl.ds(v, PAD, stride=VEC), :] = lax.dot_general(
                hot, jnp.concatenate([hi, lo], axis=0), NN_DIMS,
                preferred_element_type=jnp.float32,
            )

    def chunk(which, p):
        return contrib.at[which, pl.ds(pl.multiple_of(p * ROWS, ROWS), ROWS), :]

    def row_parts(start):
        def each(p):
            dev = base + (first_share(row) + p) % GROUP
            if start:
                turn = p // GROUP
                send(
                    chunk(0, p), part_buf.at[row % KEYS, turn, residue], part_send.at[p],
                    part_recv.at[row % KEYS, turn, residue], dev,
                )
            else:
                sent(chunk(0, p), part_send.at[p], dev)

        loop(shares(row), each)

    def place_of(owner, s):
        return jnp.where(seg_of(SHARE * owner) == s, 0, 1)

    def col_parts(start):
        def each(p):
            owner = first_share(col) + p
            if start:
                second = place_of(owner, col)
                send(
                    chunk(1, p), arrived.at[second, KEYS + row], col_send.at[p],
                    arrive_recv.at[second, KEYS + row], owner,
                )
            else:
                sent(chunk(1, p), col_send.at[p], owner)

        loop(shares(col), each)

    @pl.when(works)
    def _():
        @pl.when(off_diagonal)
        def _():
            wait_rows(col, x_col, gather_recv.at[1])
            multiply(x_col, cols_ref, col_base, row_terms, 1, NT_DIMS)

        @pl.when(on_diagonal)
        def _():
            wait_row()
            multiply(x_row, cols_ref, col_base, row_terms, 1, NT_DIMS)

        reduce(rows_vec, row_base, row_terms, 0)

        @pl.when(off_diagonal)
        def _():
            row_parts(True)
            wait_row()

        multiply(x_row, rows_ref, row_base, col_terms, 0, NN_DIMS)
        reduce(cols_vec, col_base, col_terms, 1)

        @pl.when(off_diagonal)
        def _():
            col_parts(True)

        @pl.when(on_diagonal)
        def _():
            contrib[0] = contrib[0] + contrib[1]
            row_parts(True)

    owned(to_relays(False))
    owned(to_columns(False))
    relayed(pass_on(False))

    def add_parts(start):
        def body(s, p, key, turn):
            owner = first_share(s) + p
            src = part_sum.at[key, turn]
            if start:
                low = jnp.maximum(tri(s), base)
                high = jnp.minimum(tri(s) + s, base + GROUP - 1)

                def each(i, total):
                    rank = (low + i) % GROUP
                    landed(part_buf.at[key, turn, rank], part_recv.at[key, turn, rank])
                    return total + part_buf[key, turn, rank]

                part_sum[key, turn] = lax.fori_loop(
                    0, high - low + 1, each, jnp.zeros((ROWS, WIDTH), jnp.float32)
                )
                second = place_of(owner, s)
                at = group - first_group(s)
                send(
                    src, arrived.at[second, at], sum_send.at[key, turn],
                    arrive_recv.at[second, at], owner,
                )
            else:
                sent(src, sum_send.at[key, turn], owner)

        return body

    relayed(add_parts(True))

    def collect(w, s, total):
        def each(at, total):
            landed(arrived.at[w, at], arrive_recv.at[w, at])
            return total + arrived[w, at]

        total = lax.fori_loop(KEYS + s + 1, KEYS + SEGS, each, total)
        return lax.fori_loop(0, groups_of(s), each, total)

    def put(total):
        for t in range(SHARE):
            image_ref[t] = total[t * VEC:(t + 1) * VEC]

    put(collect(0, seg_a, jnp.zeros((ROWS, WIDTH), jnp.float32)))

    @pl.when(two)
    def _():
        put(collect(1, seg_b, jnp.concatenate([image_ref[t] for t in range(SHARE)], axis=0)))

    def flat(ref):
        return jnp.concatenate([ref[t] for t in range(SHARE)], axis=1)

    image = flat(image_ref)
    both = lax.dot_general(
        jnp.concatenate([flat(x_ref), image], axis=0), image, NT_DIMS,
        precision=lax.Precision.HIGHEST, preferred_element_type=jnp.float32,
    )
    gram_own[0] = jnp.zeros((VEC, WIDTH), jnp.float32)
    gram_own[0, :, 0:VEC] = both[:VEC]
    gram_own[0, :, VEC:2 * VEC] = both[VEC:]

    circles = (
        (gram_a, z * 2 + core, lambda q: device(y, q // 2, x, q % 2)),
        (gram_b, y * 4 + x, lambda q: device(q // 4, z, q % 4, core)),
    )
    for n, (buf, rank, partner) in enumerate(circles):
        for q in range(CIRCLE):
            @pl.when(q != rank)
            def _():
                pltpu.make_async_remote_copy(
                    src_ref=gram_own.at[n], dst_ref=buf.at[rank], send_sem=gram_send.at[n, q],
                    recv_sem=gram_recv.at[n], device_id=(partner(q),), device_id_type=MESH,
                ).start()

        buf[rank] = gram_own[n]
        if n == 0:
            relayed(add_parts(False))

            @pl.when(works)
            def _():
                row_parts(False)

            @pl.when(off_diagonal)
            def _():
                col_parts(False)

        landed(buf.at[pl.ds(0, CIRCLE - 1)], gram_recv.at[n])
        terms = [buf[q] for q in range(CIRCLE)]
        while len(terms) > 1:
            terms = [a + b for a, b in zip(terms[::2], terms[1::2])]
        if n == 0:
            gram_own[1] = terms[0]
        else:
            grams_ref[...] = terms[0] * (1.0 / (TILES * WIDTH))

    for n, (_buf, rank, _partner) in enumerate(circles):
        for q in range(CIRCLE):
            @pl.when(q != rank)
            def _():
                pltpu.make_async_copy(gram_own.at[n], gram_own.at[n], gram_send.at[n, q]).wait()


def per_device(tiles, tile_rows, tile_cols, counts, block_vectors):
    f32, i32 = jnp.float32, jnp.int32
    vmem = pl.BlockSpec(memory_space=pltpu.VMEM)
    dma = pltpu.SemaphoreType.DMA
    image, grams = pl.pallas_call(
        kernel,
        out_shape=(
            jax.ShapeDtypeStruct((SHARE, VEC, WIDTH), f32),
            jax.ShapeDtypeStruct((VEC, WIDTH), f32),
        ),
        in_specs=[pl.BlockSpec(memory_space=pl.ANY)] * 7,
        out_specs=(vmem, vmem),
        scratch_shapes=[
            pltpu.VMEM((SLOTS, WIDTH, WIDTH), f32),
            pltpu.VMEM((SLOTS, WIDTH, WIDTH), jnp.bfloat16),
            pltpu.VMEM((SLOTS, WIDTH, WIDTH), jnp.bfloat16),
            pltpu.VMEM((SHARE, VEC, WIDTH), f32),
            pltpu.SMEM((SLOTS,), i32),
            pltpu.SMEM((SLOTS,), i32),
            pltpu.VMEM((1, SLOTS), i32),
            pltpu.VMEM((1, SLOTS), i32),
            pltpu.SMEM((1,), i32),
            pltpu.VMEM((WINDOW * SHARE, VEC, WIDTH), f32),
            pltpu.VMEM((WINDOW * SHARE, VEC, WIDTH), f32),
            pltpu.VMEM((KEYS, 2, SHARE, VEC, WIDTH), f32),
            pltpu.VMEM((SLOTS * VEC, WIDTH), f32),
            pltpu.VMEM((SLOTS * VEC, WIDTH), f32),
            pltpu.VMEM((2, PAD * VEC, WIDTH), f32),
            pltpu.VMEM((KEYS, 2, GROUP, ROWS, WIDTH), f32),
            pltpu.VMEM((KEYS, 2, ROWS, WIDTH), f32),
            pltpu.VMEM((2, KEYS + SEGS, ROWS, WIDTH), f32),
            pltpu.VMEM((2, VEC, WIDTH), f32),
            pltpu.VMEM((CIRCLE, VEC, WIDTH), f32),
            pltpu.VMEM((CIRCLE, VEC, WIDTH), f32),
            dma((7,)),
            dma((2 * KEYS,)),
            dma((KEYS, 2)),
            dma((KEYS, 2, GROUP)),
            dma((2 * SEGS,)),
            dma((2,)),
            dma((WINDOW,)),
            dma((KEYS, 2, GROUP)),
            dma((KEYS, 2)),
            dma((WINDOW,)),
            dma((2, KEYS + SEGS)),
            dma((2, CIRCLE)),
            dma((2,)),
        ],
        compiler_params=pltpu.CompilerParams(
            collective_id=0, has_side_effects=True, vmem_limit_bytes=60 * 1024 * 1024
        ),
    )(
        tiles, tile_rows, tile_cols, tile_rows.reshape(1, SLOTS), tile_cols.reshape(1, SLOTS),
        counts, block_vectors,
    )
    return image, grams[:, :VEC], grams[:, VEC:2 * VEC]


def solution(mesh):
    placed = (P("tri", None, None), P("tri"), P("tri"), P("tri"), P("tri", None, None))
    return jax.shard_map(
        per_device,
        mesh=mesh,
        in_specs=placed,
        out_specs=(P("tri", None, None), P(), P()),
        check_vma=False,
    )
```

```python
import jax
import jax.numpy as jnp
from jax import lax
from jax.experimental import pallas as pl
from jax.experimental.pallas import tpu as pltpu
from jax.sharding import PartitionSpec as P

MESH = pl.DeviceIdType.MESH
SEGS = 22
TILES = 1024
SHARE = 4
VEC = 8
WIDTH = 128
ROWS = SHARE * VEC
SLOTS = 32
WINDOW = 13
PAD = 64
BLOCKS = SEGS * (SEGS + 1) // 2
GROUP = 8
CIRCLE = 16
KEYS = 4
NT_DIMS = (((1,), (1,)), ((), ()))
NN_DIMS = (((1,), (0,)), ((), ()))


def seg_low(s):
    return (s * TILES) // SEGS


def seg_of(t):
    return ((t + 1) * SEGS - 1) // TILES


def first_share(s):
    return seg_low(s) // SHARE


def shares(s):
    return (seg_low(s + 1) - 1) // SHARE - first_share(s) + 1


def tri(s):
    return (s * (s + 1)) // 2


def row_of(d):
    row = 0
    for m in range(1, SEGS):
        row = row + jnp.where(d >= m * (m + 1) // 2, 1, 0)
    return row


def first_group(s):
    return tri(s) // GROUP


def groups_of(s):
    return (tri(s) + s - 1) // GROUP - first_group(s) + 1


def split(a):
    hi = a.astype(jnp.bfloat16)
    lo = (a - hi.astype(jnp.float32)).astype(jnp.bfloat16)
    return hi, lo


def kernel(
    tiles_ref, rows_hbm, cols_hbm, rows_hbm2, cols_hbm2, count_hbm, x_hbm,
    image_ref, grams_ref,
    tile_buf, hi_buf, lo_buf, x_ref, rows_ref, cols_ref, rows_vec, cols_vec, count_ref,
    x_row, x_col, relay_buf, row_terms, col_terms, contrib, part_buf, part_sum, arrived,
    gram_own, gram_a, gram_b,
    in_sem, relay_send, relay_recv, pass_send, gather_send, gather_recv,
    part_send, part_recv, sum_send, col_send, arrive_recv, gram_send, gram_recv,
):
    me = lax.axis_index("tri")
    residue = me % GROUP
    group = me // GROUP
    base = group * GROUP
    works = me < BLOCKS
    row = row_of(me)
    col = jnp.minimum(me - tri(row), row)
    off_diagonal = jnp.logical_and(works, row > col)
    on_diagonal = jnp.logical_and(works, row == col)
    top = row_of(base)
    rows_here = row_of(jnp.minimum(base + GROUP - 1, BLOCKS - 1)) - top + 1
    seg_a = seg_of(SHARE * me)
    seg_b = seg_of(SHARE * me + SHARE - 1)
    two = seg_b > seg_a

    loads = [
        pltpu.make_async_copy(src, dst, in_sem.at[n])
        for n, (src, dst) in enumerate((
            (x_hbm, x_ref), (tiles_ref, tile_buf), (rows_hbm, rows_ref), (cols_hbm, cols_ref),
            (rows_hbm2, rows_vec), (cols_hbm2, cols_vec), (count_hbm, count_ref),
        ))
    ]
    loads[0].start()

    def loop(n, body):
        def step(i, _):
            body(i)
            return 0

        lax.fori_loop(0, n, step, 0)

    def owned(body):
        body(seg_a, 0)

        @pl.when(two)
        def _():
            body(seg_b, 1)

    def span(s):
        low = jnp.maximum(tri(s), base)
        return low, jnp.minimum(tri(s) + s, base + GROUP) - low

    def relayed(body):
        def each(n):
            s = top + n
            start = (residue - first_share(s) % GROUP + GROUP) % GROUP
            for turn in range(2):
                p = start + GROUP * turn

                @pl.when(jnp.logical_and(p < shares(s), span(s)[1] > 0))
                def _():
                    body(s, p, s % KEYS, turn)

        loop(rows_here, each)

    def members(s, body):
        low, count = span(s)
        loop(count, lambda i: body(low + i))

    def send(src, dst, send_sem, recv_sem, dev):
        @pl.when(dev != me)
        def _():
            pltpu.make_async_remote_copy(
                src_ref=src, dst_ref=dst, send_sem=send_sem, recv_sem=recv_sem,
                device_id=(dev,), device_id_type=MESH,
            ).start()

        @pl.when(dev == me)
        def _():
            pltpu.make_async_copy(src, dst, recv_sem).start()

    def sent(src, send_sem, dev):
        @pl.when(dev != me)
        def _():
            pltpu.make_async_copy(src, src, send_sem).wait()

    def landed(dst, recv_sem):
        pltpu.make_async_copy(dst, dst, recv_sem).wait()

    barrier = pltpu.get_barrier_semaphore()

    def greet(dev):
        @pl.when(dev != me)
        def _():
            pl.semaphore_signal(barrier, inc=1, device_id=(dev,), device_id_type=MESH)

    @pl.when(works)
    def _():
        loop(shares(col), lambda p: greet(first_share(col) + p))

    relayed(lambda s, p, key, turn: greet(first_share(s) + p))

    core, x, z, y = me % 2, residue // 2, group % 8, me // 64

    def device(y, z, x, core):
        return ((y * 8 + z) * 4 + x) * 2 + core

    for q in range(GROUP):
        greet(base + q)
    for dz in range(1, 8):
        for q in range(2):
            greet(device(y, (z + dz) % 8, x, q))
    for dy in range(1, 4):
        for q in range(4):
            greet(device((y + dy) % 4, z, q, core))

    for load in loads[1:]:
        load.start()

    def greeters(s):
        mine = jnp.logical_and(group >= first_group(s), group < first_group(s) + groups_of(s))
        n = groups_of(s) - jnp.where(mine, 1, 0)
        return n + SEGS - s - jnp.where(jnp.logical_and(works, col == s), 1, 0)

    pl.semaphore_wait(barrier, 33 + greeters(seg_a) + jnp.where(two, greeters(seg_b), 0))
    loads[0].wait()

    def to_relays(start):
        def body(s, w):
            turn = (me - first_share(s)) // GROUP
            dst, sem = relay_buf.at[s % KEYS, turn], relay_recv.at[s % KEYS, turn]

            def each(n):
                dev = (first_group(s) + n) * GROUP + residue
                if start:
                    send(x_ref, dst, relay_send.at[w * KEYS + n], sem, dev)
                else:
                    sent(x_ref, relay_send.at[w * KEYS + n], dev)

            loop(groups_of(s), each)

        return body

    def to_columns(start):
        def body(s, w):
            dst = x_col.at[pl.ds((me - first_share(s)) * SHARE, SHARE)]

            def each(n):
                dev = tri(s + n) + s
                if start:
                    send(x_ref, dst, gather_send.at[w * SEGS + n], gather_recv.at[1], dev)
                else:
                    sent(x_ref, gather_send.at[w * SEGS + n], dev)

            loop(SEGS - s, each)

        return body

    owned(to_relays(True))
    owned(to_columns(True))

    for load in loads[1:]:
        load.wait()

    def split_tile(k):
        hi, lo = split(tile_buf[k])
        hi_buf[k] = hi
        lo_buf[k] = lo

    loop(SLOTS, split_tile)

    def pass_on(start):
        def body(s, p, key, turn):
            src = relay_buf.at[key, turn]
            dst = x_row.at[pl.ds(p * SHARE, SHARE)]
            if start:
                landed(src, relay_recv.at[key, turn])

            def each(dev):
                sem = pass_send.at[key, turn, dev % GROUP]
                if start:
                    send(src, dst, sem, gather_recv.at[0], dev)
                else:
                    sent(src, sem, dev)

            members(s, each)

        return body

    relayed(pass_on(True))

    def wait_rows(s, held, recv_sem):
        for n in (WINDOW - 1, WINDOW):
            @pl.when(shares(s) == n)
            def _():
                landed(held.at[pl.ds(0, n * SHARE)], recv_sem)

    row_base = SHARE * first_share(row)
    col_base = SHARE * first_share(col)

    def multiply(held, ids, origin, terms, axis, dims):
        def one(k):
            hi, lo = split(held[jnp.clip(ids[k] - origin, 0, WINDOW * SHARE - 1)])
            both = jnp.concatenate([hi, lo], axis=0)
            out = lax.dot_general(
                jnp.concatenate([both, both], axis=1),
                jnp.concatenate([hi_buf[k], lo_buf[k]], axis=axis), dims,
                preferred_element_type=jnp.float32,
            )
            terms[pl.ds(pl.multiple_of(k * VEC, VEC), VEC), :] = out[:VEC] + out[VEC:]

        def several(n):
            for u in range(8):
                one(8 * n + u)

        loop(SLOTS // 8, several)

    def reduce(vec, origin, terms, which):
        live = lax.broadcasted_iota(jnp.int32, (PAD, SLOTS), 1) < count_ref[0]
        place = lax.broadcasted_iota(jnp.int32, (PAD, SLOTS), 0)
        hit = jnp.logical_and(place == vec[...] - origin, live)
        hot = hit.astype(jnp.float32).astype(jnp.bfloat16)
        hot = jnp.concatenate([hot, hot], axis=1)
        for v in range(VEC):
            hi, lo = split(terms[pl.ds(v, SLOTS, stride=VEC), :])
            contrib[which, pl.ds(v, PAD, stride=VEC), :] = lax.dot_general(
                hot, jnp.concatenate([hi, lo], axis=0), NN_DIMS,
                preferred_element_type=jnp.float32,
            )

    def chunk(which, p):
        return contrib.at[which, pl.ds(pl.multiple_of(p * ROWS, ROWS), ROWS), :]

    def row_parts(start):
        def each(p):
            dev = base + (first_share(row) + p) % GROUP
            if start:
                turn = p // GROUP
                send(
                    chunk(0, p), part_buf.at[row % KEYS, turn, residue], part_send.at[p],
                    part_recv.at[row % KEYS, turn, residue], dev,
                )
            else:
                sent(chunk(0, p), part_send.at[p], dev)

        loop(shares(row), each)

    def place_of(owner, s):
        return jnp.where(seg_of(SHARE * owner) == s, 0, 1)

    def col_parts(start):
        def each(p):
            owner = first_share(col) + p
            if start:
                second = place_of(owner, col)
                send(
                    chunk(1, p), arrived.at[second, KEYS + row], col_send.at[p],
                    arrive_recv.at[second, KEYS + row], owner,
                )
            else:
                sent(chunk(1, p), col_send.at[p], owner)

        loop(shares(col), each)

    @pl.when(works)
    def _():
        wait_rows(col, x_col, gather_recv.at[1])
        multiply(x_col, cols_ref, col_base, row_terms, 1, NT_DIMS)
        reduce(rows_vec, row_base, row_terms, 0)

        @pl.when(off_diagonal)
        def _():
            row_parts(True)
            wait_rows(row, x_row, gather_recv.at[0])
            multiply(x_row, rows_ref, row_base, col_terms, 0, NN_DIMS)

        @pl.when(on_diagonal)
        def _():
            multiply(x_col, rows_ref, row_base, col_terms, 0, NN_DIMS)

        reduce(cols_vec, col_base, col_terms, 1)

        @pl.when(on_diagonal)
        def _():
            contrib[1] = contrib[0] + contrib[1]

        col_parts(True)

    owned(to_relays(False))
    owned(to_columns(False))
    relayed(pass_on(False))

    def add_parts(start):
        def body(s, p, key, turn):
            owner = first_share(s) + p
            src = part_sum.at[key, turn]
            if start:
                low, count = span(s)

                def each(i, total):
                    rank = (low + i) % GROUP
                    landed(part_buf.at[key, turn, rank], part_recv.at[key, turn, rank])
                    return total + part_buf[key, turn, rank]

                part_sum[key, turn] = lax.fori_loop(
                    0, count, each, jnp.zeros((ROWS, WIDTH), jnp.float32)
                )
                second = place_of(owner, s)
                at = group - first_group(s)
                send(
                    src, arrived.at[second, at], sum_send.at[key, turn],
                    arrive_recv.at[second, at], owner,
                )
            else:
                sent(src, sum_send.at[key, turn], owner)

        return body

    relayed(add_parts(True))

    def collect(w, s, total):
        def each(at, total):
            landed(arrived.at[w, at], arrive_recv.at[w, at])
            return total + arrived[w, at]

        total = lax.fori_loop(KEYS + s, KEYS + SEGS, each, total)
        return lax.fori_loop(0, groups_of(s), each, total)

    def put(total):
        for t in range(SHARE):
            image_ref[t] = total[t * VEC:(t + 1) * VEC]

    put(collect(0, seg_a, jnp.zeros((ROWS, WIDTH), jnp.float32)))

    @pl.when(two)
    def _():
        put(collect(1, seg_b, jnp.concatenate([image_ref[t] for t in range(SHARE)], axis=0)))

    def flat(ref):
        return jnp.concatenate([ref[t] for t in range(SHARE)], axis=1)

    image = flat(image_ref)
    both = lax.dot_general(
        jnp.concatenate([flat(x_ref), image], axis=0), image, NT_DIMS,
        precision=lax.Precision.HIGHEST, preferred_element_type=jnp.float32,
    )
    gram_own[0] = jnp.zeros((VEC, WIDTH), jnp.float32)
    gram_own[0, :, 0:VEC] = both[:VEC]
    gram_own[0, :, VEC:2 * VEC] = both[VEC:]

    circles = (
        (gram_a, z * 2 + core, lambda q: device(y, q // 2, x, q % 2)),
        (gram_b, y * 4 + x, lambda q: device(q // 4, z, q % 4, core)),
    )
    for n, (buf, rank, partner) in enumerate(circles):
        for q in range(CIRCLE):
            @pl.when(q != rank)
            def _():
                pltpu.make_async_remote_copy(
                    src_ref=gram_own.at[n], dst_ref=buf.at[rank], send_sem=gram_send.at[n, q],
                    recv_sem=gram_recv.at[n], device_id=(partner(q),), device_id_type=MESH,
                ).start()

        buf[rank] = gram_own[n]
        if n == 0:
            relayed(add_parts(False))

            @pl.when(off_diagonal)
            def _():
                row_parts(False)

            @pl.when(works)
            def _():
                col_parts(False)

        landed(buf.at[pl.ds(0, CIRCLE - 1)], gram_recv.at[n])
        terms = [buf[q] for q in range(CIRCLE)]
        while len(terms) > 1:
            terms = [a + b for a, b in zip(terms[::2], terms[1::2])]
        if n == 0:
            gram_own[1] = terms[0]
        else:
            grams_ref[...] = terms[0] * (1.0 / (TILES * WIDTH))

    for n, (_buf, rank, _partner) in enumerate(circles):
        for q in range(CIRCLE):
            @pl.when(q != rank)
            def _():
                pltpu.make_async_copy(gram_own.at[n], gram_own.at[n], gram_send.at[n, q]).wait()


def per_device(tiles, tile_rows, tile_cols, counts, block_vectors):
    f32, i32 = jnp.float32, jnp.int32
    vmem = pl.BlockSpec(memory_space=pltpu.VMEM)
    dma = pltpu.SemaphoreType.DMA
    image, grams = pl.pallas_call(
        kernel,
        out_shape=(
            pltpu.VMEM((SHARE, VEC, WIDTH), f32),
            pltpu.VMEM((VEC, WIDTH), f32),
        ),
        in_specs=[pl.BlockSpec(memory_space=pl.ANY)] * 7,
        out_specs=(vmem, vmem),
        scratch_shapes=[
            pltpu.VMEM((SLOTS, WIDTH, WIDTH), f32),
            pltpu.VMEM((SLOTS, WIDTH, WIDTH), jnp.bfloat16),
            pltpu.VMEM((SLOTS, WIDTH, WIDTH), jnp.bfloat16),
            pltpu.VMEM((SHARE, VEC, WIDTH), f32),
            pltpu.SMEM((SLOTS,), i32),
            pltpu.SMEM((SLOTS,), i32),
            pltpu.VMEM((1, SLOTS), i32),
            pltpu.VMEM((1, SLOTS), i32),
            pltpu.SMEM((1,), i32),
            pltpu.VMEM((WINDOW * SHARE, VEC, WIDTH), f32),
            pltpu.VMEM((WINDOW * SHARE, VEC, WIDTH), f32),
            pltpu.VMEM((KEYS, 2, SHARE, VEC, WIDTH), f32),
            pltpu.VMEM((SLOTS * VEC, WIDTH), f32),
            pltpu.VMEM((SLOTS * VEC, WIDTH), f32),
            pltpu.VMEM((2, PAD * VEC, WIDTH), f32),
            pltpu.VMEM((KEYS, 2, GROUP, ROWS, WIDTH), f32),
            pltpu.VMEM((KEYS, 2, ROWS, WIDTH), f32),
            pltpu.VMEM((2, KEYS + SEGS, ROWS, WIDTH), f32),
            pltpu.VMEM((2, VEC, WIDTH), f32),
            pltpu.VMEM((CIRCLE, VEC, WIDTH), f32),
            pltpu.VMEM((CIRCLE, VEC, WIDTH), f32),
            dma((7,)),
            dma((2 * KEYS,)),
            dma((KEYS, 2)),
            dma((KEYS, 2, GROUP)),
            dma((2 * SEGS,)),
            dma((2,)),
            dma((WINDOW,)),
            dma((KEYS, 2, GROUP)),
            dma((KEYS, 2)),
            dma((WINDOW,)),
            dma((2, KEYS + SEGS)),
            dma((2, CIRCLE)),
            dma((2,)),
        ],
        compiler_params=pltpu.CompilerParams(
            collective_id=0, has_side_effects=True, vmem_limit_bytes=60 * 1024 * 1024
        ),
    )(
        tiles, tile_rows, tile_cols, tile_rows.reshape(1, SLOTS), tile_cols.reshape(1, SLOTS),
        counts, block_vectors,
    )
    return image, grams[:, :VEC], grams[:, VEC:2 * VEC]


def solution(mesh):
    placed = (P("tri", None, None), P("tri"), P("tri"), P("tri"), P("tri", None, None))
    return jax.shard_map(
        per_device,
        mesh=mesh,
        in_specs=placed,
        out_specs=(P("tri", None, None), P(), P()),
        check_vma=False,
    )
```

```python
import jax
import jax.numpy as jnp
from jax import lax
from jax.experimental import pallas as pl
from jax.experimental.pallas import tpu as pltpu
from jax.sharding import PartitionSpec as P

MESH = pl.DeviceIdType.MESH
SEGS = 22
TILES = 1024
SHARE = 4
VEC = 8
WIDTH = 128
ROWS = SHARE * VEC
SLOTS = 32
WINDOW = 13
PAD = 64
BLOCKS = SEGS * (SEGS + 1) // 2
GROUP = 8
LINE = 8
PLANE = 32
KEYS = 4
NT_DIMS = (((1,), (1,)), ((), ()))
NN_DIMS = (((1,), (0,)), ((), ()))


def seg_low(s):
    return (s * TILES) // SEGS


def seg_of(t):
    return ((t + 1) * SEGS - 1) // TILES


def first_share(s):
    return seg_low(s) // SHARE


def shares(s):
    return (seg_low(s + 1) - 1) // SHARE - first_share(s) + 1


def tri(s):
    return (s * (s + 1)) // 2


def row_of(d):
    row = 0
    for m in range(1, SEGS):
        row = row + jnp.where(d >= m * (m + 1) // 2, 1, 0)
    return row


def first_group(s):
    return tri(s) // GROUP


def groups_of(s):
    return (tri(s) + s - 1) // GROUP - first_group(s) + 1


def split(a):
    hi = a.astype(jnp.bfloat16)
    lo = (a - hi.astype(jnp.float32)).astype(jnp.bfloat16)
    return hi, lo


def kernel(
    tiles_ref, rows_hbm, cols_hbm, rows_hbm2, cols_hbm2, count_hbm, x_hbm,
    image_ref, grams_ref,
    tile_buf, hi_buf, lo_buf, x_ref, rows_ref, cols_ref, rows_vec, cols_vec, count_ref,
    x_row, x_col, relay_buf, line_buf, col_buf, col_sum, row_terms, col_terms, contrib, part_buf, part_sum, arrived,
    gram_own, gram_a, gram_b,
    in_sem, relay_send, relay_recv, pass_send, line_send, line_recv, spread_send, gather_recv,
    part_send, part_recv, sum_send, col_send, col_recv, back_send, arrive_recv, gram_send, gram_recv,
):
    me = lax.axis_index("tri")
    residue = me % GROUP
    group = me // GROUP
    base = group * GROUP
    works = me < BLOCKS
    row = row_of(me)
    col = jnp.minimum(me - tri(row), row)
    off_diagonal = jnp.logical_and(works, row > col)
    on_diagonal = jnp.logical_and(works, row == col)
    top = row_of(base)
    rows_here = row_of(jnp.minimum(base + GROUP - 1, BLOCKS - 1)) - top + 1
    seg_a = seg_of(SHARE * me)
    seg_b = seg_of(SHARE * me + SHARE - 1)
    two = seg_b > seg_a

    loads = [
        pltpu.make_async_copy(src, dst, in_sem.at[n])
        for n, (src, dst) in enumerate((
            (x_hbm, x_ref), (tiles_ref, tile_buf), (rows_hbm, rows_ref), (cols_hbm, cols_ref),
            (rows_hbm2, rows_vec), (cols_hbm2, cols_vec), (count_hbm, count_ref),
        ))
    ]
    loads[0].start()

    def loop(n, body):
        def step(i, _):
            body(i)
            return 0

        lax.fori_loop(0, n, step, 0)

    def owned(body):
        body(seg_a, 0)

        @pl.when(two)
        def _():
            body(seg_b, 1)

    def span(s):
        low = jnp.maximum(tri(s), base)
        return low, jnp.minimum(tri(s) + s, base + GROUP) - low

    def relayed(body):
        def each(n):
            s = top + n
            start = (residue - first_share(s) % GROUP + GROUP) % GROUP
            for turn in range(2):
                p = start + GROUP * turn

                @pl.when(jnp.logical_and(p < shares(s), span(s)[1] > 0))
                def _():
                    body(s, p, s % KEYS, turn)

        loop(rows_here, each)

    def members(s, body):
        low, count = span(s)
        loop(count, lambda i: body(low + i))

    def send(src, dst, send_sem, recv_sem, dev):
        @pl.when(dev != me)
        def _():
            pltpu.make_async_remote_copy(
                src_ref=src, dst_ref=dst, send_sem=send_sem, recv_sem=recv_sem,
                device_id=(dev,), device_id_type=MESH,
            ).start()

        @pl.when(dev == me)
        def _():
            pltpu.make_async_copy(src, dst, recv_sem).start()

    def sent(src, send_sem, dev):
        @pl.when(dev != me)
        def _():
            pltpu.make_async_copy(src, src, send_sem).wait()

    def landed(dst, recv_sem):
        pltpu.make_async_copy(dst, dst, recv_sem).wait()

    barrier = pltpu.get_barrier_semaphore()

    def greet(dev):
        @pl.when(dev != me)
        def _():
            pl.semaphore_signal(barrier, inc=1, device_id=(dev,), device_id_type=MESH)

    core, x, z, y = me % 2, residue // 2, group % LINE, me // 64

    def line(zz):
        return (y * LINE + zz) * GROUP + residue

    def plane(q):
        return (q // GROUP * LINE + z) * GROUP + q % GROUP

    for dz in range(1, LINE):
        greet(line((z + dz) % LINE))
    for q in range(PLANE):
        greet(plane(q))
    relayed(lambda s, p, key, turn: greet(first_share(s) + p))

    for load in loads[1:]:
        load.start()

    def greeters(s):
        mine = jnp.logical_and(group >= first_group(s), group < first_group(s) + groups_of(s))
        return groups_of(s) - jnp.where(mine, 1, 0)

    pl.semaphore_wait(barrier, LINE + PLANE - 2 + greeters(seg_a) + jnp.where(two, greeters(seg_b), 0))
    loads[0].wait()

    def near_first(n):
        return (z + jnp.where(n % 2 == 1, (n + 1) // 2, LINE - n // 2)) % LINE

    def targets(zz, body):
        owner = line(zz)
        a, b = seg_of(SHARE * owner), seg_of(SHARE * owner + SHARE - 1)

        def one(s, w):
            p = owner - first_share(s)

            def each(n):
                k = s + n
                dev = tri(k) + s

                @pl.when(dev // GROUP % LINE == z)
                def _():
                    body(dev, s, p, w * SEGS + k)

            loop(SEGS - s, each)

        one(a, 0)

        @pl.when(b > a)
        def _():
            one(b, 1)

    def to_line(start):
        def each(n):
            zz = near_first(n)
            if start:
                send(x_ref, line_buf.at[z], line_send.at[zz], line_recv.at[z], line(zz))
            else:
                sent(x_ref, line_send.at[zz], line(zz))

        loop(LINE, each)

    def spread(start):
        def each(n):
            zz = near_first(n)
            src = line_buf.at[zz]
            if start:
                landed(src, line_recv.at[zz])

            def body(dev, s, p, at):
                if start:
                    dst = x_col.at[pl.ds(p * SHARE, SHARE)]
                    send(src, dst, spread_send.at[zz, at], gather_recv.at[1], dev)
                else:
                    sent(src, spread_send.at[zz, at], dev)

            targets(zz, body)

        loop(LINE, each)

    def to_relays(start):
        def body(s, w):
            turn = (me - first_share(s)) // GROUP
            dst, sem = relay_buf.at[s % KEYS, turn], relay_recv.at[s % KEYS, turn]

            def each(n):
                dev = (first_group(s) + n) * GROUP + residue
                if start:
                    send(x_ref, dst, relay_send.at[w * KEYS + n], sem, dev)
                else:
                    sent(x_ref, relay_send.at[w * KEYS + n], dev)

            loop(groups_of(s), each)

        return body

    to_line(True)
    owned(to_relays(True))

    for load in loads[1:]:
        load.wait()

    def split_tile(k):
        hi, lo = split(tile_buf[k])
        hi_buf[k] = hi
        lo_buf[k] = lo

    loop(SLOTS, split_tile)

    def pass_on(start):
        def body(s, p, key, turn):
            src = relay_buf.at[key, turn]
            dst = x_row.at[pl.ds(p * SHARE, SHARE)]
            if start:
                landed(src, relay_recv.at[key, turn])

            def each(dev):
                sem = pass_send.at[key, turn, dev % GROUP]
                if start:
                    send(src, dst, sem, gather_recv.at[0], dev)
                else:
                    sent(src, sem, dev)

            members(s, each)

        return body

    spread(True)
    relayed(pass_on(True))

    def wait_rows(s, held, recv_sem):
        for n in (WINDOW - 1, WINDOW):
            @pl.when(shares(s) == n)
            def _():
                landed(held.at[pl.ds(0, n * SHARE)], recv_sem)

    row_base = SHARE * first_share(row)
    col_base = SHARE * first_share(col)

    def multiply(held, ids, origin, terms, axis, dims):
        def one(k):
            hi, lo = split(held[jnp.clip(ids[k] - origin, 0, WINDOW * SHARE - 1)])
            both = jnp.concatenate([hi, lo], axis=0)
            out = lax.dot_general(
                jnp.concatenate([both, both], axis=1),
                jnp.concatenate([hi_buf[k], lo_buf[k]], axis=axis), dims,
                preferred_element_type=jnp.float32,
            )
            terms[pl.ds(pl.multiple_of(k * VEC, VEC), VEC), :] = out[:VEC] + out[VEC:]

        def several(n):
            for u in range(8):
                one(8 * n + u)

        loop(SLOTS // 8, several)

    def reduce(vec, origin, terms, which):
        live = lax.broadcasted_iota(jnp.int32, (PAD, SLOTS), 1) < count_ref[0]
        place = lax.broadcasted_iota(jnp.int32, (PAD, SLOTS), 0)
        hit = jnp.logical_and(place == vec[...] - origin, live)
        hot = hit.astype(jnp.float32).astype(jnp.bfloat16)
        hot = jnp.concatenate([hot, hot], axis=1)
        for v in range(VEC):
            hi, lo = split(terms[pl.ds(v, SLOTS, stride=VEC), :])
            contrib[which, pl.ds(v, PAD, stride=VEC), :] = lax.dot_general(
                hot, jnp.concatenate([hi, lo], axis=0), NN_DIMS,
                preferred_element_type=jnp.float32,
            )

    def chunk(which, p):
        return contrib.at[which, pl.ds(pl.multiple_of(p * ROWS, ROWS), ROWS), :]

    def row_parts(start):
        def each(p):
            dev = base + (first_share(row) + p) % GROUP
            if start:
                turn = p // GROUP
                send(
                    chunk(0, p), part_buf.at[row % KEYS, turn, residue], part_send.at[p],
                    part_recv.at[row % KEYS, turn, residue], dev,
                )
            else:
                sent(chunk(0, p), part_send.at[p], dev)

        loop(shares(row), each)

    def place_of(owner, s):
        return jnp.where(seg_of(SHARE * owner) == s, 0, 1)

    def col_parts(start):
        def each(p):
            owner = first_share(col) + p
            dev = (owner // 64 * LINE + z) * GROUP + owner % GROUP
            if start:
                zz = owner // GROUP % LINE
                at = place_of(owner, col) * SEGS + row
                send(chunk(1, p), col_buf.at[zz, at], col_send.at[p], col_recv.at[zz, at], dev)
            else:
                sent(chunk(1, p), col_send.at[p], dev)

        loop(shares(col), each)

    @pl.when(works)
    def _():
        wait_rows(col, x_col, gather_recv.at[1])
        multiply(x_col, cols_ref, col_base, row_terms, 1, NT_DIMS)
        reduce(rows_vec, row_base, row_terms, 0)

        @pl.when(off_diagonal)
        def _():
            row_parts(True)
            wait_rows(row, x_row, gather_recv.at[0])
            multiply(x_row, rows_ref, row_base, col_terms, 0, NN_DIMS)

        @pl.when(on_diagonal)
        def _():
            multiply(x_col, rows_ref, row_base, col_terms, 0, NN_DIMS)

        reduce(cols_vec, col_base, col_terms, 1)

        @pl.when(on_diagonal)
        def _():
            contrib[1] = contrib[0] + contrib[1]

        col_parts(True)

    to_line(False)
    owned(to_relays(False))
    spread(False)
    relayed(pass_on(False))

    def add_parts(start):
        def body(s, p, key, turn):
            owner = first_share(s) + p
            src = part_sum.at[key, turn]
            if start:
                low, count = span(s)

                def each(i, total):
                    rank = (low + i) % GROUP
                    landed(part_buf.at[key, turn, rank], part_recv.at[key, turn, rank])
                    return total + part_buf[key, turn, rank]

                part_sum[key, turn] = lax.fori_loop(
                    0, count, each, jnp.zeros((ROWS, WIDTH), jnp.float32)
                )
                at = place_of(owner, s) * KEYS + group - first_group(s)
                send(src, arrived.at[at], sum_send.at[key, turn], arrive_recv.at[at], owner)
            else:
                sent(src, sum_send.at[key, turn], owner)

        return body

    def add_cols(n):
        zz = near_first(LINE - 1 - n)
        col_sum[zz] = jnp.zeros((ROWS, WIDTH), jnp.float32)

        def body(dev, s, p, at):
            landed(col_buf.at[zz, at], col_recv.at[zz, at])
            col_sum[zz] = col_sum[zz] + col_buf[zz, at]

        targets(zz, body)
        at = 2 * KEYS + z
        send(col_sum.at[zz], arrived.at[at], back_send.at[zz], arrive_recv.at[at], line(zz))

    relayed(add_parts(True))
    loop(LINE, add_cols)

    def each(at, total):
        landed(arrived.at[at], arrive_recv.at[at])
        return total + arrived[at]

    def collect(w, s, total):
        return lax.fori_loop(w * KEYS, w * KEYS + groups_of(s), each, total)

    def put(total):
        for t in range(SHARE):
            image_ref[t] = total[t * VEC:(t + 1) * VEC]

    total = collect(0, seg_a, jnp.zeros((ROWS, WIDTH), jnp.float32))
    put(lax.fori_loop(2 * KEYS, 2 * KEYS + LINE, each, total))

    @pl.when(two)
    def _():
        put(collect(1, seg_b, jnp.concatenate([image_ref[t] for t in range(SHARE)], axis=0)))

    def flat(ref):
        return jnp.concatenate([ref[t] for t in range(SHARE)], axis=1)

    image = flat(image_ref)
    both = lax.dot_general(
        jnp.concatenate([flat(x_ref), image], axis=0), image, NT_DIMS,
        precision=lax.Precision.HIGHEST, preferred_element_type=jnp.float32,
    )
    gram_own[0] = jnp.zeros((VEC, WIDTH), jnp.float32)
    gram_own[0, :, 0:VEC] = both[:VEC]
    gram_own[0, :, VEC:2 * VEC] = both[VEC:]

    circles = (
        (gram_a, z, LINE, line),
        (gram_b, y * GROUP + residue, PLANE, plane),
    )
    for n, (buf, rank, size, partner) in enumerate(circles):
        for q in range(size):
            @pl.when(q != rank)
            def _():
                pltpu.make_async_remote_copy(
                    src_ref=gram_own.at[n], dst_ref=buf.at[rank], send_sem=gram_send.at[n, q],
                    recv_sem=gram_recv.at[n], device_id=(partner(q),), device_id_type=MESH,
                ).start()

        buf[rank] = gram_own[n]
        if n == 0:
            relayed(add_parts(False))

            @pl.when(off_diagonal)
            def _():
                row_parts(False)

            @pl.when(works)
            def _():
                col_parts(False)

            loop(LINE, lambda zz: sent(col_sum.at[zz], back_send.at[zz], line(zz)))

        landed(buf.at[pl.ds(0, size - 1)], gram_recv.at[n])
        terms = [buf[q] for q in range(size)]
        while len(terms) > 1:
            terms = [a + b for a, b in zip(terms[::2], terms[1::2])]
        if n == 0:
            gram_own[1] = terms[0]
        else:
            grams_ref[...] = terms[0] * (1.0 / (TILES * WIDTH))

    for n, (_buf, rank, size, _partner) in enumerate(circles):
        for q in range(size):
            @pl.when(q != rank)
            def _():
                pltpu.make_async_copy(gram_own.at[n], gram_own.at[n], gram_send.at[n, q]).wait()


def per_device(tiles, tile_rows, tile_cols, counts, block_vectors):
    f32, i32 = jnp.float32, jnp.int32
    vmem = pl.BlockSpec(memory_space=pltpu.VMEM)
    dma = pltpu.SemaphoreType.DMA
    image, grams = pl.pallas_call(
        kernel,
        out_shape=(
            pltpu.VMEM((SHARE, VEC, WIDTH), f32),
            pltpu.VMEM((VEC, WIDTH), f32),
        ),
        in_specs=[pl.BlockSpec(memory_space=pl.ANY)] * 7,
        out_specs=(vmem, vmem),
        scratch_shapes=[
            pltpu.VMEM((SLOTS, WIDTH, WIDTH), f32),
            pltpu.VMEM((SLOTS, WIDTH, WIDTH), jnp.bfloat16),
            pltpu.VMEM((SLOTS, WIDTH, WIDTH), jnp.bfloat16),
            pltpu.VMEM((SHARE, VEC, WIDTH), f32),
            pltpu.SMEM((SLOTS,), i32),
            pltpu.SMEM((SLOTS,), i32),
            pltpu.VMEM((1, SLOTS), i32),
            pltpu.VMEM((1, SLOTS), i32),
            pltpu.SMEM((1,), i32),
            pltpu.VMEM((WINDOW * SHARE, VEC, WIDTH), f32),
            pltpu.VMEM((WINDOW * SHARE, VEC, WIDTH), f32),
            pltpu.VMEM((KEYS, 2, SHARE, VEC, WIDTH), f32),
            pltpu.VMEM((LINE, SHARE, VEC, WIDTH), f32),
            pltpu.VMEM((LINE, 2 * SEGS, ROWS, WIDTH), f32),
            pltpu.VMEM((LINE, ROWS, WIDTH), f32),
            pltpu.VMEM((SLOTS * VEC, WIDTH), f32),
            pltpu.VMEM((SLOTS * VEC, WIDTH), f32),
            pltpu.VMEM((2, PAD * VEC, WIDTH), f32),
            pltpu.VMEM((KEYS, 2, GROUP, ROWS, WIDTH), f32),
            pltpu.VMEM((KEYS, 2, ROWS, WIDTH), f32),
            pltpu.VMEM((2 * KEYS + LINE, ROWS, WIDTH), f32),
            pltpu.VMEM((2, VEC, WIDTH), f32),
            pltpu.VMEM((LINE, VEC, WIDTH), f32),
            pltpu.VMEM((PLANE, VEC, WIDTH), f32),
            dma((7,)),
            dma((2 * KEYS,)),
            dma((KEYS, 2)),
            dma((KEYS, 2, GROUP)),
            dma((LINE,)),
            dma((LINE,)),
            dma((LINE, 2 * SEGS)),
            dma((2,)),
            dma((WINDOW,)),
            dma((KEYS, 2, GROUP)),
            dma((KEYS, 2)),
            dma((WINDOW,)),
            dma((LINE, 2 * SEGS)),
            dma((LINE,)),
            dma((2 * KEYS + LINE,)),
            dma((2, PLANE)),
            dma((2,)),
        ],
        compiler_params=pltpu.CompilerParams(
            collective_id=0, has_side_effects=True, vmem_limit_bytes=60 * 1024 * 1024
        ),
    )(
        tiles, tile_rows, tile_cols, tile_rows.reshape(1, SLOTS), tile_cols.reshape(1, SLOTS),
        counts, block_vectors,
    )
    return image, grams[:, :VEC], grams[:, VEC:2 * VEC]


def solution(mesh):
    placed = (P("tri", None, None), P("tri"), P("tri"), P("tri"), P("tri", None, None))
    return jax.shard_map(
        per_device,
        mesh=mesh,
        in_specs=placed,
        out_specs=(P("tri", None, None), P(), P()),
        check_vma=False,
    )
```

```python
import jax
import jax.numpy as jnp
from jax import lax
from jax.experimental import pallas as pl
from jax.experimental.pallas import tpu as pltpu
from jax.sharding import PartitionSpec as P

MESH = pl.DeviceIdType.MESH
SEGS = 22
TILES = 1024
SHARE = 4
VEC = 8
WIDTH = 128
ROWS = SHARE * VEC
SLOTS = 32
WINDOW = 13
PAD = 64
BLOCKS = SEGS * (SEGS + 1) // 2
DEVICES = 256
LOW_SCALE, LOW_SHIFT = 2979, 6
GROUP = 8
LINE = 8
PLANE = 32
KEYS = 4
NT_DIMS = (((1,), (1,)), ((), ()))
NN_DIMS = (((1,), (0,)), ((), ()))


def seg_low(s):
    return (s * LOW_SCALE) >> LOW_SHIFT


def seg_of(t):
    return ((t + 1) * SEGS - 1) >> 10


def first_share(s):
    return seg_low(s) >> 2


def shares(s):
    return ((seg_low(s + 1) - 1) >> 2) - first_share(s) + 1


def tri(s):
    return (s * (s + 1)) >> 1


def row_of(d, low=0, high=DEVICES):
    marks = [m * (m + 1) // 2 for m in range(1, SEGS)]
    row = sum(m <= low for m in marks)
    for m in marks:
        if low < m < high:
            row = row + (d >= m).astype(jnp.int32)
    return row


def first_group(s):
    return tri(s) >> 3


def groups_of(s):
    return ((tri(s) + s - 1) >> 3) - first_group(s) + 1


def split(a):
    hi = a.astype(jnp.bfloat16)
    lo = (a - hi.astype(jnp.float32)).astype(jnp.bfloat16)
    return hi, lo


def kernel(
    tiles_ref, rows_hbm, cols_hbm, rows_hbm2, cols_hbm2, count_hbm, x_hbm,
    image_ref, grams_ref,
    tile_buf, hi_buf, lo_buf, x_ref, rows_ref, cols_ref, rows_vec, cols_vec, count_ref,
    x_row, x_col, relay_buf, line_buf, col_buf, col_sum, row_terms, col_terms, contrib, part_buf, part_sum, arrived,
    gram_own, gram_a, gram_b,
    in_sem, relay_send, relay_recv, pass_send, line_send, line_recv, spread_send, gather_recv,
    part_send, part_recv, sum_send, col_send, col_recv, back_send, arrive_recv, gram_send, gram_recv,
):
    me = lax.axis_index("tri")
    residue = me & 7
    group = me >> 3
    base = group * GROUP
    works = me < BLOCKS
    row = row_of(me)
    col = jnp.minimum(me - tri(row), row)
    off_diagonal = jnp.logical_and(works, row > col)
    on_diagonal = jnp.logical_and(works, row == col)
    top = row_of(base)
    rows_here = row_of(jnp.minimum(base + GROUP - 1, BLOCKS - 1)) - top + 1
    seg_a = seg_of(SHARE * me)
    seg_b = seg_of(SHARE * me + SHARE - 1)
    two = seg_b > seg_a

    loads = [
        pltpu.make_async_copy(src, dst, in_sem.at[n])
        for n, (src, dst) in enumerate((
            (x_hbm, x_ref), (tiles_ref, tile_buf), (rows_hbm, rows_ref), (cols_hbm, cols_ref),
            (rows_hbm2, rows_vec), (cols_hbm2, cols_vec), (count_hbm, count_ref),
        ))
    ]
    loads[0].start()

    def loop(n, body):
        def step(i, _):
            body(i)
            return 0

        lax.fori_loop(0, n, step, 0)

    def owned(body):
        body(seg_a, 0)

        @pl.when(two)
        def _():
            body(seg_b, 1)

    def span(s):
        low = jnp.maximum(tri(s), base)
        return low, jnp.minimum(tri(s) + s, base + GROUP) - low

    def relayed(body):
        def each(n):
            s = top + n
            start = (residue - first_share(s)) & 7
            for turn in range(2):
                p = start + GROUP * turn

                @pl.when(jnp.logical_and(p < shares(s), span(s)[1] > 0))
                def _():
                    body(s, p, s & 3, turn)

        loop(rows_here, each)

    def members(s, body):
        low, count = span(s)
        loop(count, lambda i: body(low + i))

    def send(src, dst, send_sem, recv_sem, dev):
        @pl.when(dev != me)
        def _():
            pltpu.make_async_remote_copy(
                src_ref=src, dst_ref=dst, send_sem=send_sem, recv_sem=recv_sem,
                device_id=(dev,), device_id_type=MESH,
            ).start()

        @pl.when(dev == me)
        def _():
            pltpu.make_async_copy(src, dst, recv_sem).start()

    def sent(src, send_sem, dev):
        @pl.when(dev != me)
        def _():
            pltpu.make_async_copy(src, src, send_sem).wait()

    def landed(dst, recv_sem):
        pltpu.make_async_copy(dst, dst, recv_sem).wait()

    barrier = pltpu.get_barrier_semaphore()

    def greet(dev):
        @pl.when(dev != me)
        def _():
            pl.semaphore_signal(barrier, inc=1, device_id=(dev,), device_id_type=MESH)

    z, y = group & 7, me >> 6

    def line(zz):
        return (y * LINE + zz) * GROUP + residue

    def plane(q):
        return ((q >> 3) * LINE + z) * GROUP + (q & 7)

    for dz in range(1, LINE):
        greet(line((z + dz) & 7))
    for q in range(PLANE):
        greet(plane(q))
    relayed(lambda s, p, key, turn: greet(first_share(s) + p))

    for load in loads[1:]:
        load.start()

    def greeters(s):
        mine = jnp.logical_and(group >= first_group(s), group < first_group(s) + groups_of(s))
        return groups_of(s) - jnp.where(mine, 1, 0)

    pl.semaphore_wait(barrier, LINE + PLANE - 2 + greeters(seg_a) + jnp.where(two, greeters(seg_b), 0))
    loads[0].wait()

    def near_first(n):
        return (z + jnp.where((n & 1) == 1, (n + 1) >> 1, LINE - (n >> 1))) & 7

    def targets(zz, body):
        owner = line(zz)
        a, b = seg_of(SHARE * owner), seg_of(SHARE * owner + SHARE - 1)

        def one(s):
            for low, top_row, end_row in here:
                def each(i, low=low, top_row=top_row):
                    k = top_row + i
                    dev = tri(k) + s

                    @pl.when(jnp.logical_and(((dev - low) >> 3) == 0, s <= k))
                    def _():
                        body(dev, s, owner - first_share(s))

                loop(end_row - top_row + 1, each)

        one(a)

        @pl.when(b > a)
        def _():
            one(b)

    def rank_of(dev):
        return ((dev >> 6) << 3) + (dev & 7)

    def to_line(n):
        zz = near_first(n)
        send(x_ref, line_buf.at[z], line_send, line_recv.at[z], line(zz))

    def spread(start):
        def each(n):
            zz = near_first(n)
            src = line_buf.at[zz]
            if start:
                landed(src, line_recv.at[zz])

            def body(dev, s, p):
                if start:
                    dst = x_col.at[pl.ds(p * SHARE, SHARE)]
                    send(src, dst, spread_send, gather_recv.at[1], dev)
                else:
                    sent(src, spread_send, dev)

            targets(zz, body)

        loop(LINE, each)

    def to_relays(start):
        def body(s, w):
            turn = (me - first_share(s)) >> 3
            dst, sem = relay_buf.at[s & 3, turn], relay_recv.at[s & 3, turn]

            def each(n):
                dev = (first_group(s) + n) * GROUP + residue
                if start:
                    send(x_ref, dst, relay_send, sem, dev)
                else:
                    sent(x_ref, relay_send, dev)

            loop(groups_of(s), each)

        return body

    loop(LINE, to_line)
    owned(to_relays(True))

    here = []
    for yy in range(4):
        low = yy * 64 + z * GROUP
        bounds = (yy * 64, yy * 64 + 64)
        end = jnp.minimum(low + GROUP - 1, BLOCKS - 1)
        here.append((low, row_of(low, *bounds), row_of(end, *bounds)))

    for load in loads[1:]:
        load.wait()

    def split_tile(k):
        hi, lo = split(tile_buf[k])
        hi_buf[k] = hi
        lo_buf[k] = lo

    loop(SLOTS, split_tile)

    def pass_on(start):
        def body(s, p, key, turn):
            src = relay_buf.at[key, turn]
            dst = x_row.at[pl.ds(p * SHARE, SHARE)]
            if start:
                landed(src, relay_recv.at[key, turn])

            def each(dev):
                if start:
                    send(src, dst, pass_send, gather_recv.at[0], dev)
                else:
                    sent(src, pass_send, dev)

            members(s, each)

        return body

    spread(True)
    relayed(pass_on(True))

    def wait_rows(s, held, recv_sem):
        for n in (WINDOW - 1, WINDOW):
            @pl.when(shares(s) == n)
            def _():
                landed(held.at[pl.ds(0, n * SHARE)], recv_sem)

    row_base = SHARE * first_share(row)
    col_base = SHARE * first_share(col)

    def multiply(held, ids, origin, terms, axis, dims):
        def one(k):
            hi, lo = split(held[jnp.clip(ids[k] - origin, 0, WINDOW * SHARE - 1)])
            both = jnp.concatenate([hi, lo], axis=0)
            out = lax.dot_general(
                jnp.concatenate([both, both], axis=1),
                jnp.concatenate([hi_buf[k], lo_buf[k]], axis=axis), dims,
                preferred_element_type=jnp.float32,
            )
            terms[pl.ds(pl.multiple_of(k * VEC, VEC), VEC), :] = out[:VEC] + out[VEC:]

        def several(n):
            for u in range(8):
                one(8 * n + u)

        loop(SLOTS // 8, several)

    def reduce(vec, origin, terms, which):
        live = lax.broadcasted_iota(jnp.int32, (PAD, SLOTS), 1) < count_ref[0]
        place = lax.broadcasted_iota(jnp.int32, (PAD, SLOTS), 0)
        hit = jnp.logical_and(place == vec[...] - origin, live)
        hot = hit.astype(jnp.float32).astype(jnp.bfloat16)
        hot = jnp.concatenate([hot, hot], axis=1)
        for v in range(VEC):
            hi, lo = split(terms[pl.ds(v, SLOTS, stride=VEC), :])
            contrib[which, pl.ds(v, PAD, stride=VEC), :] = lax.dot_general(
                hot, jnp.concatenate([hi, lo], axis=0), NN_DIMS,
                preferred_element_type=jnp.float32,
            )

    def chunk(which, p):
        return contrib.at[which, pl.ds(pl.multiple_of(p * ROWS, ROWS), ROWS), :]

    def row_parts(p):
        turn = p >> 3
        send(
            chunk(0, p), part_buf.at[turn, residue], part_send, part_recv.at[turn, residue],
            base + ((first_share(row) + p) & 7),
        )

    def all_sent(which, s, same_y, sem):
        n = shares(s)
        for turn in range(2):
            p = ((residue - first_share(s)) & 7) + GROUP * turn
            mine = p < shares(s)
            if same_y:
                mine = jnp.logical_and(mine, ((first_share(s) + p) >> 6) == y)
            n = n - mine.astype(jnp.int32)
        for count in range(WINDOW - 3, WINDOW + 1):
            @pl.when(n == count)
            def _():
                landed(contrib.at[which, pl.ds(0, count * ROWS), :], sem)

    def place_of(owner, s):
        return jnp.where(seg_of(SHARE * owner) == s, 0, 1)

    def col_parts(p):
        owner = first_share(col) + p
        at = rank_of(me) * 2 + (p >> 3)
        dev = (((owner >> 6) << 3) + z) * GROUP + (owner & 7)
        send(chunk(1, p), col_buf.at[at], col_send, col_recv.at[at], dev)

    @pl.when(works)
    def _():
        wait_rows(col, x_col, gather_recv.at[1])
        multiply(x_col, cols_ref, col_base, row_terms, 1, NT_DIMS)
        reduce(rows_vec, row_base, row_terms, 0)

        @pl.when(off_diagonal)
        def _():
            loop(shares(row), row_parts)
            wait_rows(row, x_row, gather_recv.at[0])
            multiply(x_row, rows_ref, row_base, col_terms, 0, NN_DIMS)

        @pl.when(on_diagonal)
        def _():
            multiply(x_col, rows_ref, row_base, col_terms, 0, NN_DIMS)

        reduce(cols_vec, col_base, col_terms, 1)

        @pl.when(on_diagonal)
        def _():
            contrib[1] = contrib[0] + contrib[1]

        loop(shares(col), col_parts)

    landed(line_buf.at[pl.ds(0, LINE - 1)], line_send)
    owned(to_relays(False))
    spread(False)
    relayed(pass_on(False))

    def add_parts(start):
        def body(s, p, key, turn):
            owner = first_share(s) + p
            src = part_sum.at[key, turn]
            if start:
                low, count = span(s)

                def each(i, total):
                    rank = (low + i) & 7
                    landed(part_buf.at[turn, rank], part_recv.at[turn, rank])
                    return total + part_buf[turn, rank]

                part_sum[key, turn] = lax.fori_loop(
                    0, count, each, jnp.zeros((ROWS, WIDTH), jnp.float32)
                )
                at = place_of(owner, s) * KEYS + group - first_group(s)
                send(src, arrived.at[at], sum_send, arrive_recv.at[at], owner)
            else:
                sent(src, sum_send, owner)

        return body

    def add_cols(n):
        zz = near_first(LINE - 1 - n)
        col_sum[zz] = jnp.zeros((ROWS, WIDTH), jnp.float32)

        def body(dev, s, p):
            at = rank_of(dev) * 2 + (p >> 3)
            landed(col_buf.at[at], col_recv.at[at])
            col_sum[zz] = col_sum[zz] + col_buf[at]

        targets(zz, body)
        at = 2 * KEYS + z
        send(col_sum.at[zz], arrived.at[at], back_send, arrive_recv.at[at], line(zz))

    relayed(add_parts(True))
    loop(LINE, add_cols)

    def each(at, total):
        landed(arrived.at[at], arrive_recv.at[at])
        return total + arrived[at]

    def collect(w, s, total):
        return lax.fori_loop(w * KEYS, w * KEYS + groups_of(s), each, total)

    def put(total):
        for t in range(SHARE):
            image_ref[t] = total[t * VEC:(t + 1) * VEC]

    total = collect(0, seg_a, jnp.zeros((ROWS, WIDTH), jnp.float32))
    put(lax.fori_loop(2 * KEYS, 2 * KEYS + LINE, each, total))

    @pl.when(two)
    def _():
        put(collect(1, seg_b, jnp.concatenate([image_ref[t] for t in range(SHARE)], axis=0)))

    def flat(ref):
        return jnp.concatenate([ref[t] for t in range(SHARE)], axis=1)

    image = flat(image_ref)
    both = lax.dot_general(
        jnp.concatenate([flat(x_ref), image], axis=0), image, NT_DIMS,
        precision=lax.Precision.HIGHEST, preferred_element_type=jnp.float32,
    )
    gram_own[0] = jnp.zeros((VEC, WIDTH), jnp.float32)
    gram_own[0, :, 0:VEC] = both[:VEC]
    gram_own[0, :, VEC:2 * VEC] = both[VEC:]

    circles = (
        (gram_a, z, LINE, line),
        (gram_b, y * GROUP + residue, PLANE, plane),
    )
    for n, (buf, rank, size, partner) in enumerate(circles):
        for q in range(size):
            @pl.when(q != rank)
            def _():
                pltpu.make_async_remote_copy(
                    src_ref=gram_own.at[n], dst_ref=buf.at[rank], send_sem=gram_send.at[n],
                    recv_sem=gram_recv.at[n], device_id=(partner(q),), device_id_type=MESH,
                ).start()

        buf[rank] = gram_own[n]
        if n == 0:
            relayed(add_parts(False))

            @pl.when(off_diagonal)
            def _():
                all_sent(0, row, False, part_send)

            @pl.when(works)
            def _():
                all_sent(1, col, True, col_send)

            landed(col_sum.at[pl.ds(0, LINE - 1)], back_send)

        landed(buf.at[pl.ds(0, size - 1)], gram_recv.at[n])
        terms = [buf[q] for q in range(size)]
        while len(terms) > 1:
            terms = [a + b for a, b in zip(terms[::2], terms[1::2])]
        if n == 0:
            gram_own[1] = terms[0]
        else:
            grams_ref[...] = terms[0] * (1.0 / (TILES * WIDTH))

    for n, (buf, _rank, size, _partner) in enumerate(circles):
        landed(buf.at[pl.ds(0, size - 1)], gram_send.at[n])


def per_device(tiles, tile_rows, tile_cols, counts, block_vectors):
    f32, i32 = jnp.float32, jnp.int32
    vmem = pl.BlockSpec(memory_space=pltpu.VMEM)
    dma = pltpu.SemaphoreType.DMA
    image, grams = pl.pallas_call(
        kernel,
        out_shape=(
            pltpu.VMEM((SHARE, VEC, WIDTH), f32),
            pltpu.VMEM((VEC, WIDTH), f32),
        ),
        in_specs=[pl.BlockSpec(memory_space=pl.ANY)] * 7,
        out_specs=(vmem, vmem),
        scratch_shapes=[
            pltpu.VMEM((SLOTS, WIDTH, WIDTH), f32),
            pltpu.VMEM((SLOTS, WIDTH, WIDTH), jnp.bfloat16),
            pltpu.VMEM((SLOTS, WIDTH, WIDTH), jnp.bfloat16),
            pltpu.VMEM((SHARE, VEC, WIDTH), f32),
            pltpu.SMEM((SLOTS,), i32),
            pltpu.SMEM((SLOTS,), i32),
            pltpu.VMEM((1, SLOTS), i32),
            pltpu.VMEM((1, SLOTS), i32),
            pltpu.SMEM((1,), i32),
            pltpu.VMEM((WINDOW * SHARE, VEC, WIDTH), f32),
            pltpu.VMEM((WINDOW * SHARE, VEC, WIDTH), f32),
            pltpu.VMEM((KEYS, 2, SHARE, VEC, WIDTH), f32),
            pltpu.VMEM((LINE, SHARE, VEC, WIDTH), f32),
            pltpu.VMEM((2 * PLANE, ROWS, WIDTH), f32),
            pltpu.VMEM((LINE, ROWS, WIDTH), f32),
            pltpu.VMEM((SLOTS * VEC, WIDTH), f32),
            pltpu.VMEM((SLOTS * VEC, WIDTH), f32),
            pltpu.VMEM((2, PAD * VEC, WIDTH), f32),
            pltpu.VMEM((2, GROUP, ROWS, WIDTH), f32),
            pltpu.VMEM((KEYS, 2, ROWS, WIDTH), f32),
            pltpu.VMEM((2 * KEYS + LINE, ROWS, WIDTH), f32),
            pltpu.VMEM((2, VEC, WIDTH), f32),
            pltpu.VMEM((LINE, VEC, WIDTH), f32),
            pltpu.VMEM((PLANE, VEC, WIDTH), f32),
            dma((7,)),
            dma,
            dma((KEYS, 2)),
            dma,
            dma,
            dma((LINE,)),
            dma,
            dma((2,)),
            dma,
            dma((2, GROUP)),
            dma,
            dma,
            dma((2 * PLANE,)),
            dma,
            dma((2 * KEYS + LINE,)),
            dma((2,)),
            dma((2,)),
        ],
        compiler_params=pltpu.CompilerParams(
            collective_id=0, has_side_effects=True, vmem_limit_bytes=60 * 1024 * 1024
        ),
    )(
        tiles, tile_rows, tile_cols, tile_rows.reshape(1, SLOTS), tile_cols.reshape(1, SLOTS),
        counts, block_vectors,
    )
    return image, grams[:, :VEC], grams[:, VEC:2 * VEC]


def solution(mesh):
    placed = (P("tri", None, None), P("tri"), P("tri"), P("tri"), P("tri", None, None))
    return jax.shard_map(
        per_device,
        mesh=mesh,
        in_specs=placed,
        out_specs=(P("tri", None, None), P(), P()),
        check_vma=False,
    )
```

```python
import jax
import jax.numpy as jnp
from jax import lax
from jax.experimental import pallas as pl
from jax.experimental.pallas import tpu as pltpu
from jax.sharding import PartitionSpec as P

MESH = pl.DeviceIdType.MESH
SEGS = 22
TILES = 1024
SHARE = 4
VEC = 8
WIDTH = 128
ROWS = SHARE * VEC
SLOTS = 32
WINDOW = 13
PAD = 64
BLOCKS = SEGS * (SEGS + 1) // 2
DEVICES = 256
LOW_SCALE, LOW_SHIFT = 2979, 6
GROUP = 8
LINE = 8
PLANE = 32
ROWS_AT = (4, 2, 2, 2)
KEYS = 4
NT_DIMS = (((1,), (1,)), ((), ()))
NN_DIMS = (((1,), (0,)), ((), ()))


def seg_low(s):
    return (s * LOW_SCALE) >> LOW_SHIFT


def seg_of(t):
    return ((t + 1) * SEGS - 1) >> 10


def first_share(s):
    return seg_low(s) >> 2


def shares(s):
    return ((seg_low(s + 1) - 1) >> 2) - first_share(s) + 1


def tri(s):
    return (s * (s + 1)) >> 1


def row_of(d, low=0, high=DEVICES):
    marks = [m * (m + 1) // 2 for m in range(1, SEGS)]
    row = sum(m <= low for m in marks)
    for m in marks:
        if low < m < high:
            row = row + (d >= m).astype(jnp.int32)
    return row


def first_group(s):
    return tri(s) >> 3


def groups_of(s):
    return ((tri(s) + s - 1) >> 3) - first_group(s) + 1


def split(a):
    hi = a.astype(jnp.bfloat16)
    lo = (a - hi.astype(jnp.float32)).astype(jnp.bfloat16)
    return hi, lo


def kernel(
    tiles_ref, rows_hbm, cols_hbm, rows_hbm2, cols_hbm2, count_hbm, x_hbm,
    image_ref, grams_ref,
    tile_buf, hi_buf, lo_buf, x_ref, rows_ref, cols_ref, rows_vec, cols_vec, count_ref,
    x_row, x_col, relay_buf, line_buf, row_terms, col_terms, contrib, part_buf, part_sum, arrived,
    gram_own, gram_a, gram_b,
    in_sem, relay_send, relay_recv, pass_send, line_send, line_recv, spread_send, gather_recv,
    part_send, part_recv, sum_send, col_send, arrive_recv, gram_send, gram_recv,
):
    me = lax.axis_index("tri")
    residue = me & 7
    group = me >> 3
    base = group * GROUP
    works = me < BLOCKS
    row = row_of(me)
    col = jnp.minimum(me - tri(row), row)
    off_diagonal = jnp.logical_and(works, row > col)
    on_diagonal = jnp.logical_and(works, row == col)
    top = row_of(base)
    rows_here = row_of(jnp.minimum(base + GROUP - 1, BLOCKS - 1)) - top + 1
    seg_a = seg_of(SHARE * me)
    seg_b = seg_of(SHARE * me + SHARE - 1)
    two = seg_b > seg_a

    loads = [
        pltpu.make_async_copy(src, dst, in_sem.at[n])
        for n, (src, dst) in enumerate((
            (x_hbm, x_ref), (tiles_ref, tile_buf), (rows_hbm, rows_ref), (cols_hbm, cols_ref),
            (rows_hbm2, rows_vec), (cols_hbm2, cols_vec), (count_hbm, count_ref),
        ))
    ]
    loads[0].start()

    def loop(n, body):
        def step(i, _):
            body(i)
            return 0

        lax.fori_loop(0, n, step, 0)

    def owned(body):
        body(seg_a, 0)

        @pl.when(two)
        def _():
            body(seg_b, 1)

    def span(s):
        low = jnp.maximum(tri(s), base)
        return low, jnp.minimum(tri(s) + s, base + GROUP) - low

    def relayed(body):
        def each(n):
            s = top + n
            start = (residue - first_share(s)) & 7
            for turn in range(2):
                p = start + GROUP * turn

                @pl.when(jnp.logical_and(p < shares(s), span(s)[1] > 0))
                def _():
                    body(s, p, s & 3, turn)

        loop(rows_here, each)

    def members(s, body):
        low, count = span(s)
        loop(count, lambda i: body(low + i))

    def send(src, dst, send_sem, recv_sem, dev):
        def remote():
            pltpu.make_async_remote_copy(
                src_ref=src, dst_ref=dst, send_sem=send_sem, recv_sem=recv_sem,
                device_id=(dev,), device_id_type=MESH,
            ).start()

        def local():
            pltpu.make_async_copy(src, dst, recv_sem).start()

        lax.cond(dev != me, remote, local)

    def sent(src, send_sem, dev):
        @pl.when(dev != me)
        def _():
            pltpu.make_async_copy(src, src, send_sem).wait()

    def landed(dst, recv_sem):
        pltpu.make_async_copy(dst, dst, recv_sem).wait()

    barrier = pltpu.get_barrier_semaphore()

    def greet(dev):
        @pl.when(dev != me)
        def _():
            pl.semaphore_signal(barrier, inc=1, device_id=(dev,), device_id_type=MESH)

    z, y = group & 7, me >> 6

    def rank_of(dev):
        return ((dev >> 6) << 3) + (dev & 7)

    def line(zz):
        return (y * LINE + zz) * GROUP + residue

    def plane(q):
        return ((q >> 3) * LINE + z) * GROUP + (q & 7)

    for dz in range(1, LINE):
        pl.semaphore_signal(barrier, inc=1, device_id=(line((z + dz) & 7),), device_id_type=MESH)
    for m in range(1, PLANE):
        pl.semaphore_signal(
            barrier, inc=1, device_id=(plane(rank_of(me) ^ m),), device_id_type=MESH
        )
    relayed(lambda s, p, key, turn: greet(first_share(s) + p))

    for load in loads[1:]:
        load.start()

    def greeters(s):
        mine = jnp.logical_and(group >= first_group(s), group < first_group(s) + groups_of(s))
        return groups_of(s) - jnp.where(mine, 1, 0)

    pl.semaphore_wait(barrier, LINE + PLANE - 2 + greeters(seg_a) + jnp.where(two, greeters(seg_b), 0))
    loads[0].wait()

    def near_first(n):
        return (z + jnp.where((n & 1) == 1, (n + 1) >> 1, LINE - (n >> 1))) & 7

    def targets(zz, body):
        owner = line(zz)
        a, b = seg_of(SHARE * owner), seg_of(SHARE * owner + SHARE - 1)

        def one(w):
            s = a + w
            p = owner - first_share(s)
            for k, first, low in here:
                dev = first + s

                @pl.when(jnp.logical_and(((dev - low) >> 3) == 0, s <= k))
                def _(dev=dev):
                    body(dev, s, p)

        loop(1 + (b > a).astype(jnp.int32), one)

    def to_line(n):
        zz = near_first(LINE - 1 - n)
        send(x_ref, line_buf.at[z], line_send, line_recv.at[z], line(zz))

    def spread(start):
        def each(n):
            zz = near_first(n)
            src = line_buf.at[zz]
            if start:
                landed(src, line_recv.at[zz])

            def body(dev, s, p):
                if start:
                    dst = x_col.at[pl.ds(p * SHARE, SHARE)]
                    send(src, dst, spread_send, gather_recv.at[1], dev)
                else:
                    sent(src, spread_send, dev)

            targets(zz, body)

        loop(LINE, each)

    def to_relays(start):
        def body(s, w):
            turn = (me - first_share(s)) >> 3
            dst, sem = relay_buf.at[s & 3, turn], relay_recv.at[s & 3, turn]

            def each(n):
                dev = (first_group(s) + n) * GROUP + residue
                if start:
                    send(x_ref, dst, relay_send, sem, dev)
                else:
                    sent(x_ref, relay_send, dev)

            loop(groups_of(s), each)

        return body

    loop(LINE, to_line)
    owned(to_relays(True))

    here = []
    for yy in (2, 1, 3, 0):
        low = yy * 64 + z * GROUP
        first_row = row_of(low, yy * 64, yy * 64 + 64)
        for k in [first_row + i for i in range(ROWS_AT[yy])]:
            here.append((k, jnp.where(k < SEGS, tri(k), 2 * DEVICES), low))

    for load in loads[1:]:
        load.wait()

    def split_tile(k):
        hi, lo = split(tile_buf[k])
        hi_buf[k] = hi
        lo_buf[k] = lo

    loop(SLOTS, split_tile)

    def pass_on(start):
        def body(s, p, key, turn):
            src = relay_buf.at[key, turn]
            dst = x_row.at[pl.ds(p * SHARE, SHARE)]
            if start:
                landed(src, relay_recv.at[key, turn])

            def each(dev):
                if start:
                    send(src, dst, pass_send, gather_recv.at[0], dev)
                else:
                    sent(src, pass_send, dev)

            members(s, each)

        return body

    spread(True)
    relayed(pass_on(True))

    def wait_rows(s, held, recv_sem):
        for n in (WINDOW - 1, WINDOW):
            @pl.when(shares(s) == n)
            def _():
                landed(held.at[pl.ds(0, n * SHARE)], recv_sem)

    row_base = SHARE * first_share(row)
    col_base = SHARE * first_share(col)

    def multiply(held, ids, origin, terms, axis, dims):
        def one(k):
            hi, lo = split(held[jnp.clip(ids[k] - origin, 0, WINDOW * SHARE - 1)])
            both = jnp.concatenate([hi, lo], axis=0)
            out = lax.dot_general(
                jnp.concatenate([both, both], axis=1),
                jnp.concatenate([hi_buf[k], lo_buf[k]], axis=axis), dims,
                preferred_element_type=jnp.float32,
            )
            terms[pl.ds(pl.multiple_of(k * VEC, VEC), VEC), :] = out[:VEC] + out[VEC:]

        def several(n):
            for u in range(8):
                one(8 * n + u)

        loop(SLOTS // 8, several)

    def reduce(vec, origin, terms, which):
        live = lax.broadcasted_iota(jnp.int32, (PAD, SLOTS), 1) < count_ref[0]
        place = lax.broadcasted_iota(jnp.int32, (PAD, SLOTS), 0)
        hit = jnp.logical_and(place == vec[...] - origin, live)
        hot = hit.astype(jnp.float32).astype(jnp.bfloat16)
        hot = jnp.concatenate([hot, hot], axis=1)
        for v in range(VEC):
            hi, lo = split(terms[pl.ds(v, SLOTS, stride=VEC), :])
            contrib[which, pl.ds(v, PAD, stride=VEC), :] = lax.dot_general(
                hot, jnp.concatenate([hi, lo], axis=0), NN_DIMS,
                preferred_element_type=jnp.float32,
            )

    def chunk(which, p):
        return contrib.at[which, pl.ds(pl.multiple_of(p * ROWS, ROWS), ROWS), :]

    def row_parts(p):
        turn = p >> 3
        send(
            chunk(0, p), part_buf.at[turn, residue], part_send, part_recv.at[turn, residue],
            base + ((first_share(row) + p) & 7),
        )

    def all_sent(which, n, sem):
        for count in range(WINDOW - 3, WINDOW + 1):
            @pl.when(n == count)
            def _():
                landed(contrib.at[which, pl.ds(0, count * ROWS), :], sem)

    def place_of(owner, s):
        return jnp.where(seg_of(SHARE * owner) == s, 0, 1)

    def slot_of(owner, s):
        return place_of(owner, s) * (KEYS + SEGS)

    def col_parts(p):
        owner = first_share(col) + p
        at = slot_of(owner, col) + KEYS + row
        send(chunk(1, p), arrived.at[at], col_send, arrive_recv.at[at], owner)

    @pl.when(works)
    def _():
        wait_rows(col, x_col, gather_recv.at[1])
        multiply(x_col, cols_ref, col_base, row_terms, 1, NT_DIMS)
        reduce(rows_vec, row_base, row_terms, 0)

        @pl.when(off_diagonal)
        def _():
            loop(shares(row), row_parts)
            wait_rows(row, x_row, gather_recv.at[0])
            multiply(x_row, rows_ref, row_base, col_terms, 0, NN_DIMS)

        @pl.when(on_diagonal)
        def _():
            multiply(x_col, rows_ref, row_base, col_terms, 0, NN_DIMS)

        reduce(cols_vec, col_base, col_terms, 1)

        @pl.when(on_diagonal)
        def _():
            contrib[1] = contrib[0] + contrib[1]

        loop(shares(col), col_parts)

    landed(line_buf.at[pl.ds(0, LINE - 1)], line_send)
    owned(to_relays(False))
    spread(False)
    relayed(pass_on(False))

    def add_parts(start):
        def body(s, p, key, turn):
            owner = first_share(s) + p
            src = part_sum.at[key, turn]
            if start:
                low, count = span(s)

                def each(i, total):
                    rank = (low + i) & 7
                    landed(part_buf.at[turn, rank], part_recv.at[turn, rank])
                    return total + part_buf[turn, rank]

                part_sum[key, turn] = lax.fori_loop(
                    0, count, each, jnp.zeros((ROWS, WIDTH), jnp.float32)
                )
                at = slot_of(owner, s) + group - first_group(s)
                send(src, arrived.at[at], sum_send, arrive_recv.at[at], owner)
            else:
                sent(src, sum_send, owner)

        return body

    relayed(add_parts(True))

    def each(at, total):
        landed(arrived.at[at], arrive_recv.at[at])
        return total + arrived[at]

    def collect(w, s, total):
        start = w * (KEYS + SEGS)
        total = lax.fori_loop(start + KEYS + s, start + KEYS + SEGS, each, total)
        return lax.fori_loop(start, start + groups_of(s), each, total)

    def put(total):
        for t in range(SHARE):
            image_ref[t] = total[t * VEC:(t + 1) * VEC]

    put(collect(0, seg_a, jnp.zeros((ROWS, WIDTH), jnp.float32)))

    @pl.when(two)
    def _():
        put(collect(1, seg_b, jnp.concatenate([image_ref[t] for t in range(SHARE)], axis=0)))

    def flat(ref):
        return jnp.concatenate([ref[t] for t in range(SHARE)], axis=1)

    image = flat(image_ref)
    both = lax.dot_general(
        jnp.concatenate([flat(x_ref), image], axis=0), image, NT_DIMS,
        precision=lax.Precision.HIGHEST, preferred_element_type=jnp.float32,
    )
    gram_own[0] = jnp.zeros((VEC, WIDTH), jnp.float32)
    gram_own[0, :, 0:VEC] = both[:VEC]
    gram_own[0, :, VEC:2 * VEC] = both[VEC:]

    def hops(m):
        return [0, 1, 2, 1][m >> 3] + [0, 1, 2, 1][(m >> 1) & 3]

    rank = rank_of(me)
    circles = (
        (gram_a, z, LINE, [line((z + dz) & 7) for dz in (4, 3, 5, 2, 6, 1, 7)]),
        (gram_b, rank, PLANE, [plane(rank ^ m) for m in sorted(range(1, PLANE), key=hops, reverse=True)]),
    )
    for n, (buf, rank, size, partners) in enumerate(circles):
        for dev in partners:
            pltpu.make_async_remote_copy(
                src_ref=gram_own.at[n], dst_ref=buf.at[rank], send_sem=gram_send.at[n],
                recv_sem=gram_recv.at[n], device_id=(dev,), device_id_type=MESH,
            ).start()

        buf[rank] = gram_own[n]
        if n == 0:
            relayed(add_parts(False))

            @pl.when(off_diagonal)
            def _():
                p = (residue - first_share(row)) & 7
                n_sent = shares(row) - 1 - (p + GROUP < shares(row)).astype(jnp.int32)
                all_sent(0, n_sent, part_send)

            @pl.when(works)
            def _():
                p = me - first_share(col)
                mine = jnp.logical_and(p >= 0, p < shares(col)).astype(jnp.int32)
                all_sent(1, shares(col) - mine, col_send)

        landed(buf.at[pl.ds(0, size - 1)], gram_recv.at[n])
        terms = [buf[q] for q in range(size)]
        while len(terms) > 1:
            terms = [a + b for a, b in zip(terms[::2], terms[1::2])]
        if n == 0:
            gram_own[1] = terms[0]
        else:
            grams_ref[...] = terms[0] * (1.0 / (TILES * WIDTH))

    for n, (buf, _rank, size, _partners) in enumerate(circles):
        landed(buf.at[pl.ds(0, size - 1)], gram_send.at[n])


def per_device(tiles, tile_rows, tile_cols, counts, block_vectors):
    f32, i32 = jnp.float32, jnp.int32
    vmem = pl.BlockSpec(memory_space=pltpu.VMEM)
    dma = pltpu.SemaphoreType.DMA
    image, grams = pl.pallas_call(
        kernel,
        out_shape=(
            pltpu.VMEM((SHARE, VEC, WIDTH), f32),
            pltpu.VMEM((VEC, WIDTH), f32),
        ),
        in_specs=[pl.BlockSpec(memory_space=pl.ANY)] * 7,
        out_specs=(vmem, vmem),
        scratch_shapes=[
            pltpu.VMEM((SLOTS, WIDTH, WIDTH), f32),
            pltpu.VMEM((SLOTS, WIDTH, WIDTH), jnp.bfloat16),
            pltpu.VMEM((SLOTS, WIDTH, WIDTH), jnp.bfloat16),
            pltpu.VMEM((SHARE, VEC, WIDTH), f32),
            pltpu.SMEM((SLOTS,), i32),
            pltpu.SMEM((SLOTS,), i32),
            pltpu.VMEM((1, SLOTS), i32),
            pltpu.VMEM((1, SLOTS), i32),
            pltpu.SMEM((1,), i32),
            pltpu.VMEM((WINDOW * SHARE, VEC, WIDTH), f32),
            pltpu.VMEM((WINDOW * SHARE, VEC, WIDTH), f32),
            pltpu.VMEM((KEYS, 2, SHARE, VEC, WIDTH), f32),
            pltpu.VMEM((LINE, SHARE, VEC, WIDTH), f32),
            pltpu.VMEM((SLOTS * VEC, WIDTH), f32),
            pltpu.VMEM((SLOTS * VEC, WIDTH), f32),
            pltpu.VMEM((2, PAD * VEC, WIDTH), f32),
            pltpu.VMEM((2, GROUP, ROWS, WIDTH), f32),
            pltpu.VMEM((KEYS, 2, ROWS, WIDTH), f32),
            pltpu.VMEM((2 * (KEYS + SEGS), ROWS, WIDTH), f32),
            pltpu.VMEM((2, VEC, WIDTH), f32),
            pltpu.VMEM((LINE, VEC, WIDTH), f32),
            pltpu.VMEM((PLANE, VEC, WIDTH), f32),
            dma((7,)),
            dma,
            dma((KEYS, 2)),
            dma,
            dma,
            dma((LINE,)),
            dma,
            dma((2,)),
            dma,
            dma((2, GROUP)),
            dma,
            dma,
            dma((2 * (KEYS + SEGS),)),
            dma((2,)),
            dma((2,)),
        ],
        compiler_params=pltpu.CompilerParams(
            collective_id=0, has_side_effects=True, vmem_limit_bytes=60 * 1024 * 1024
        ),
    )(
        tiles, tile_rows, tile_cols, tile_rows.reshape(1, SLOTS), tile_cols.reshape(1, SLOTS),
        counts, block_vectors,
    )
    return image, grams[:, :VEC], grams[:, VEC:2 * VEC]


def solution(mesh):
    placed = (P("tri", None, None), P("tri"), P("tri"), P("tri"), P("tri", None, None))
    return jax.shard_map(
        per_device,
        mesh=mesh,
        in_specs=placed,
        out_specs=(P("tri", None, None), P(), P()),
        check_vma=False,
    )
```

```python
import jax
import jax.numpy as jnp
from jax import lax
from jax.experimental import pallas as pl
from jax.experimental.pallas import tpu as pltpu
from jax.sharding import PartitionSpec as P

MESH = pl.DeviceIdType.MESH
SEGS = 22
TILES = 1024
SHARE = 4
VEC = 8
WIDTH = 128
ROWS = SHARE * VEC
SLOTS = 32
WINDOW = 13
PAD = 64
BLOCKS = SEGS * (SEGS + 1) // 2
DEVICES = 256
LOW_SCALE, LOW_SHIFT = 2979, 6
GROUP = 8
LINE = 8
PLANE = 32
KEYS = 4
NT_DIMS = (((1,), (1,)), ((), ()))
NN_DIMS = (((1,), (0,)), ((), ()))


def seg_low(s):
    return (s * LOW_SCALE) >> LOW_SHIFT


def seg_of(t):
    return ((t + 1) * SEGS - 1) >> 10


def first_share(s):
    return seg_low(s) >> 2


def shares(s):
    return ((seg_low(s + 1) - 1) >> 2) - first_share(s) + 1


def tri(s):
    return (s * (s + 1)) >> 1


def row_of(d, low=0, high=DEVICES):
    marks = [m * (m + 1) // 2 for m in range(1, SEGS)]
    row = sum(m <= low for m in marks)
    for m in marks:
        if low < m < high:
            row = row + (d >= m).astype(jnp.int32)
    return row


def first_group(s):
    return tri(s) >> 3


def groups_of(s):
    return ((tri(s) + s - 1) >> 3) - first_group(s) + 1


def split(a):
    hi = a.astype(jnp.bfloat16)
    lo = (a - hi.astype(jnp.float32)).astype(jnp.bfloat16)
    return hi, lo


def kernel(
    tiles_ref, rows_hbm, cols_hbm, rows_hbm2, cols_hbm2, count_hbm, x_hbm,
    image_ref, grams_ref,
    tile_buf, hi_buf, lo_buf, x_ref, rows_ref, cols_ref, rows_vec, cols_vec, count_ref,
    x_row, x_col, relay_buf, row_terms, col_terms, contrib, part_buf, part_sum, arrived,
    gram_own, gram_a, gram_b,
    in_sem, relay_send, relay_recv, pass_send, direct_send, gather_recv,
    part_send, part_recv, sum_send, col_send, arrive_recv, gram_send, gram_recv,
):
    me = lax.axis_index("tri")
    residue = me & 7
    group = me >> 3
    base = group * GROUP
    works = me < BLOCKS
    row = row_of(me)
    col = jnp.minimum(me - tri(row), row)
    off_diagonal = jnp.logical_and(works, row > col)
    on_diagonal = jnp.logical_and(works, row == col)
    top = row_of(base)
    rows_here = row_of(jnp.minimum(base + GROUP - 1, BLOCKS - 1)) - top + 1
    seg_a = seg_of(SHARE * me)
    seg_b = seg_of(SHARE * me + SHARE - 1)
    two = seg_b > seg_a

    loads = [
        pltpu.make_async_copy(src, dst, in_sem.at[n])
        for n, (src, dst) in enumerate((
            (x_hbm, x_ref), (tiles_ref, tile_buf), (rows_hbm, rows_ref), (cols_hbm, cols_ref),
            (rows_hbm2, rows_vec), (cols_hbm2, cols_vec), (count_hbm, count_ref),
        ))
    ]
    loads[0].start()

    def loop(n, body):
        def step(i, _):
            body(i)
            return 0

        lax.fori_loop(0, n, step, 0)

    def owned(body):
        body(seg_a, 0)

        @pl.when(two)
        def _():
            body(seg_b, 1)

    def span(s):
        low = jnp.maximum(tri(s), base)
        return low, jnp.minimum(tri(s) + s, base + GROUP) - low

    def relayed(body):
        def each(n):
            s = top + n
            start = (residue - first_share(s)) & 7
            for turn in range(2):
                p = start + GROUP * turn

                @pl.when(jnp.logical_and(p < shares(s), span(s)[1] > 0))
                def _():
                    body(s, p, s & 3, turn)

        loop(rows_here, each)

    def members(s, body):
        low, count = span(s)
        loop(count, lambda i: body(low + i))

    def send(src, dst, send_sem, recv_sem, dev):
        def remote():
            pltpu.make_async_remote_copy(
                src_ref=src, dst_ref=dst, send_sem=send_sem, recv_sem=recv_sem,
                device_id=(dev,), device_id_type=MESH,
            ).start()

        def local():
            pltpu.make_async_copy(src, dst, recv_sem).start()

        lax.cond(dev != me, remote, local)

    def sent(src, send_sem, dev):
        @pl.when(dev != me)
        def _():
            pltpu.make_async_copy(src, src, send_sem).wait()

    def landed(dst, recv_sem):
        pltpu.make_async_copy(dst, dst, recv_sem).wait()

    barrier = pltpu.get_barrier_semaphore()

    def greet(dev):
        @pl.when(dev != me)
        def _():
            pl.semaphore_signal(barrier, inc=1, device_id=(dev,), device_id_type=MESH)

    z, y = group & 7, me >> 6

    def rank_of(dev):
        return ((dev >> 6) << 3) + (dev & 7)

    def line(zz):
        return (y * LINE + zz) * GROUP + residue

    def plane(q):
        return ((q >> 3) * LINE + z) * GROUP + (q & 7)

    @pl.when(works)
    def _():
        loop(shares(col), lambda p: greet(first_share(col) + p))

    for dz in range(1, LINE):
        pl.semaphore_signal(barrier, inc=1, device_id=(line((z + dz) & 7),), device_id_type=MESH)
    for m in range(1, PLANE):
        pl.semaphore_signal(
            barrier, inc=1, device_id=(plane(rank_of(me) ^ m),), device_id_type=MESH
        )
    relayed(lambda s, p, key, turn: greet(first_share(s) + p))

    for load in loads[1:]:
        load.start()

    def greeters(s):
        mine = jnp.logical_and(group >= first_group(s), group < first_group(s) + groups_of(s))
        n = groups_of(s) - jnp.where(mine, 1, 0)
        return n + SEGS - s - jnp.logical_and(works, col == s).astype(jnp.int32)

    pl.semaphore_wait(barrier, LINE + PLANE - 2 + greeters(seg_a) + jnp.where(two, greeters(seg_b), 0))
    loads[0].wait()

    def to_columns(start):
        def body(s, w):
            dst = x_col.at[pl.ds((me - first_share(s)) * SHARE, SHARE)]

            def each(n):
                dev = tri(s + n) + s
                if start:
                    send(x_ref, dst, direct_send, gather_recv.at[1], dev)
                else:
                    sent(x_ref, direct_send, dev)

            loop(SEGS - s, each)

        return body

    def to_relays(start):
        def body(s, w):
            turn = (me - first_share(s)) >> 3
            dst, sem = relay_buf.at[s & 3, turn], relay_recv.at[s & 3, turn]

            def each(n):
                dev = (first_group(s) + n) * GROUP + residue
                if start:
                    send(x_ref, dst, relay_send, sem, dev)
                else:
                    sent(x_ref, relay_send, dev)

            loop(groups_of(s), each)

        return body

    owned(to_relays(True))
    owned(to_columns(True))

    for load in loads[1:]:
        load.wait()

    def split_tile(k):
        hi, lo = split(tile_buf[k])
        hi_buf[k] = hi
        lo_buf[k] = lo

    loop(SLOTS, split_tile)

    def pass_on(start):
        def body(s, p, key, turn):
            src = relay_buf.at[key, turn]
            dst = x_row.at[pl.ds(p * SHARE, SHARE)]
            if start:
                landed(src, relay_recv.at[key, turn])

            def each(dev):
                if start:
                    send(src, dst, pass_send, gather_recv.at[0], dev)
                else:
                    sent(src, pass_send, dev)

            members(s, each)

        return body

    relayed(pass_on(True))

    def wait_rows(s, held, recv_sem):
        for n in (WINDOW - 1, WINDOW):
            @pl.when(shares(s) == n)
            def _():
                landed(held.at[pl.ds(0, n * SHARE)], recv_sem)

    row_base = SHARE * first_share(row)
    col_base = SHARE * first_share(col)

    def multiply(held, ids, origin, terms, axis, dims):
        def one(k):
            hi, lo = split(held[jnp.clip(ids[k] - origin, 0, WINDOW * SHARE - 1)])
            both = jnp.concatenate([hi, lo], axis=0)
            out = lax.dot_general(
                jnp.concatenate([both, both], axis=1),
                jnp.concatenate([hi_buf[k], lo_buf[k]], axis=axis), dims,
                preferred_element_type=jnp.float32,
            )
            terms[pl.ds(pl.multiple_of(k * VEC, VEC), VEC), :] = out[:VEC] + out[VEC:]

        def several(n):
            for u in range(8):
                one(8 * n + u)

        loop(SLOTS // 8, several)

    def reduce(vec, origin, terms, which):
        live = lax.broadcasted_iota(jnp.int32, (PAD, SLOTS), 1) < count_ref[0]
        place = lax.broadcasted_iota(jnp.int32, (PAD, SLOTS), 0)
        hit = jnp.logical_and(place == vec[...] - origin, live)
        hot = hit.astype(jnp.float32).astype(jnp.bfloat16)
        hot = jnp.concatenate([hot, hot], axis=1)
        for v in range(VEC):
            hi, lo = split(terms[pl.ds(v, SLOTS, stride=VEC), :])
            contrib[which, pl.ds(v, PAD, stride=VEC), :] = lax.dot_general(
                hot, jnp.concatenate([hi, lo], axis=0), NN_DIMS,
                preferred_element_type=jnp.float32,
            )

    def chunk(which, p):
        return contrib.at[which, pl.ds(pl.multiple_of(p * ROWS, ROWS), ROWS), :]

    def row_parts(p):
        turn = p >> 3
        send(
            chunk(0, p), part_buf.at[turn, residue], part_send, part_recv.at[turn, residue],
            base + ((first_share(row) + p) & 7),
        )

    def all_sent(which, n, sem):
        for count in range(WINDOW - 3, WINDOW + 1):
            @pl.when(n == count)
            def _():
                landed(contrib.at[which, pl.ds(0, count * ROWS), :], sem)

    def place_of(owner, s):
        return jnp.where(seg_of(SHARE * owner) == s, 0, 1)

    def slot_of(owner, s):
        return place_of(owner, s) * (KEYS + SEGS)

    def col_parts(p):
        owner = first_share(col) + p
        at = slot_of(owner, col) + KEYS + row
        send(chunk(1, p), arrived.at[at], col_send, arrive_recv.at[at], owner)

    @pl.when(works)
    def _():
        wait_rows(col, x_col, gather_recv.at[1])
        multiply(x_col, cols_ref, col_base, row_terms, 1, NT_DIMS)
        reduce(rows_vec, row_base, row_terms, 0)

        @pl.when(off_diagonal)
        def _():
            loop(shares(row), row_parts)
            wait_rows(row, x_row, gather_recv.at[0])
            multiply(x_row, rows_ref, row_base, col_terms, 0, NN_DIMS)

        @pl.when(on_diagonal)
        def _():
            multiply(x_col, rows_ref, row_base, col_terms, 0, NN_DIMS)

        reduce(cols_vec, col_base, col_terms, 1)

        @pl.when(on_diagonal)
        def _():
            contrib[1] = contrib[0] + contrib[1]

        loop(shares(col), col_parts)

    owned(to_relays(False))
    owned(to_columns(False))
    relayed(pass_on(False))

    def add_parts(start):
        def body(s, p, key, turn):
            owner = first_share(s) + p
            src = part_sum.at[key, turn]
            if start:
                low, count = span(s)

                def each(i, total):
                    rank = (low + i) & 7
                    landed(part_buf.at[turn, rank], part_recv.at[turn, rank])
                    return total + part_buf[turn, rank]

                part_sum[key, turn] = lax.fori_loop(
                    0, count, each, jnp.zeros((ROWS, WIDTH), jnp.float32)
                )
                at = slot_of(owner, s) + group - first_group(s)
                send(src, arrived.at[at], sum_send, arrive_recv.at[at], owner)
            else:
                sent(src, sum_send, owner)

        return body

    relayed(add_parts(True))

    def each(at, total):
        landed(arrived.at[at], arrive_recv.at[at])
        return total + arrived[at]

    def collect(w, s, total):
        start = w * (KEYS + SEGS)
        total = lax.fori_loop(start + KEYS + s, start + KEYS + SEGS, each, total)
        return lax.fori_loop(start, start + groups_of(s), each, total)

    def put(total):
        for t in range(SHARE):
            image_ref[t] = total[t * VEC:(t + 1) * VEC]

    put(collect(0, seg_a, jnp.zeros((ROWS, WIDTH), jnp.float32)))

    @pl.when(two)
    def _():
        put(collect(1, seg_b, jnp.concatenate([image_ref[t] for t in range(SHARE)], axis=0)))

    def flat(ref):
        return jnp.concatenate([ref[t] for t in range(SHARE)], axis=1)

    image = flat(image_ref)
    both = lax.dot_general(
        jnp.concatenate([flat(x_ref), image], axis=0), image, NT_DIMS,
        precision=lax.Precision.HIGHEST, preferred_element_type=jnp.float32,
    )
    gram_own[0] = jnp.zeros((VEC, WIDTH), jnp.float32)
    gram_own[0, :, 0:VEC] = both[:VEC]
    gram_own[0, :, VEC:2 * VEC] = both[VEC:]

    def hops(m):
        return [0, 1, 2, 1][m >> 3] + [0, 1, 2, 1][(m >> 1) & 3]

    rank = rank_of(me)
    circles = (
        (gram_a, z, LINE, [line((z + dz) & 7) for dz in (4, 3, 5, 2, 6, 1, 7)]),
        (gram_b, rank, PLANE, [plane(rank ^ m) for m in sorted(range(1, PLANE), key=hops, reverse=True)]),
    )
    for n, (buf, rank, size, partners) in enumerate(circles):
        for dev in partners:
            pltpu.make_async_remote_copy(
                src_ref=gram_own.at[n], dst_ref=buf.at[rank], send_sem=gram_send.at[n],
                recv_sem=gram_recv.at[n], device_id=(dev,), device_id_type=MESH,
            ).start()

        buf[rank] = gram_own[n]
        if n == 0:
            relayed(add_parts(False))

            @pl.when(off_diagonal)
            def _():
                p = (residue - first_share(row)) & 7
                n_sent = shares(row) - 1 - (p + GROUP < shares(row)).astype(jnp.int32)
                all_sent(0, n_sent, part_send)

            @pl.when(works)
            def _():
                p = me - first_share(col)
                mine = jnp.logical_and(p >= 0, p < shares(col)).astype(jnp.int32)
                all_sent(1, shares(col) - mine, col_send)

        landed(buf.at[pl.ds(0, size - 1)], gram_recv.at[n])
        terms = [buf[q] for q in range(size)]
        while len(terms) > 1:
            terms = [a + b for a, b in zip(terms[::2], terms[1::2])]
        if n == 0:
            gram_own[1] = terms[0]
        else:
            grams_ref[...] = terms[0] * (1.0 / (TILES * WIDTH))

    for n, (buf, _rank, size, _partners) in enumerate(circles):
        landed(buf.at[pl.ds(0, size - 1)], gram_send.at[n])


def per_device(tiles, tile_rows, tile_cols, counts, block_vectors):
    f32, i32 = jnp.float32, jnp.int32
    vmem = pl.BlockSpec(memory_space=pltpu.VMEM)
    dma = pltpu.SemaphoreType.DMA
    image, grams = pl.pallas_call(
        kernel,
        out_shape=(
            pltpu.VMEM((SHARE, VEC, WIDTH), f32),
            pltpu.VMEM((VEC, WIDTH), f32),
        ),
        in_specs=[pl.BlockSpec(memory_space=pl.ANY)] * 7,
        out_specs=(vmem, vmem),
        scratch_shapes=[
            pltpu.VMEM((SLOTS, WIDTH, WIDTH), f32),
            pltpu.VMEM((SLOTS, WIDTH, WIDTH), jnp.bfloat16),
            pltpu.VMEM((SLOTS, WIDTH, WIDTH), jnp.bfloat16),
            pltpu.VMEM((SHARE, VEC, WIDTH), f32),
            pltpu.SMEM((SLOTS,), i32),
            pltpu.SMEM((SLOTS,), i32),
            pltpu.VMEM((1, SLOTS), i32),
            pltpu.VMEM((1, SLOTS), i32),
            pltpu.SMEM((1,), i32),
            pltpu.VMEM((WINDOW * SHARE, VEC, WIDTH), f32),
            pltpu.VMEM((WINDOW * SHARE, VEC, WIDTH), f32),
            pltpu.VMEM((KEYS, 2, SHARE, VEC, WIDTH), f32),
            pltpu.VMEM((SLOTS * VEC, WIDTH), f32),
            pltpu.VMEM((SLOTS * VEC, WIDTH), f32),
            pltpu.VMEM((2, PAD * VEC, WIDTH), f32),
            pltpu.VMEM((2, GROUP, ROWS, WIDTH), f32),
            pltpu.VMEM((KEYS, 2, ROWS, WIDTH), f32),
            pltpu.VMEM((2 * (KEYS + SEGS), ROWS, WIDTH), f32),
            pltpu.VMEM((2, VEC, WIDTH), f32),
            pltpu.VMEM((LINE, VEC, WIDTH), f32),
            pltpu.VMEM((PLANE, VEC, WIDTH), f32),
            dma((7,)),
            dma,
            dma((KEYS, 2)),
            dma,
            dma,
            dma((2,)),
            dma,
            dma((2, GROUP)),
            dma,
            dma,
            dma((2 * (KEYS + SEGS),)),
            dma((2,)),
            dma((2,)),
        ],
        compiler_params=pltpu.CompilerParams(
            collective_id=0, has_side_effects=True, vmem_limit_bytes=60 * 1024 * 1024
        ),
    )(
        tiles, tile_rows, tile_cols, tile_rows.reshape(1, SLOTS), tile_cols.reshape(1, SLOTS),
        counts, block_vectors,
    )
    return image, grams[:, :VEC], grams[:, VEC:2 * VEC]


def solution(mesh):
    placed = (P("tri", None, None), P("tri"), P("tri"), P("tri"), P("tri", None, None))
    return jax.shard_map(
        per_device,
        mesh=mesh,
        in_specs=placed,
        out_specs=(P("tri", None, None), P(), P()),
        check_vma=False,
    )
```

```python
import jax
import jax.numpy as jnp
from jax import lax
from jax.experimental import pallas as pl
from jax.experimental.pallas import tpu as pltpu
from jax.sharding import PartitionSpec as P

MESH = pl.DeviceIdType.MESH
SEGS = 22
TILES = 1024
SHARE = 4
VEC = 8
WIDTH = 128
ROWS = SHARE * VEC
SLOTS = 32
WINDOW = 13
PAD = 64
BLOCKS = SEGS * (SEGS + 1) // 2
DEVICES = 256
LOW_SCALE, LOW_SHIFT = 2979, 6
GROUP = 8
LINE = 8
PLANE = 32
ROWS_AT = (4, 2, 2, 2)
KEYS = 4
NT_DIMS = (((1,), (1,)), ((), ()))
NN_DIMS = (((1,), (0,)), ((), ()))


def seg_low(s):
    return (s * LOW_SCALE) >> LOW_SHIFT


def seg_of(t):
    return ((t + 1) * SEGS - 1) >> 10


def first_share(s):
    return seg_low(s) >> 2


def shares(s):
    return ((seg_low(s + 1) - 1) >> 2) - first_share(s) + 1


def tri(s):
    return (s * (s + 1)) >> 1


def row_of(d, low=0, high=DEVICES):
    marks = [m * (m + 1) // 2 for m in range(1, SEGS)]
    row = sum(m <= low for m in marks)
    for m in marks:
        if low < m < high:
            row = row + (d >= m).astype(jnp.int32)
    return row


def first_group(s):
    return tri(s) >> 3


def groups_of(s):
    return ((tri(s) + s - 1) >> 3) - first_group(s) + 1


def split(a):
    hi = a.astype(jnp.bfloat16)
    lo = (a - hi.astype(jnp.float32)).astype(jnp.bfloat16)
    return hi, lo


def kernel(
    tiles_ref, rows_hbm, cols_hbm, rows_hbm2, cols_hbm2, count_hbm, x_hbm,
    image_ref, grams_ref,
    tile_buf, hi_buf, lo_buf, x_ref, rows_ref, cols_ref, rows_vec, cols_vec, count_ref,
    x_row, x_col, relay_buf, line_buf, col_buf, col_sum, row_terms, col_terms, contrib, part_buf, part_sum, arrived,
    gram_tile, gram_own, gram_a, gram_b,
    in_sem, relay_send, relay_recv, pass_send, line_send, line_recv, spread_send, gather_recv,
    part_send, part_recv, sum_send, col_send, col_recv, back_send, arrive_recv, gram_send, gram_recv,
):
    me = lax.axis_index("tri")
    residue = me & 7
    group = me >> 3
    base = group * GROUP
    works = me < BLOCKS
    row = row_of(me)
    col = jnp.minimum(me - tri(row), row)
    off_diagonal = jnp.logical_and(works, row > col)
    on_diagonal = jnp.logical_and(works, row == col)
    top = row_of(base)
    rows_here = row_of(jnp.minimum(base + GROUP - 1, BLOCKS - 1)) - top + 1
    seg_a = seg_of(SHARE * me)
    seg_b = seg_of(SHARE * me + SHARE - 1)
    two = seg_b > seg_a

    loads = [
        pltpu.make_async_copy(src, dst, in_sem.at[n])
        for n, (src, dst) in enumerate((
            (x_hbm, x_ref), (tiles_ref, tile_buf), (rows_hbm, rows_ref), (cols_hbm, cols_ref),
            (rows_hbm2, rows_vec), (cols_hbm2, cols_vec), (count_hbm, count_ref),
        ))
    ]
    def loop(n, body):
        def step(i, _):
            body(i)
            return 0

        lax.fori_loop(0, n, step, 0)

    def owned(body):
        body(seg_a, 0)

        @pl.when(two)
        def _():
            body(seg_b, 1)

    def span(s):
        low = jnp.maximum(tri(s), base)
        return low, jnp.minimum(tri(s) + s, base + GROUP) - low

    def relayed(body):
        def each(n):
            s = top + n
            start = (residue - first_share(s)) & 7
            for turn in range(2):
                p = start + GROUP * turn

                @pl.when(jnp.logical_and(p < shares(s), span(s)[1] > 0))
                def _():
                    body(s, p, s & 3, turn)

        loop(rows_here, each)

    def members(s, body):
        low, count = span(s)
        loop(count, lambda i: body(low + i))

    def send(src, dst, send_sem, recv_sem, dev):
        def remote():
            pltpu.make_async_remote_copy(
                src_ref=src, dst_ref=dst, send_sem=send_sem, recv_sem=recv_sem,
                device_id=(dev,), device_id_type=MESH,
            ).start()

        def local():
            pltpu.make_async_copy(src, dst, recv_sem).start()

        lax.cond(dev != me, remote, local)

    def sent(src, send_sem, dev):
        @pl.when(dev != me)
        def _():
            pltpu.make_async_copy(src, src, send_sem).wait()

    def landed(dst, recv_sem):
        pltpu.make_async_copy(dst, dst, recv_sem).wait()

    barrier = pltpu.get_barrier_semaphore()

    def greet(dev):
        @pl.when(dev != me)
        def _():
            pl.semaphore_signal(barrier, inc=1, device_id=(dev,), device_id_type=MESH)

    z, y = group & 7, me >> 6

    def rank_of(dev):
        return ((dev >> 6) << 3) + (dev & 7)

    def line(zz):
        return (y * LINE + zz) * GROUP + residue

    def plane(q):
        return ((q >> 3) * LINE + z) * GROUP + (q & 7)

    relayed(lambda s, p, key, turn: greet(first_share(s) + p))
    for dz in (4, 3, 5, 2, 6, 1, 7):
        pl.semaphore_signal(barrier, inc=1, device_id=(line((z + dz) & 7),), device_id_type=MESH)
    def hops(m):
        return [0, 1, 2, 1][m >> 3] + [0, 1, 2, 1][(m >> 1) & 3]

    far_first = sorted(range(1, PLANE), key=hops, reverse=True)
    for m in far_first:
        pl.semaphore_signal(
            barrier, inc=1, device_id=(plane(rank_of(me) ^ m),), device_id_type=MESH
        )
    def greeters(s):
        mine = jnp.logical_and(group >= first_group(s), group < first_group(s) + groups_of(s))
        return groups_of(s) - jnp.where(mine, 1, 0)

    pl.semaphore_wait(barrier, LINE + PLANE - 2 + greeters(seg_a) + jnp.where(two, greeters(seg_b), 0))

    def near_first(n):
        return (z + jnp.where((n & 1) == 1, (n + 1) >> 1, LINE - (n >> 1))) & 7

    def targets(zz, body):
        owner = line(zz)
        a, b = seg_of(SHARE * owner), seg_of(SHARE * owner + SHARE - 1)

        def one(w):
            s = a + w
            p = owner - first_share(s)
            for k, first, low in here:
                dev = first + s

                @pl.when(jnp.logical_and(((dev - low) >> 3) == 0, s <= k))
                def _(dev=dev):
                    body(dev, s, p)

        loop(1 + (b > a).astype(jnp.int32), one)

    def to_line(n):
        zz = near_first(LINE - 1 - n)
        send(x_hbm, line_buf.at[z], line_send, line_recv.at[z], line(zz))

    def spread(start):
        def each(n):
            zz = near_first(n)
            src = line_buf.at[zz]
            if start:
                landed(src, line_recv.at[zz])

            def body(dev, s, p):
                if start:
                    dst = x_col.at[pl.ds(p * SHARE, SHARE)]
                    send(src, dst, spread_send, gather_recv.at[1], dev)
                else:
                    sent(src, spread_send, dev)

            targets(zz, body)

        loop(LINE, each)

    def to_relays(start):
        def body(s, w):
            turn = (me - first_share(s)) >> 3
            dst, sem = relay_buf.at[s & 3, turn], relay_recv.at[s & 3, turn]

            def each(n):
                dev = (first_group(s) + n) * GROUP + residue
                if start:
                    send(x_hbm, dst, relay_send, sem, dev)
                else:
                    sent(x_hbm, relay_send, dev)

            loop(groups_of(s), each)

        return body

    loop(LINE, to_line)
    owned(to_relays(True))

    for load in loads:
        load.start()

    here = []
    for yy in (2, 1, 3, 0):
        low = yy * 64 + z * GROUP
        first_row = row_of(low, yy * 64, yy * 64 + 64)
        for k in [first_row + i for i in range(ROWS_AT[yy])]:
            here.append((k, jnp.where(k < SEGS, tri(k), 2 * DEVICES), low))

    for load in loads:
        load.wait()

    def split_tile(k):
        hi, lo = split(tile_buf[k])
        hi_buf[k] = hi
        lo_buf[k] = lo

    loop(SLOTS, split_tile)

    def pass_on(start):
        def body(s, p, key, turn):
            src = relay_buf.at[key, turn]
            dst = x_row.at[pl.ds(p * SHARE, SHARE)]
            if start:
                landed(src, relay_recv.at[key, turn])

            def each(dev):
                if start:
                    send(src, dst, pass_send, gather_recv.at[0], dev)
                else:
                    sent(src, pass_send, dev)

            members(s, each)

        return body

    spread(True)
    relayed(pass_on(True))

    def wait_rows(s, held, recv_sem):
        for n in (WINDOW - 1, WINDOW):
            @pl.when(shares(s) == n)
            def _():
                landed(held.at[pl.ds(0, n * SHARE)], recv_sem)

    row_base = SHARE * first_share(row)
    col_base = SHARE * first_share(col)

    def multiply(held, ids, origin, terms, axis, dims):
        def one(k):
            hi, lo = split(held[jnp.clip(ids[k] - origin, 0, WINDOW * SHARE - 1)])
            both = jnp.concatenate([hi, lo], axis=0)
            out = lax.dot_general(
                jnp.concatenate([both, both], axis=1),
                jnp.concatenate([hi_buf[k], lo_buf[k]], axis=axis), dims,
                preferred_element_type=jnp.float32,
            )
            terms[pl.ds(pl.multiple_of(k * VEC, VEC), VEC), :] = out[:VEC] + out[VEC:]

        def several(n):
            for u in range(8):
                one(8 * n + u)

        loop(SLOTS // 8, several)

    def reduce(vec, origin, terms, which):
        live = lax.broadcasted_iota(jnp.int32, (PAD, SLOTS), 1) < count_ref[0]
        place = lax.broadcasted_iota(jnp.int32, (PAD, SLOTS), 0)
        hit = jnp.logical_and(place == vec[...] - origin, live)
        hot = hit.astype(jnp.float32).astype(jnp.bfloat16)
        hot = jnp.concatenate([hot, hot], axis=1)
        for v in range(VEC):
            hi, lo = split(terms[pl.ds(v, SLOTS, stride=VEC), :])
            contrib[which, pl.ds(v, PAD, stride=VEC), :] = lax.dot_general(
                hot, jnp.concatenate([hi, lo], axis=0), NN_DIMS,
                preferred_element_type=jnp.float32,
            )

    def chunk(which, p):
        return contrib.at[which, pl.ds(pl.multiple_of(p * ROWS, ROWS), ROWS), :]

    def row_parts(p):
        turn = p >> 3
        send(
            chunk(0, p), part_buf.at[turn, residue], part_send, part_recv.at[turn, residue],
            base + ((first_share(row) + p) & 7),
        )

    def all_sent(which, s, same_y, sem):
        n = shares(s)
        for turn in range(2):
            p = ((residue - first_share(s)) & 7) + GROUP * turn
            mine = p < shares(s)
            if same_y:
                mine = jnp.logical_and(mine, ((first_share(s) + p) >> 6) == y)
            n = n - mine.astype(jnp.int32)
        for count in range(WINDOW - 3, WINDOW + 1):
            @pl.when(n == count)
            def _():
                landed(contrib.at[which, pl.ds(0, count * ROWS), :], sem)

    def place_of(owner, s):
        return jnp.where(seg_of(SHARE * owner) == s, 0, 1)

    def col_parts(p):
        owner = first_share(col) + p
        at = rank_of(me) * 2 + (p >> 3)
        dev = (((owner >> 6) << 3) + z) * GROUP + (owner & 7)
        send(chunk(1, p), col_buf.at[at], col_send, col_recv.at[at], dev)

    @pl.when(works)
    def _():
        wait_rows(col, x_col, gather_recv.at[1])
        multiply(x_col, cols_ref, col_base, row_terms, 1, NT_DIMS)
        reduce(rows_vec, row_base, row_terms, 0)

        @pl.when(off_diagonal)
        def _():
            loop(shares(row), row_parts)
            wait_rows(row, x_row, gather_recv.at[0])
            multiply(x_row, rows_ref, row_base, col_terms, 0, NN_DIMS)

        @pl.when(on_diagonal)
        def _():
            multiply(x_col, rows_ref, row_base, col_terms, 0, NN_DIMS)

        reduce(cols_vec, col_base, col_terms, 1)

        @pl.when(on_diagonal)
        def _():
            contrib[1] = contrib[0] + contrib[1]

        loop(shares(col), col_parts)

    landed(line_buf.at[pl.ds(0, LINE - 1)], line_send)
    owned(to_relays(False))
    spread(False)
    relayed(pass_on(False))

    def add_parts(start):
        def body(s, p, key, turn):
            owner = first_share(s) + p
            src = part_sum.at[key, turn]
            if start:
                low, count = span(s)

                def each(i, total):
                    rank = (low + i) & 7
                    landed(part_buf.at[turn, rank], part_recv.at[turn, rank])
                    return total + part_buf[turn, rank]

                part_sum[key, turn] = lax.fori_loop(
                    0, count, each, jnp.zeros((ROWS, WIDTH), jnp.float32)
                )
                at = place_of(owner, s) * KEYS + group - first_group(s)
                send(src, arrived.at[at], sum_send, arrive_recv.at[at], owner)
            else:
                sent(src, sum_send, owner)

        return body

    def add_cols(n):
        zz = near_first(LINE - 1 - n)
        col_sum[zz] = jnp.zeros((ROWS, WIDTH), jnp.float32)

        def body(dev, s, p):
            at = rank_of(dev) * 2 + (p >> 3)
            landed(col_buf.at[at], col_recv.at[at])
            col_sum[zz] = col_sum[zz] + col_buf[at]

        targets(zz, body)
        at = 2 * KEYS + z
        send(col_sum.at[zz], arrived.at[at], back_send, arrive_recv.at[at], line(zz))

    relayed(add_parts(True))
    loop(LINE, add_cols)

    def each(at, total):
        landed(arrived.at[at], arrive_recv.at[at])
        return total + arrived[at]

    def collect(w, s, total):
        return lax.fori_loop(w * KEYS, w * KEYS + groups_of(s), each, total)

    def put(total):
        for t in range(SHARE):
            image_ref[t] = total[t * VEC:(t + 1) * VEC]

    total = collect(0, seg_a, jnp.zeros((ROWS, WIDTH), jnp.float32))
    put(lax.fori_loop(2 * KEYS, 2 * KEYS + LINE, each, total))

    @pl.when(two)
    def _():
        put(collect(1, seg_b, jnp.concatenate([image_ref[t] for t in range(SHARE)], axis=0)))

    def flat(ref):
        return jnp.concatenate([ref[t] for t in range(SHARE)], axis=1)

    image = flat(image_ref)
    both = lax.dot_general(
        jnp.concatenate([flat(x_ref), image], axis=0), image, NT_DIMS,
        precision=lax.Precision.HIGHEST, preferred_element_type=jnp.float32,
    )
    gram_tile[...] = jnp.zeros((VEC, WIDTH), jnp.float32)
    gram_tile[:, 0:VEC] = both[:VEC]
    gram_tile[:, VEC:2 * VEC] = both[VEC:]
    moved = pltpu.roll(gram_tile[...], 0, 1, stride=2 * VEC, stride_axis=0)
    gram_own[0] = jnp.sum(moved, axis=0, keepdims=True)

    rank = rank_of(me)
    circles = (
        (gram_a, z, LINE, [line((z + dz) & 7) for dz in (4, 3, 5, 2, 6, 1, 7)]),
        (gram_b, rank, PLANE, [plane(rank ^ m) for m in far_first]),
    )
    for n, (buf, rank, size, partners) in enumerate(circles):
        for dev in partners:
            pltpu.make_async_remote_copy(
                src_ref=gram_own.at[n], dst_ref=buf.at[rank], send_sem=gram_send.at[n],
                recv_sem=gram_recv.at[n], device_id=(dev,), device_id_type=MESH,
            ).start()

        buf[rank] = gram_own[n]
        if n == 0:
            relayed(add_parts(False))

            @pl.when(off_diagonal)
            def _():
                all_sent(0, row, False, part_send)

            @pl.when(works)
            def _():
                all_sent(1, col, True, col_send)

            landed(col_sum.at[pl.ds(0, LINE - 1)], back_send)

        landed(buf.at[pl.ds(0, size - 1)], gram_recv.at[n])
        terms = [buf[q] for q in range(size)]
        while len(terms) > 1:
            terms = [a + b for a, b in zip(terms[::2], terms[1::2])]
        if n == 0:
            gram_own[1] = terms[0]
        else:
            grams_ref[...] = terms[0] * (1.0 / (TILES * WIDTH))

    for n, (buf, _rank, size, _partners) in enumerate(circles):
        landed(buf.at[pl.ds(0, size - 1)], gram_send.at[n])


def per_device(tiles, tile_rows, tile_cols, counts, block_vectors):
    f32, i32 = jnp.float32, jnp.int32
    vmem = pl.BlockSpec(memory_space=pltpu.VMEM)
    dma = pltpu.SemaphoreType.DMA
    image, grams = pl.pallas_call(
        kernel,
        out_shape=(
            pltpu.VMEM((SHARE, VEC, WIDTH), f32),
            pltpu.VMEM((1, WIDTH), f32),
        ),
        in_specs=[pl.BlockSpec(memory_space=pl.ANY)] * 7,
        out_specs=(vmem, vmem),
        scratch_shapes=[
            pltpu.VMEM((SLOTS, WIDTH, WIDTH), f32),
            pltpu.VMEM((SLOTS, WIDTH, WIDTH), jnp.bfloat16),
            pltpu.VMEM((SLOTS, WIDTH, WIDTH), jnp.bfloat16),
            pltpu.VMEM((SHARE, VEC, WIDTH), f32),
            pltpu.SMEM((SLOTS,), i32),
            pltpu.SMEM((SLOTS,), i32),
            pltpu.VMEM((1, SLOTS), i32),
            pltpu.VMEM((1, SLOTS), i32),
            pltpu.SMEM((1,), i32),
            pltpu.VMEM((WINDOW * SHARE, VEC, WIDTH), f32),
            pltpu.VMEM((WINDOW * SHARE, VEC, WIDTH), f32),
            pltpu.VMEM((KEYS, 2, SHARE, VEC, WIDTH), f32),
            pltpu.VMEM((LINE, SHARE, VEC, WIDTH), f32),
            pltpu.VMEM((2 * PLANE, ROWS, WIDTH), f32),
            pltpu.VMEM((LINE, ROWS, WIDTH), f32),
            pltpu.VMEM((SLOTS * VEC, WIDTH), f32),
            pltpu.VMEM((SLOTS * VEC, WIDTH), f32),
            pltpu.VMEM((2, PAD * VEC, WIDTH), f32),
            pltpu.VMEM((2, GROUP, ROWS, WIDTH), f32),
            pltpu.VMEM((KEYS, 2, ROWS, WIDTH), f32),
            pltpu.VMEM((2 * KEYS + LINE, ROWS, WIDTH), f32),
            pltpu.VMEM((VEC, WIDTH), f32),
            pltpu.VMEM((2, 1, WIDTH), f32),
            pltpu.VMEM((LINE, 1, WIDTH), f32),
            pltpu.VMEM((PLANE, 1, WIDTH), f32),
            dma((7,)),
            dma,
            dma((KEYS, 2)),
            dma,
            dma,
            dma((LINE,)),
            dma,
            dma((2,)),
            dma,
            dma((2, GROUP)),
            dma,
            dma,
            dma((2 * PLANE,)),
            dma,
            dma((2 * KEYS + LINE,)),
            dma((2,)),
            dma((2,)),
        ],
        compiler_params=pltpu.CompilerParams(
            collective_id=0, has_side_effects=True, vmem_limit_bytes=60 * 1024 * 1024
        ),
    )(
        tiles, tile_rows, tile_cols, tile_rows.reshape(1, SLOTS), tile_cols.reshape(1, SLOTS),
        counts, block_vectors,
    )
    grams = grams.reshape(VEC, 2 * VEC)
    return image, grams[:, :VEC], grams[:, VEC:]


def solution(mesh):
    placed = (P("tri", None, None), P("tri"), P("tri"), P("tri"), P("tri", None, None))
    return jax.shard_map(
        per_device,
        mesh=mesh,
        in_specs=placed,
        out_specs=(P("tri", None, None), P(), P()),
        check_vma=False,
    )
```

```python
import jax
import jax.numpy as jnp
from jax import lax
from jax.experimental import pallas as pl
from jax.experimental.pallas import tpu as pltpu
from jax.sharding import PartitionSpec as P

MESH = pl.DeviceIdType.MESH
SEGS = 22
TILES = 1024
SHARE = 4
VEC = 8
WIDTH = 128
ROWS = SHARE * VEC
SLOTS = 32
WINDOW = 13
PAD = 64
BLOCKS = SEGS * (SEGS + 1) // 2
DEVICES = 256
LOW_SCALE, LOW_SHIFT = 2979, 6
GROUP = 8
LINE = 8
PLANE = 32
ROWS_AT = (4, 2, 2, 2)
KEYS = 4
NT_DIMS = (((1,), (1,)), ((), ()))
NN_DIMS = (((1,), (0,)), ((), ()))


def seg_low(s):
    return (s * LOW_SCALE) >> LOW_SHIFT


def seg_of(t):
    return ((t + 1) * SEGS - 1) >> 10


def first_share(s):
    return seg_low(s) >> 2


def shares(s):
    return ((seg_low(s + 1) - 1) >> 2) - first_share(s) + 1


def tri(s):
    return (s * (s + 1)) >> 1


def row_of(d, low=0, high=DEVICES):
    marks = [m * (m + 1) // 2 for m in range(1, SEGS)]
    row = sum(m <= low for m in marks)
    for m in marks:
        if low < m < high:
            row = row + (d >= m).astype(jnp.int32)
    return row


def first_group(s):
    return tri(s) >> 3


def groups_of(s):
    return ((tri(s) + s - 1) >> 3) - first_group(s) + 1


def split(a):
    hi = a.astype(jnp.bfloat16)
    lo = (a - hi.astype(jnp.float32)).astype(jnp.bfloat16)
    return hi, lo


def kernel(
    tiles_ref, rows_hbm, cols_hbm, rows_hbm2, cols_hbm2, count_hbm, x_hbm,
    image_ref, grams_ref,
    tile_buf, hi_buf, lo_buf, x_ref, rows_ref, cols_ref, rows_vec, cols_vec, count_ref,
    x_row, x_col, relay_buf, line_buf, col_buf, col_sum, row_terms, col_terms, contrib, part_buf, part_sum, arrived,
    gram_tile, gram_own, gram_a, gram_b,
    in_sem, relay_send, relay_recv, pass_send, line_send, line_recv, spread_send, gather_recv,
    part_send, part_recv, sum_send, col_send, col_recv, back_send, arrive_recv, gram_send, gram_recv,
):
    me = lax.axis_index("tri")
    residue = me & 7
    group = me >> 3
    base = group * GROUP
    works = me < BLOCKS
    row = row_of(me)
    col = jnp.minimum(me - tri(row), row)
    off_diagonal = jnp.logical_and(works, row > col)
    on_diagonal = jnp.logical_and(works, row == col)
    top = row_of(base)
    rows_here = row_of(jnp.minimum(base + GROUP - 1, BLOCKS - 1)) - top + 1
    seg_a = seg_of(SHARE * me)
    seg_b = seg_of(SHARE * me + SHARE - 1)
    two = seg_b > seg_a

    loads = [
        pltpu.make_async_copy(src, dst, in_sem.at[n])
        for n, (src, dst) in enumerate((
            (x_hbm, x_ref), (tiles_ref, tile_buf), (rows_hbm, rows_ref), (cols_hbm, cols_ref),
            (rows_hbm2, rows_vec), (cols_hbm2, cols_vec), (count_hbm, count_ref),
        ))
    ]
    def loop(n, body):
        def step(i, _):
            body(i)
            return 0

        lax.fori_loop(0, n, step, 0)

    def owned(body):
        body(seg_a, 0)

        @pl.when(two)
        def _():
            body(seg_b, 1)

    def span(s):
        low = jnp.maximum(tri(s), base)
        return low, jnp.minimum(tri(s) + s, base + GROUP) - low

    def relayed(body):
        def each(n):
            s = top + n
            start = (residue - first_share(s)) & 7
            for turn in range(2):
                p = start + GROUP * turn

                @pl.when(jnp.logical_and(p < shares(s), span(s)[1] > 0))
                def _():
                    body(s, p, s & 3, turn)

        loop(rows_here, each)

    def members(s, body):
        low, count = span(s)
        loop(count, lambda i: body(low + i))

    def send(src, dst, send_sem, recv_sem, dev):
        def remote():
            pltpu.make_async_remote_copy(
                src_ref=src, dst_ref=dst, send_sem=send_sem, recv_sem=recv_sem,
                device_id=(dev,), device_id_type=MESH,
            ).start()

        def local():
            pltpu.make_async_copy(src, dst, recv_sem).start()

        lax.cond(dev != me, remote, local)

    def sent(src, send_sem, dev):
        @pl.when(dev != me)
        def _():
            pltpu.make_async_copy(src, src, send_sem).wait()

    def landed(dst, recv_sem):
        pltpu.make_async_copy(dst, dst, recv_sem).wait()

    barrier = pltpu.get_barrier_semaphore()

    def greet(dev):
        @pl.when(dev != me)
        def _():
            pl.semaphore_signal(barrier, inc=1, device_id=(dev,), device_id_type=MESH)

    z, y = group & 7, me >> 6

    def rank_of(dev):
        return ((dev >> 6) << 3) + (dev & 7)

    def line(zz):
        return (y * LINE + zz) * GROUP + residue

    def plane(q):
        return ((q >> 3) * LINE + z) * GROUP + (q & 7)

    relayed(lambda s, p, key, turn: greet(first_share(s) + p))
    for dz in (4, 3, 5, 2, 6, 1, 7):
        pl.semaphore_signal(barrier, inc=1, device_id=(line((z + dz) & 7),), device_id_type=MESH)
    def hops(m):
        return [0, 1, 2, 1][m >> 3] + [0, 1, 2, 1][(m >> 1) & 3]

    far_first = sorted(range(1, PLANE), key=hops, reverse=True)
    for m in far_first:
        pl.semaphore_signal(
            barrier, inc=1, device_id=(plane(rank_of(me) ^ m),), device_id_type=MESH
        )
    def greeters(s):
        mine = jnp.logical_and(group >= first_group(s), group < first_group(s) + groups_of(s))
        return groups_of(s) - jnp.where(mine, 1, 0)

    pl.semaphore_wait(barrier, LINE + PLANE - 2 + greeters(seg_a) + jnp.where(two, greeters(seg_b), 0))

    def near_first(n):
        return (z + jnp.where((n & 1) == 1, (n + 1) >> 1, LINE - (n >> 1))) & 7

    def targets(zz, body):
        owner = line(zz)
        a, b = seg_of(SHARE * owner), seg_of(SHARE * owner + SHARE - 1)

        def one(w):
            s = a + w
            p = owner - first_share(s)
            for k, first, low in here:
                dev = first + s

                @pl.when(jnp.logical_and(((dev - low) >> 3) == 0, s <= k))
                def _(dev=dev):
                    body(dev, s, p)

        loop(1 + (b > a).astype(jnp.int32), one)

    def to_line(n):
        zz = near_first(LINE - 1 - n)
        send(x_hbm, line_buf.at[z], line_send, line_recv.at[z], line(zz))

    def spread(start):
        def each(n):
            zz = near_first(n)
            src = line_buf.at[zz]
            if start:
                landed(src, line_recv.at[zz])

            def body(dev, s, p):
                if start:
                    dst = x_col.at[pl.ds(p * SHARE, SHARE)]
                    send(src, dst, spread_send, gather_recv.at[1], dev)
                else:
                    sent(src, spread_send, dev)

            targets(zz, body)

        loop(LINE, each)

    def to_relays(start):
        def body(s, w):
            turn = (me - first_share(s)) >> 3
            dst, sem = relay_buf.at[s & 3, turn], relay_recv.at[s & 3, turn]

            def each(n):
                dev = (first_group(s) + n) * GROUP + residue
                if start:
                    send(x_hbm, dst, relay_send, sem, dev)
                else:
                    sent(x_hbm, relay_send, dev)

            loop(groups_of(s), each)

        return body

    loop(LINE, to_line)
    owned(to_relays(True))

    for load in loads:
        load.start()

    here = []
    for yy in (2, 1, 3, 0):
        low = yy * 64 + z * GROUP
        first_row = row_of(low, yy * 64, yy * 64 + 64)
        for k in [first_row + i for i in range(ROWS_AT[yy])]:
            here.append((k, jnp.where(k < SEGS, tri(k), 2 * DEVICES), low))

    for load in loads:
        load.wait()

    def split_tile(k):
        hi, lo = split(tile_buf[k])
        hi_buf[k] = hi
        lo_buf[k] = lo

    loop(SLOTS, split_tile)

    def pass_on(start):
        def body(s, p, key, turn):
            src = relay_buf.at[key, turn]
            dst = x_row.at[pl.ds(p * SHARE, SHARE)]
            if start:
                landed(src, relay_recv.at[key, turn])

            def each(dev):
                if start:
                    send(src, dst, pass_send, gather_recv.at[0], dev)
                else:
                    sent(src, pass_send, dev)

            members(s, each)

        return body

    spread(True)
    relayed(pass_on(True))

    def wait_rows(s, held, recv_sem):
        for n in (WINDOW - 1, WINDOW):
            @pl.when(shares(s) == n)
            def _():
                landed(held.at[pl.ds(0, n * SHARE)], recv_sem)

    row_base = SHARE * first_share(row)
    col_base = SHARE * first_share(col)

    def multiply(held, ids, origin, terms, axis, dims):
        def one(k):
            hi, lo = split(held[jnp.clip(ids[k] - origin, 0, WINDOW * SHARE - 1)])
            both = jnp.concatenate([hi, lo], axis=0)
            out = lax.dot_general(
                jnp.concatenate([both, both], axis=1),
                jnp.concatenate([hi_buf[k], lo_buf[k]], axis=axis), dims,
                preferred_element_type=jnp.float32,
            )
            terms[pl.ds(pl.multiple_of(k * VEC, VEC), VEC), :] = out[:VEC] + out[VEC:]

        def several(n):
            for u in range(8):
                one(8 * n + u)

        loop(SLOTS // 8, several)

    def reduce(vec, origin, terms, which):
        live = lax.broadcasted_iota(jnp.int32, (PAD, SLOTS), 1) < count_ref[0]
        place = lax.broadcasted_iota(jnp.int32, (PAD, SLOTS), 0)
        hit = jnp.logical_and(place == vec[...] - origin, live)
        hot = hit.astype(jnp.float32).astype(jnp.bfloat16)
        hot = jnp.concatenate([hot, hot], axis=1)
        for v in range(VEC):
            hi, lo = split(terms[pl.ds(v, SLOTS, stride=VEC), :])
            contrib[which, pl.ds(v, PAD, stride=VEC), :] = lax.dot_general(
                hot, jnp.concatenate([hi, lo], axis=0), NN_DIMS,
                preferred_element_type=jnp.float32,
            )

    def chunk(which, p):
        return contrib.at[which, pl.ds(pl.multiple_of(p * ROWS, ROWS), ROWS), :]

    def row_parts(p):
        turn = p >> 3
        send(
            chunk(0, p), part_buf.at[turn, residue], part_send, part_recv.at[turn, residue],
            base + ((first_share(row) + p) & 7),
        )

    def all_sent(which, s, same_y, sem):
        n = shares(s)
        for turn in range(2):
            p = ((residue - first_share(s)) & 7) + GROUP * turn
            mine = p < shares(s)
            if same_y:
                mine = jnp.logical_and(mine, ((first_share(s) + p) >> 6) == y)
            n = n - mine.astype(jnp.int32)
        for count in range(WINDOW - 3, WINDOW + 1):
            @pl.when(n == count)
            def _():
                landed(contrib.at[which, pl.ds(0, count * ROWS), :], sem)

    def place_of(owner, s):
        return jnp.where(seg_of(SHARE * owner) == s, 0, 1)

    def col_parts(p):
        owner = first_share(col) + p
        at = rank_of(me) * 2 + (p >> 3)
        dev = (((owner >> 6) << 3) + z) * GROUP + (owner & 7)
        send(chunk(1, p), col_buf.at[at], col_send, col_recv.at[at], dev)

    @pl.when(works)
    def _():
        wait_rows(col, x_col, gather_recv.at[1])
        multiply(x_col, cols_ref, col_base, row_terms, 1, NT_DIMS)
        reduce(rows_vec, row_base, row_terms, 0)

        @pl.when(off_diagonal)
        def _():
            loop(shares(row), row_parts)
            wait_rows(row, x_row, gather_recv.at[0])
            multiply(x_row, rows_ref, row_base, col_terms, 0, NN_DIMS)

        @pl.when(on_diagonal)
        def _():
            multiply(x_col, rows_ref, row_base, col_terms, 0, NN_DIMS)

        reduce(cols_vec, col_base, col_terms, 1)

        @pl.when(on_diagonal)
        def _():
            contrib[1] = contrib[0] + contrib[1]

        loop(shares(col), col_parts)

    landed(line_buf.at[pl.ds(0, LINE - 1)], line_send)
    owned(to_relays(False))
    spread(False)
    relayed(pass_on(False))

    def add_parts(start):
        def body(s, p, key, turn):
            owner = first_share(s) + p
            src = part_sum.at[key, turn]
            if start:
                low, count = span(s)

                def each(i, total):
                    rank = (low + i) & 7
                    landed(part_buf.at[turn, rank], part_recv.at[turn, rank])
                    return total + part_buf[turn, rank]

                part_sum[key, turn] = lax.fori_loop(
                    0, count, each, jnp.zeros((ROWS, WIDTH), jnp.float32)
                )
                at = place_of(owner, s) * KEYS + group - first_group(s)
                send(src, arrived.at[at], sum_send, arrive_recv.at[at], owner)
            else:
                sent(src, sum_send, owner)

        return body

    def add_cols(n):
        zz = near_first(LINE - 1 - n)
        col_sum[zz] = jnp.zeros((ROWS, WIDTH), jnp.float32)

        def body(dev, s, p):
            at = rank_of(dev) * 2 + (p >> 3)
            landed(col_buf.at[at], col_recv.at[at])
            col_sum[zz] = col_sum[zz] + col_buf[at]

        targets(zz, body)
        at = 2 * KEYS + z
        send(col_sum.at[zz], arrived.at[at], back_send, arrive_recv.at[at], line(zz))

    relayed(add_parts(True))
    loop(LINE, add_cols)

    def each(at, total):
        landed(arrived.at[at], arrive_recv.at[at])
        return total + arrived[at]

    def collect(w, s, total):
        return lax.fori_loop(w * KEYS, w * KEYS + groups_of(s), each, total)

    def put(total):
        for t in range(SHARE):
            image_ref[t] = total[t * VEC:(t + 1) * VEC]

    total = collect(0, seg_a, jnp.zeros((ROWS, WIDTH), jnp.float32))
    put(lax.fori_loop(2 * KEYS, 2 * KEYS + LINE, each, total))

    @pl.when(two)
    def _():
        put(collect(1, seg_b, jnp.concatenate([image_ref[t] for t in range(SHARE)], axis=0)))

    def flat(ref):
        return jnp.concatenate([ref[t] for t in range(SHARE)], axis=1)

    image = flat(image_ref)
    both = lax.dot_general(
        jnp.concatenate([flat(x_ref), image], axis=0), image, NT_DIMS,
        precision=lax.Precision.HIGHEST, preferred_element_type=jnp.float32,
    )
    gram_tile[...] = jnp.zeros((VEC, WIDTH), jnp.float32)
    gram_tile[:, 0:VEC] = both[:VEC]
    gram_tile[:, VEC:2 * VEC] = both[VEC:]
    moved = pltpu.roll(gram_tile[...], 0, 1, stride=2 * VEC, stride_axis=0)
    gram_own[0] = jnp.sum(moved, axis=0, keepdims=True)

    rank = rank_of(me)
    circles = (
        (gram_a, z, LINE, [line((z + dz) & 7) for dz in (4, 3, 5, 2, 6, 1, 7)]),
        (gram_b, rank, PLANE, [plane(rank ^ m) for m in far_first]),
    )
    for n, (buf, rank, size, partners) in enumerate(circles):
        for dev in partners:
            pltpu.make_async_remote_copy(
                src_ref=gram_own.at[n], dst_ref=buf.at[rank], send_sem=gram_send.at[n],
                recv_sem=gram_recv.at[n], device_id=(dev,), device_id_type=MESH,
            ).start()

        buf[rank] = gram_own[n]
        if n == 0:
            relayed(add_parts(False))

            @pl.when(off_diagonal)
            def _():
                all_sent(0, row, False, part_send)

            @pl.when(works)
            def _():
                all_sent(1, col, True, col_send)

            landed(col_sum.at[pl.ds(0, LINE - 1)], back_send)

        landed(buf.at[pl.ds(0, size - 1)], gram_recv.at[n])
        terms = [buf[q] for q in range(size)]
        while len(terms) > 1:
            terms = [a + b for a, b in zip(terms[::2], terms[1::2])]
        if n == 0:
            gram_own[1] = terms[0]
        else:
            out = jnp.broadcast_to(terms[0] * (1.0 / (TILES * WIDTH)), (VEC, WIDTH))
            block = lax.broadcasted_iota(jnp.int32, (VEC, WIDTH), 1) >> 4
            out = jnp.where(block == lax.broadcasted_iota(jnp.int32, (VEC, WIDTH), 0), out, 0.0)
            for shift in (64, 32, 16):
                out = out + pltpu.roll(out, shift, 1)
            grams_ref[...] = out

    for n, (buf, _rank, size, _partners) in enumerate(circles):
        landed(buf.at[pl.ds(0, size - 1)], gram_send.at[n])


def per_device(tiles, tile_rows, tile_cols, counts, block_vectors):
    f32, i32 = jnp.float32, jnp.int32
    vmem = pl.BlockSpec(memory_space=pltpu.VMEM)
    dma = pltpu.SemaphoreType.DMA
    image, grams = pl.pallas_call(
        kernel,
        out_shape=(
            pltpu.VMEM((SHARE, VEC, WIDTH), f32),
            pltpu.VMEM((VEC, WIDTH), f32),
        ),
        in_specs=[pl.BlockSpec(memory_space=pl.ANY)] * 7,
        out_specs=(vmem, vmem),
        scratch_shapes=[
            pltpu.VMEM((SLOTS, WIDTH, WIDTH), f32),
            pltpu.VMEM((SLOTS, WIDTH, WIDTH), jnp.bfloat16),
            pltpu.VMEM((SLOTS, WIDTH, WIDTH), jnp.bfloat16),
            pltpu.VMEM((SHARE, VEC, WIDTH), f32),
            pltpu.SMEM((SLOTS,), i32),
            pltpu.SMEM((SLOTS,), i32),
            pltpu.VMEM((1, SLOTS), i32),
            pltpu.VMEM((1, SLOTS), i32),
            pltpu.SMEM((1,), i32),
            pltpu.VMEM((WINDOW * SHARE, VEC, WIDTH), f32),
            pltpu.VMEM((WINDOW * SHARE, VEC, WIDTH), f32),
            pltpu.VMEM((KEYS, 2, SHARE, VEC, WIDTH), f32),
            pltpu.VMEM((LINE, SHARE, VEC, WIDTH), f32),
            pltpu.VMEM((2 * PLANE, ROWS, WIDTH), f32),
            pltpu.VMEM((LINE, ROWS, WIDTH), f32),
            pltpu.VMEM((SLOTS * VEC, WIDTH), f32),
            pltpu.VMEM((SLOTS * VEC, WIDTH), f32),
            pltpu.VMEM((2, PAD * VEC, WIDTH), f32),
            pltpu.VMEM((2, GROUP, ROWS, WIDTH), f32),
            pltpu.VMEM((KEYS, 2, ROWS, WIDTH), f32),
            pltpu.VMEM((2 * KEYS + LINE, ROWS, WIDTH), f32),
            pltpu.VMEM((VEC, WIDTH), f32),
            pltpu.VMEM((2, 1, WIDTH), f32),
            pltpu.VMEM((LINE, 1, WIDTH), f32),
            pltpu.VMEM((PLANE, 1, WIDTH), f32),
            dma((7,)),
            dma,
            dma((KEYS, 2)),
            dma,
            dma,
            dma((LINE,)),
            dma,
            dma((2,)),
            dma,
            dma((2, GROUP)),
            dma,
            dma,
            dma((2 * PLANE,)),
            dma,
            dma((2 * KEYS + LINE,)),
            dma((2,)),
            dma((2,)),
        ],
        compiler_params=pltpu.CompilerParams(
            collective_id=0, has_side_effects=True, vmem_limit_bytes=60 * 1024 * 1024
        ),
    )(
        tiles, tile_rows, tile_cols, tile_rows.reshape(1, SLOTS), tile_cols.reshape(1, SLOTS),
        counts, block_vectors,
    )
    return image, grams[:, :VEC], grams[:, VEC:2 * VEC]


def solution(mesh):
    placed = (P("tri", None, None), P("tri"), P("tri"), P("tri"), P("tri", None, None))
    return jax.shard_map(
        per_device,
        mesh=mesh,
        in_specs=placed,
        out_specs=(P("tri", None, None), P(), P()),
        check_vma=False,
    )
```

```python
import jax
import jax.numpy as jnp
from jax import lax
from jax.experimental import pallas as pl
from jax.experimental.pallas import tpu as pltpu
from jax.sharding import PartitionSpec as P

MESH = pl.DeviceIdType.MESH
SEGS = 22
TILES = 1024
SHARE = 4
VEC = 8
WIDTH = 128
ROWS = SHARE * VEC
SLOTS = 32
WINDOW = 13
PAD = 64
BLOCKS = SEGS * (SEGS + 1) // 2
DEVICES = 256
LOW_SCALE, LOW_SHIFT = 2979, 6
GROUP = 8
LINE = 8
PLANE = 32
ROWS_AT = (4, 2, 2, 2)
KEYS = 4
NT_DIMS = (((1,), (1,)), ((), ()))
NN_DIMS = (((1,), (0,)), ((), ()))


def seg_low(s):
    return (s * LOW_SCALE) >> LOW_SHIFT


def seg_of(t):
    return ((t + 1) * SEGS - 1) >> 10


def first_share(s):
    return seg_low(s) >> 2


def shares(s):
    return ((seg_low(s + 1) - 1) >> 2) - first_share(s) + 1


def tri(s):
    return (s * (s + 1)) >> 1


def row_of(d, low=0, high=DEVICES):
    marks = [m * (m + 1) // 2 for m in range(1, SEGS)]
    row = sum(m <= low for m in marks)
    for m in marks:
        if low < m < high:
            row = row + (d >= m).astype(jnp.int32)
    return row


def first_group(s):
    return tri(s) >> 3


def groups_of(s):
    return ((tri(s) + s - 1) >> 3) - first_group(s) + 1


def split(a):
    hi = a.astype(jnp.bfloat16)
    lo = (a - hi.astype(jnp.float32)).astype(jnp.bfloat16)
    return hi, lo


def kernel(
    tiles_ref, rows_hbm, cols_hbm, rows_hbm2, cols_hbm2, count_hbm, x_hbm,
    image_ref, grams_ref,
    tile_buf, hi_buf, lo_buf, x_ref, rows_ref, cols_ref, rows_vec, cols_vec, count_ref,
    x_row, x_col, relay_buf, line_buf, col_buf, col_sum, row_terms, col_terms, contrib, part_buf, part_sum, arrived,
    gram_tile, gram_own, gram_a, gram_b,
    in_sem, relay_send, relay_recv, pass_send, line_send, line_recv, spread_send, gather_recv,
    part_send, part_recv, sum_send, col_send, col_recv, back_send, arrive_recv, gram_send, gram_recv,
):
    me = lax.axis_index("tri")
    residue = me & 7
    group = me >> 3
    base = group * GROUP
    works = me < BLOCKS
    row = row_of(me)
    col = jnp.minimum(me - tri(row), row)
    off_diagonal = jnp.logical_and(works, row > col)
    on_diagonal = jnp.logical_and(works, row == col)
    top = row_of(base)
    rows_here = row_of(jnp.minimum(base + GROUP - 1, BLOCKS - 1)) - top + 1
    seg_a = seg_of(SHARE * me)
    seg_b = seg_of(SHARE * me + SHARE - 1)
    two = seg_b > seg_a

    loads = [
        pltpu.make_async_copy(src, dst, in_sem.at[n])
        for n, (src, dst) in enumerate((
            (x_hbm, x_ref), (tiles_ref, tile_buf), (rows_hbm, rows_ref), (cols_hbm, cols_ref),
            (rows_hbm2, rows_vec), (cols_hbm2, cols_vec), (count_hbm, count_ref),
        ))
    ]
    def loop(n, body):
        def step(i, _):
            body(i)
            return 0

        lax.fori_loop(0, n, step, 0)

    def owned(body):
        body(seg_a, 0)

        @pl.when(two)
        def _():
            body(seg_b, 1)

    def span(s):
        low = jnp.maximum(tri(s), base)
        return low, jnp.minimum(tri(s) + s, base + GROUP) - low

    def relayed(body):
        def each(n):
            s = top + n
            start = (residue - first_share(s)) & 7
            for turn in range(2):
                p = start + GROUP * turn

                @pl.when(jnp.logical_and(p < shares(s), span(s)[1] > 0))
                def _():
                    body(s, p, s & 3, turn)

        loop(rows_here, each)

    def members(s, body):
        low, count = span(s)
        loop(count, lambda i: body(low + i))

    def send(src, dst, send_sem, recv_sem, dev):
        def remote():
            pltpu.make_async_remote_copy(
                src_ref=src, dst_ref=dst, send_sem=send_sem, recv_sem=recv_sem,
                device_id=(dev,), device_id_type=MESH,
            ).start()

        def local():
            pltpu.make_async_copy(src, dst, recv_sem).start()

        lax.cond(dev != me, remote, local)

    def sent(src, send_sem, dev):
        @pl.when(dev != me)
        def _():
            pltpu.make_async_copy(src, src, send_sem).wait()

    def landed(dst, recv_sem):
        pltpu.make_async_copy(dst, dst, recv_sem).wait()

    def all_landed(held, n, limit, recv_sem):
        def narrow(low, high):
            if high - low > 1:
                mid = (low + high) // 2
                lax.cond(n < mid, lambda: narrow(low, mid), lambda: narrow(mid, high))
            elif low:
                landed(held.at[pl.ds(0, low)], recv_sem)

        narrow(0, limit + 1)

    barrier = pltpu.get_barrier_semaphore()

    def greet(dev):
        @pl.when(dev != me)
        def _():
            pl.semaphore_signal(barrier, inc=1, device_id=(dev,), device_id_type=MESH)

    z, y = group & 7, me >> 6

    def rank_of(dev):
        return ((dev >> 6) << 3) + (dev & 7)

    def line(zz):
        return (y * LINE + zz) * GROUP + residue

    def plane(q):
        return ((q >> 3) * LINE + z) * GROUP + (q & 7)

    relayed(lambda s, p, key, turn: greet(first_share(s) + p))
    for dz in (4, 3, 5, 2, 6, 1, 7):
        pl.semaphore_signal(barrier, inc=1, device_id=(line((z + dz) & 7),), device_id_type=MESH)
    def hops(m):
        return [0, 1, 2, 1][m >> 3] + [0, 1, 2, 1][(m >> 1) & 3]

    far_first = sorted(range(1, PLANE), key=hops, reverse=True)
    for m in far_first:
        pl.semaphore_signal(
            barrier, inc=1, device_id=(plane(rank_of(me) ^ m),), device_id_type=MESH
        )
    def greeters(s):
        mine = jnp.logical_and(group >= first_group(s), group < first_group(s) + groups_of(s))
        return groups_of(s) - jnp.where(mine, 1, 0)

    pl.semaphore_wait(barrier, LINE + PLANE - 2 + greeters(seg_a) + jnp.where(two, greeters(seg_b), 0))

    def near_first(n):
        return (z + jnp.where((n & 1) == 1, (n + 1) >> 1, LINE - (n >> 1))) & 7

    def at_my_z(s, k, first, low):
        return jnp.logical_and(((first + s - low) >> 3) == 0, s <= k)

    def owned_by(zz):
        owner = line(zz)
        a = seg_of(SHARE * owner)
        return owner, a, seg_of(SHARE * owner + SHARE - 1) - a + 1

    def targets(zz, body):
        owner, a, count = owned_by(zz)

        def one(w):
            s = a + w
            p = owner - first_share(s)
            for k, first, low in here:
                @pl.when(at_my_z(s, k, first, low))
                def _(first=first):
                    body(first + s, s, p)

        loop(count, one)

    def count_targets(zz, total):
        _owner, a, count = owned_by(zz)

        def one(w, total):
            for k, first, low in here:
                total = total + at_my_z(a + w, k, first, low).astype(jnp.int32)
            return total

        return lax.fori_loop(0, count, one, total)

    def to_line(n):
        zz = near_first(LINE - 1 - n)
        send(x_hbm, line_buf.at[z], line_send, line_recv.at[z], line(zz))

    def spread(start):
        def each(n):
            zz = near_first(n)
            src = line_buf.at[zz]
            if start:
                landed(src, line_recv.at[zz])

            def body(dev, s, p):
                if start:
                    dst = x_col.at[pl.ds(p * SHARE, SHARE)]
                    send(src, dst, spread_send, gather_recv.at[1], dev)
                else:
                    sent(src, spread_send, dev)

            targets(zz, body)

        loop(LINE, each)

    def to_relays(start):
        def body(s, w):
            turn = (me - first_share(s)) >> 3
            dst, sem = relay_buf.at[s & 3, turn], relay_recv.at[s & 3, turn]

            def each(n):
                dev = (first_group(s) + n) * GROUP + residue
                if start:
                    send(x_hbm, dst, relay_send, sem, dev)
                else:
                    sent(x_hbm, relay_send, dev)

            loop(groups_of(s), each)

        return body

    loop(LINE, to_line)
    owned(to_relays(True))

    for load in loads:
        load.start()

    here = []
    for yy in (2, 1, 3, 0):
        low = yy * 64 + z * GROUP
        first_row = row_of(low, yy * 64, yy * 64 + 64)
        for k in [first_row + i for i in range(ROWS_AT[yy])]:
            here.append((k, jnp.where(k < SEGS, tri(k), 2 * DEVICES), low))

    for load in loads:
        load.wait()

    def split_tile(k):
        hi, lo = split(tile_buf[k])
        hi_buf[k] = hi
        lo_buf[k] = lo

    loop(SLOTS, split_tile)

    def pass_on(start):
        def body(s, p, key, turn):
            src = relay_buf.at[key, turn]
            dst = x_row.at[pl.ds(p * SHARE, SHARE)]
            if start:
                landed(src, relay_recv.at[key, turn])

            def each(dev):
                if start:
                    send(src, dst, pass_send, gather_recv.at[0], dev)
                else:
                    sent(src, pass_send, dev)

            members(s, each)

        return body

    spread(True)
    relayed(pass_on(True))

    def wait_rows(s, held, recv_sem):
        for n in (WINDOW - 1, WINDOW):
            @pl.when(shares(s) == n)
            def _():
                landed(held.at[pl.ds(0, n * SHARE)], recv_sem)

    row_base = SHARE * first_share(row)
    col_base = SHARE * first_share(col)

    def multiply(held, ids, origin, terms, axis, dims):
        def one(k):
            hi, lo = split(held[jnp.clip(ids[k] - origin, 0, WINDOW * SHARE - 1)])
            both = jnp.concatenate([hi, lo], axis=0)
            out = lax.dot_general(
                jnp.concatenate([both, both], axis=1),
                jnp.concatenate([hi_buf[k], lo_buf[k]], axis=axis), dims,
                preferred_element_type=jnp.float32,
            )
            terms[pl.ds(pl.multiple_of(k * VEC, VEC), VEC), :] = out[:VEC] + out[VEC:]

        def several(n):
            for u in range(8):
                one(8 * n + u)

        loop(SLOTS // 8, several)

    def reduce(vec, origin, terms, which):
        live = lax.broadcasted_iota(jnp.int32, (PAD, SLOTS), 1) < count_ref[0]
        place = lax.broadcasted_iota(jnp.int32, (PAD, SLOTS), 0)
        hit = jnp.logical_and(place == vec[...] - origin, live)
        hot = hit.astype(jnp.float32).astype(jnp.bfloat16)
        hot = jnp.concatenate([hot, hot], axis=1)
        for v in range(VEC):
            hi, lo = split(terms[pl.ds(v, SLOTS, stride=VEC), :])
            contrib[which, pl.ds(v, PAD, stride=VEC), :] = lax.dot_general(
                hot, jnp.concatenate([hi, lo], axis=0), NN_DIMS,
                preferred_element_type=jnp.float32,
            )

    def chunk(which, p):
        return contrib.at[which, pl.ds(pl.multiple_of(p * ROWS, ROWS), ROWS), :]

    def row_parts(p):
        turn = p >> 3
        send(
            chunk(0, p), part_buf.at[turn * GROUP + residue], part_send, part_recv,
            base + ((first_share(row) + p) & 7),
        )

    def all_sent(which, s, same_y, sem):
        n = shares(s)
        for turn in range(2):
            p = ((residue - first_share(s)) & 7) + GROUP * turn
            mine = p < shares(s)
            if same_y:
                mine = jnp.logical_and(mine, ((first_share(s) + p) >> 6) == y)
            n = n - mine.astype(jnp.int32)
        for count in range(WINDOW - 3, WINDOW + 1):
            @pl.when(n == count)
            def _():
                landed(contrib.at[which, pl.ds(0, count * ROWS), :], sem)

    def place_of(owner, s):
        return jnp.where(seg_of(SHARE * owner) == s, 0, 1)

    def col_parts(p):
        owner = first_share(col) + p
        at = rank_of(me) * 2 + (p >> 3)
        dev = (((owner >> 6) << 3) + z) * GROUP + (owner & 7)
        send(chunk(1, p), col_buf.at[at], col_send, col_recv, dev)

    @pl.when(works)
    def _():
        wait_rows(col, x_col, gather_recv.at[1])
        multiply(x_col, cols_ref, col_base, row_terms, 1, NT_DIMS)
        reduce(rows_vec, row_base, row_terms, 0)

        @pl.when(off_diagonal)
        def _():
            loop(shares(row), row_parts)
            wait_rows(row, x_row, gather_recv.at[0])
            multiply(x_row, rows_ref, row_base, col_terms, 0, NN_DIMS)

        @pl.when(on_diagonal)
        def _():
            multiply(x_col, rows_ref, row_base, col_terms, 0, NN_DIMS)

        reduce(cols_vec, col_base, col_terms, 1)

        @pl.when(on_diagonal)
        def _():
            contrib[1] = contrib[0] + contrib[1]

        loop(shares(col), col_parts)

    landed(line_buf.at[pl.ds(0, LINE - 1)], line_send)
    owned(to_relays(False))
    spread(False)
    relayed(pass_on(False))

    def add_parts(start):
        def body(s, p, key, turn):
            owner = first_share(s) + p
            src = part_sum.at[key, turn]
            if start:
                low, count = span(s)

                def each(i, total):
                    rank = (low + i) & 7
                    return total + part_buf[turn * GROUP + rank]

                part_sum[key, turn] = lax.fori_loop(
                    0, count, each, jnp.zeros((ROWS, WIDTH), jnp.float32)
                )
                at = place_of(owner, s) * KEYS + group - first_group(s)
                send(src, arrived.at[at], sum_send, arrive_recv, owner)
            else:
                sent(src, sum_send, owner)

        return body

    def add_cols(n):
        zz = near_first(LINE - 1 - n)
        col_sum[zz] = jnp.zeros((ROWS, WIDTH), jnp.float32)

        def body(dev, s, p):
            at = rank_of(dev) * 2 + (p >> 3)
            col_sum[zz] = col_sum[zz] + col_buf[at]

        targets(zz, body)
        at = 2 * KEYS + z
        send(col_sum.at[zz], arrived.at[at], back_send, arrive_recv, line(zz))

    def parts_of(n, total):
        s = top + n
        start = (residue - first_share(s)) & 7
        turns = (start < shares(s)).astype(jnp.int32) + (start + GROUP < shares(s)).astype(jnp.int32)
        return total + turns * jnp.maximum(span(s)[1], 0)

    n_parts = lax.fori_loop(0, rows_here, parts_of, 0)
    n_cols = lax.fori_loop(0, LINE, count_targets, 0)
    all_landed(part_buf, n_parts, 2 * GROUP, part_recv)
    relayed(add_parts(True))
    all_landed(col_buf, n_cols, 2 * PLANE, col_recv)
    loop(LINE, add_cols)

    def each(at, total):
        return total + arrived[at]

    def collect(w, s, total):
        return lax.fori_loop(w * KEYS, w * KEYS + groups_of(s), each, total)

    n_arrived = LINE + groups_of(seg_a) + jnp.where(two, groups_of(seg_b), 0)
    all_landed(arrived, n_arrived, 2 * KEYS + LINE, arrive_recv)

    def put(total):
        for t in range(SHARE):
            image_ref[t] = total[t * VEC:(t + 1) * VEC]

    total = collect(0, seg_a, jnp.zeros((ROWS, WIDTH), jnp.float32))
    put(lax.fori_loop(2 * KEYS, 2 * KEYS + LINE, each, total))

    @pl.when(two)
    def _():
        put(collect(1, seg_b, jnp.concatenate([image_ref[t] for t in range(SHARE)], axis=0)))

    def flat(ref):
        return jnp.concatenate([ref[t] for t in range(SHARE)], axis=1)

    image = flat(image_ref)
    both = lax.dot_general(
        jnp.concatenate([flat(x_ref), image], axis=0), image, NT_DIMS,
        precision=lax.Precision.HIGHEST, preferred_element_type=jnp.float32,
    )
    gram_tile[...] = jnp.zeros((VEC, WIDTH), jnp.float32)
    gram_tile[:, 0:VEC] = both[:VEC]
    gram_tile[:, VEC:2 * VEC] = both[VEC:]
    moved = pltpu.roll(gram_tile[...], 0, 1, stride=2 * VEC, stride_axis=0)
    gram_own[0] = jnp.sum(moved, axis=0, keepdims=True)

    rank = rank_of(me)
    circles = (
        (gram_a, z, LINE, [line((z + dz) & 7) for dz in (4, 3, 5, 2, 6, 1, 7)]),
        (gram_b, rank, PLANE, [plane(rank ^ m) for m in far_first]),
    )
    for n, (buf, rank, size, partners) in enumerate(circles):
        for dev in partners:
            pltpu.make_async_remote_copy(
                src_ref=gram_own.at[n], dst_ref=buf.at[rank], send_sem=gram_send.at[n],
                recv_sem=gram_recv.at[n], device_id=(dev,), device_id_type=MESH,
            ).start()

        buf[rank] = gram_own[n]
        if n == 0:
            relayed(add_parts(False))

            @pl.when(off_diagonal)
            def _():
                all_sent(0, row, False, part_send)

            @pl.when(works)
            def _():
                all_sent(1, col, True, col_send)

            landed(col_sum.at[pl.ds(0, LINE - 1)], back_send)

        landed(buf.at[pl.ds(0, size - 1)], gram_recv.at[n])
        terms = [buf[q] for q in range(size)]
        while len(terms) > 1:
            terms = [a + b for a, b in zip(terms[::2], terms[1::2])]
        if n == 0:
            gram_own[1] = terms[0]
        else:
            out = jnp.broadcast_to(terms[0] * (1.0 / (TILES * WIDTH)), (VEC, WIDTH))
            block = lax.broadcasted_iota(jnp.int32, (VEC, WIDTH), 1) >> 4
            out = jnp.where(block == lax.broadcasted_iota(jnp.int32, (VEC, WIDTH), 0), out, 0.0)
            for shift in (64, 32, 16):
                out = out + pltpu.roll(out, shift, 1)
            grams_ref[...] = out

    for n, (buf, _rank, size, _partners) in enumerate(circles):
        landed(buf.at[pl.ds(0, size - 1)], gram_send.at[n])


def per_device(tiles, tile_rows, tile_cols, counts, block_vectors):
    f32, i32 = jnp.float32, jnp.int32
    vmem = pl.BlockSpec(memory_space=pltpu.VMEM)
    dma = pltpu.SemaphoreType.DMA
    image, grams = pl.pallas_call(
        kernel,
        out_shape=(
            pltpu.VMEM((SHARE, VEC, WIDTH), f32),
            pltpu.VMEM((VEC, WIDTH), f32),
        ),
        in_specs=[pl.BlockSpec(memory_space=pl.ANY)] * 7,
        out_specs=(vmem, vmem),
        scratch_shapes=[
            pltpu.VMEM((SLOTS, WIDTH, WIDTH), f32),
            pltpu.VMEM((SLOTS, WIDTH, WIDTH), jnp.bfloat16),
            pltpu.VMEM((SLOTS, WIDTH, WIDTH), jnp.bfloat16),
            pltpu.VMEM((SHARE, VEC, WIDTH), f32),
            pltpu.SMEM((SLOTS,), i32),
            pltpu.SMEM((SLOTS,), i32),
            pltpu.VMEM((1, SLOTS), i32),
            pltpu.VMEM((1, SLOTS), i32),
            pltpu.SMEM((1,), i32),
            pltpu.VMEM((WINDOW * SHARE, VEC, WIDTH), f32),
            pltpu.VMEM((WINDOW * SHARE, VEC, WIDTH), f32),
            pltpu.VMEM((KEYS, 2, SHARE, VEC, WIDTH), f32),
            pltpu.VMEM((LINE, SHARE, VEC, WIDTH), f32),
            pltpu.VMEM((2 * PLANE, ROWS, WIDTH), f32),
            pltpu.VMEM((LINE, ROWS, WIDTH), f32),
            pltpu.VMEM((SLOTS * VEC, WIDTH), f32),
            pltpu.VMEM((SLOTS * VEC, WIDTH), f32),
            pltpu.VMEM((2, PAD * VEC, WIDTH), f32),
            pltpu.VMEM((2 * GROUP, ROWS, WIDTH), f32),
            pltpu.VMEM((KEYS, 2, ROWS, WIDTH), f32),
            pltpu.VMEM((2 * KEYS + LINE, ROWS, WIDTH), f32),
            pltpu.VMEM((VEC, WIDTH), f32),
            pltpu.VMEM((2, 1, WIDTH), f32),
            pltpu.VMEM((LINE, 1, WIDTH), f32),
            pltpu.VMEM((PLANE, 1, WIDTH), f32),
            dma((7,)),
            dma,
            dma((KEYS, 2)),
            dma,
            dma,
            dma((LINE,)),
            dma,
            dma((2,)),
            dma,
            dma,
            dma,
            dma,
            dma,
            dma,
            dma,
            dma((2,)),
            dma((2,)),
        ],
        compiler_params=pltpu.CompilerParams(
            collective_id=0, has_side_effects=True, vmem_limit_bytes=60 * 1024 * 1024
        ),
    )(
        tiles, tile_rows, tile_cols, tile_rows.reshape(1, SLOTS), tile_cols.reshape(1, SLOTS),
        counts, block_vectors,
    )
    return image, grams[:, :VEC], grams[:, VEC:2 * VEC]


def solution(mesh):
    placed = (P("tri", None, None), P("tri"), P("tri"), P("tri"), P("tri", None, None))
    return jax.shard_map(
        per_device,
        mesh=mesh,
        in_specs=placed,
        out_specs=(P("tri", None, None), P(), P()),
        check_vma=False,
    )
```

```python
import jax
import jax.numpy as jnp
from jax import lax
from jax.experimental import pallas as pl
from jax.experimental.pallas import tpu as pltpu
from jax.sharding import PartitionSpec as P

MESH = pl.DeviceIdType.MESH
SEGS = 22
TILES = 1024
SHARE = 4
VEC = 8
WIDTH = 128
ROWS = SHARE * VEC
SLOTS = 32
WINDOW = 13
PAD = 64
BLOCKS = SEGS * (SEGS + 1) // 2
DEVICES = 256
LOW_SCALE, LOW_SHIFT = 2979, 6
GROUP = 8
LINE = 8
PLANE = 32
ROWS_AT = (4, 2, 2, 2)
KEYS = 4
NT_DIMS = (((1,), (1,)), ((), ()))
NN_DIMS = (((1,), (0,)), ((), ()))


def seg_low(s):
    return (s * LOW_SCALE) >> LOW_SHIFT


def seg_of(t):
    return ((t + 1) * SEGS - 1) >> 10


def first_share(s):
    return seg_low(s) >> 2


def shares(s):
    return ((seg_low(s + 1) - 1) >> 2) - first_share(s) + 1


def tri(s):
    return (s * (s + 1)) >> 1


def row_of(d, low=0, high=DEVICES):
    marks = [m * (m + 1) // 2 for m in range(1, SEGS)]
    row = sum(m <= low for m in marks)
    for m in marks:
        if low < m < high:
            row = row + (d >= m).astype(jnp.int32)
    return row


def first_group(s):
    return tri(s) >> 3


def groups_of(s):
    return ((tri(s) + s - 1) >> 3) - first_group(s) + 1


def split(a):
    hi = a.astype(jnp.bfloat16)
    lo = (a - hi.astype(jnp.float32)).astype(jnp.bfloat16)
    return hi, lo


def kernel(
    tiles_ref, rows_hbm, cols_hbm, rows_hbm2, cols_hbm2, count_hbm, x_hbm,
    image_ref, grams_ref,
    tile_buf, hi_buf, lo_buf, x_ref, rows_ref, cols_ref, rows_vec, cols_vec, count_ref,
    x_row, x_col, relay_buf, line_buf, col_buf, col_sum, row_terms, col_terms, contrib, part_buf, part_sum, arrived,
    gram_tile, gram_own, gram_a, gram_b,
    in_sem, relay_send, relay_recv, pass_send, line_send, line_recv, spread_send, gather_recv,
    part_send, part_recv, sum_send, col_send, col_recv, back_send, arrive_recv, gram_send, gram_recv,
):
    me = lax.axis_index("tri")
    residue = me & 7
    group = me >> 3
    base = group * GROUP
    works = me < BLOCKS
    row = row_of(me)
    col = jnp.minimum(me - tri(row), row)
    off_diagonal = jnp.logical_and(works, row > col)
    on_diagonal = jnp.logical_and(works, row == col)
    top = row_of(base)
    rows_here = row_of(jnp.minimum(base + GROUP - 1, BLOCKS - 1)) - top + 1
    seg_a = seg_of(SHARE * me)
    seg_b = seg_of(SHARE * me + SHARE - 1)
    two = seg_b > seg_a

    loads = [
        pltpu.make_async_copy(src, dst, in_sem.at[n])
        for n, (src, dst) in enumerate((
            (x_hbm, x_ref), (tiles_ref, tile_buf), (rows_hbm, rows_ref), (cols_hbm, cols_ref),
            (rows_hbm2, rows_vec), (cols_hbm2, cols_vec), (count_hbm, count_ref),
        ))
    ]
    def loop(n, body):
        def step(i, _):
            body(i)
            return 0

        lax.fori_loop(0, n, step, 0)

    def owned(body):
        body(seg_a, 0)

        @pl.when(two)
        def _():
            body(seg_b, 1)

    def span(s):
        low = jnp.maximum(tri(s), base)
        return low, jnp.minimum(tri(s) + s, base + GROUP) - low

    def relayed(body):
        def each(n):
            s = top + n
            start = (residue - first_share(s)) & 7
            for turn in range(2):
                p = start + GROUP * turn

                @pl.when(jnp.logical_and(p < shares(s), span(s)[1] > 0))
                def _():
                    body(s, p, s & 3, turn)

        loop(rows_here, each)

    def members(s, body):
        low, count = span(s)
        loop(count, lambda i: body(low + i))

    def send(src, dst, send_sem, recv_sem, dev):
        def remote():
            pltpu.make_async_remote_copy(
                src_ref=src, dst_ref=dst, send_sem=send_sem, recv_sem=recv_sem,
                device_id=(dev,), device_id_type=MESH,
            ).start()

        def local():
            pltpu.make_async_copy(src, dst, recv_sem).start()

        lax.cond(dev != me, remote, local)

    def sent(src, send_sem, dev):
        @pl.when(dev != me)
        def _():
            pltpu.make_async_copy(src, src, send_sem).wait()

    def landed(dst, recv_sem):
        pltpu.make_async_copy(dst, dst, recv_sem).wait()

    def all_landed(held, n, limit, recv_sem):
        def narrow(low, high):
            if high - low > 1:
                mid = (low + high) // 2
                lax.cond(n < mid, lambda: narrow(low, mid), lambda: narrow(mid, high))
            elif low:
                landed(held.at[pl.ds(0, low)], recv_sem)

        narrow(0, limit + 1)

    barrier = pltpu.get_barrier_semaphore()

    def greet(dev):
        @pl.when(dev != me)
        def _():
            pl.semaphore_signal(barrier, inc=1, device_id=(dev,), device_id_type=MESH)

    z, y = group & 7, me >> 6

    def rank_of(dev):
        return ((dev >> 6) << 3) + (dev & 7)

    def line(zz):
        return (y * LINE + zz) * GROUP + residue

    def plane(q):
        return ((q >> 3) * LINE + z) * GROUP + (q & 7)

    relayed(lambda s, p, key, turn: greet(first_share(s) + p))
    for dz in (4, 3, 5, 2, 6, 1, 7):
        pl.semaphore_signal(barrier, inc=1, device_id=(line((z + dz) & 7),), device_id_type=MESH)
    def hops(m):
        return [0, 1, 2, 1][m >> 3] + [0, 1, 2, 1][(m >> 1) & 3]

    far_first = sorted(range(1, PLANE), key=hops, reverse=True)
    for m in far_first:
        pl.semaphore_signal(
            barrier, inc=1, device_id=(plane(rank_of(me) ^ m),), device_id_type=MESH
        )
    def greeters(s):
        mine = jnp.logical_and(group >= first_group(s), group < first_group(s) + groups_of(s))
        return groups_of(s) - jnp.where(mine, 1, 0)

    pl.semaphore_wait(barrier, LINE + PLANE - 2 + greeters(seg_a) + jnp.where(two, greeters(seg_b), 0))

    def near_first(n):
        return (z + jnp.where((n & 1) == 1, (n + 1) >> 1, LINE - (n >> 1))) & 7

    def at_my_z(s, k, first, low):
        return jnp.logical_and(((first + s - low) >> 3) == 0, s <= k)

    def owned_by(zz):
        owner = line(zz)
        a = seg_of(SHARE * owner)
        return owner, a, seg_of(SHARE * owner + SHARE - 1) - a + 1

    def targets(zz, body):
        owner, a, count = owned_by(zz)

        def one(w):
            s = a + w
            p = owner - first_share(s)
            for k, first, low in here:
                @pl.when(at_my_z(s, k, first, low))
                def _(first=first):
                    body(first + s, s, p)

        loop(count, one)

    def count_targets(zz, total):
        _owner, a, count = owned_by(zz)

        def one(w, total):
            for k, first, low in here:
                total = total + at_my_z(a + w, k, first, low).astype(jnp.int32)
            return total

        return lax.fori_loop(0, count, one, total)

    def to_line(n):
        zz = near_first(n)
        send(x_hbm, line_buf.at[z], line_send, line_recv.at[z], line(zz))

    def spread(start):
        def each(n):
            zz = near_first(n)
            src = line_buf.at[zz]
            if start:
                landed(src, line_recv.at[zz])

            def body(dev, s, p):
                if start:
                    dst = x_col.at[pl.ds(p * SHARE, SHARE)]
                    send(src, dst, spread_send, gather_recv.at[1], dev)
                else:
                    sent(src, spread_send, dev)

            targets(zz, body)

        loop(LINE, each)

    def to_relays(start):
        def body(s, w):
            turn = (me - first_share(s)) >> 3
            dst, sem = relay_buf.at[s & 3, turn], relay_recv.at[s & 3, turn]

            def each(n):
                dev = (first_group(s) + n) * GROUP + residue
                if start:
                    send(x_hbm, dst, relay_send, sem, dev)
                else:
                    sent(x_hbm, relay_send, dev)

            loop(groups_of(s), each)

        return body

    loop(LINE, to_line)
    owned(to_relays(True))

    for load in loads:
        load.start()

    here = []
    for yy in (2, 1, 3, 0):
        low = yy * 64 + z * GROUP
        first_row = row_of(low, yy * 64, yy * 64 + 64)
        for k in [first_row + i for i in range(ROWS_AT[yy])]:
            here.append((k, jnp.where(k < SEGS, tri(k), 2 * DEVICES), low))

    for load in loads:
        load.wait()

    def split_tile(k):
        hi, lo = split(tile_buf[k])
        hi_buf[k] = hi
        lo_buf[k] = lo

    loop(SLOTS, split_tile)

    def pass_on(start):
        def body(s, p, key, turn):
            src = relay_buf.at[key, turn]
            dst = x_row.at[pl.ds(p * SHARE, SHARE)]
            if start:
                landed(src, relay_recv.at[key, turn])

            def each(dev):
                if start:
                    send(src, dst, pass_send, gather_recv.at[0], dev)
                else:
                    sent(src, pass_send, dev)

            members(s, each)

        return body

    spread(True)
    relayed(pass_on(True))

    def wait_rows(s, held, recv_sem):
        for n in (WINDOW - 1, WINDOW):
            @pl.when(shares(s) == n)
            def _():
                landed(held.at[pl.ds(0, n * SHARE)], recv_sem)

    row_base = SHARE * first_share(row)
    col_base = SHARE * first_share(col)

    def multiply(held, ids, origin, terms, axis, dims):
        def one(k):
            hi, lo = split(held[jnp.clip(ids[k] - origin, 0, WINDOW * SHARE - 1)])
            both = jnp.concatenate([hi, lo], axis=0)
            out = lax.dot_general(
                jnp.concatenate([both, both], axis=1),
                jnp.concatenate([hi_buf[k], lo_buf[k]], axis=axis), dims,
                preferred_element_type=jnp.float32,
            )
            terms[pl.ds(pl.multiple_of(k * VEC, VEC), VEC), :] = out[:VEC] + out[VEC:]

        def several(n):
            for u in range(8):
                one(8 * n + u)

        loop(SLOTS // 8, several)

    def reduce(vec, origin, terms, which):
        live = lax.broadcasted_iota(jnp.int32, (PAD, SLOTS), 1) < count_ref[0]
        place = lax.broadcasted_iota(jnp.int32, (PAD, SLOTS), 0)
        hit = jnp.logical_and(place == vec[...] - origin, live)
        hot = hit.astype(jnp.float32).astype(jnp.bfloat16)
        hot = jnp.concatenate([hot, hot], axis=1)
        for v in range(VEC):
            hi, lo = split(terms[pl.ds(v, SLOTS, stride=VEC), :])
            contrib[which, pl.ds(v, PAD, stride=VEC), :] = lax.dot_general(
                hot, jnp.concatenate([hi, lo], axis=0), NN_DIMS,
                preferred_element_type=jnp.float32,
            )

    def chunk(which, p):
        return contrib.at[which, pl.ds(pl.multiple_of(p * ROWS, ROWS), ROWS), :]

    def row_parts(p):
        turn = p >> 3
        send(
            chunk(0, p), part_buf.at[turn * GROUP + residue], part_send, part_recv,
            base + ((first_share(row) + p) & 7),
        )

    def all_sent(which, s, same_y, sem):
        n = shares(s)
        for turn in range(2):
            p = ((residue - first_share(s)) & 7) + GROUP * turn
            mine = p < shares(s)
            if same_y:
                mine = jnp.logical_and(mine, ((first_share(s) + p) >> 6) == y)
            n = n - mine.astype(jnp.int32)
        for count in range(WINDOW - 3, WINDOW + 1):
            @pl.when(n == count)
            def _():
                landed(contrib.at[which, pl.ds(0, count * ROWS), :], sem)

    def place_of(owner, s):
        return jnp.where(seg_of(SHARE * owner) == s, 0, 1)

    def col_parts(p):
        owner = first_share(col) + p
        at = rank_of(me) * 2 + (p >> 3)
        dev = (((owner >> 6) << 3) + z) * GROUP + (owner & 7)
        send(chunk(1, p), col_buf.at[at], col_send, col_recv, dev)

    @pl.when(works)
    def _():
        wait_rows(col, x_col, gather_recv.at[1])
        multiply(x_col, cols_ref, col_base, row_terms, 1, NT_DIMS)
        reduce(rows_vec, row_base, row_terms, 0)

        @pl.when(off_diagonal)
        def _():
            loop(shares(row), row_parts)
            wait_rows(row, x_row, gather_recv.at[0])
            multiply(x_row, rows_ref, row_base, col_terms, 0, NN_DIMS)

        @pl.when(on_diagonal)
        def _():
            multiply(x_col, rows_ref, row_base, col_terms, 0, NN_DIMS)

        reduce(cols_vec, col_base, col_terms, 1)

        @pl.when(on_diagonal)
        def _():
            contrib[1] = contrib[0] + contrib[1]

        loop(shares(col), col_parts)

    landed(line_buf.at[pl.ds(0, LINE - 1)], line_send)
    owned(to_relays(False))
    spread(False)
    relayed(pass_on(False))

    def add_parts(start):
        def body(s, p, key, turn):
            owner = first_share(s) + p
            src = part_sum.at[key, turn]
            if start:
                low, count = span(s)

                def each(i, total):
                    rank = (low + i) & 7
                    return total + part_buf[turn * GROUP + rank]

                part_sum[key, turn] = lax.fori_loop(
                    0, count, each, jnp.zeros((ROWS, WIDTH), jnp.float32)
                )
                at = place_of(owner, s) * KEYS + group - first_group(s)
                send(src, arrived.at[at], sum_send, arrive_recv, owner)
            else:
                sent(src, sum_send, owner)

        return body

    def add_cols(n):
        zz = near_first(LINE - 1 - n)
        col_sum[zz] = jnp.zeros((ROWS, WIDTH), jnp.float32)

        def body(dev, s, p):
            at = rank_of(dev) * 2 + (p >> 3)
            col_sum[zz] = col_sum[zz] + col_buf[at]

        targets(zz, body)
        at = 2 * KEYS + z
        send(col_sum.at[zz], arrived.at[at], back_send, arrive_recv, line(zz))

    def parts_of(n, total):
        s = top + n
        start = (residue - first_share(s)) & 7
        turns = (start < shares(s)).astype(jnp.int32) + (start + GROUP < shares(s)).astype(jnp.int32)
        return total + turns * jnp.maximum(span(s)[1], 0)

    n_parts = lax.fori_loop(0, rows_here, parts_of, 0)
    n_cols = lax.fori_loop(0, LINE, count_targets, 0)
    all_landed(part_buf, n_parts, 2 * GROUP, part_recv)
    relayed(add_parts(True))
    all_landed(col_buf, n_cols, 2 * PLANE, col_recv)
    loop(LINE, add_cols)

    def each(at, total):
        return total + arrived[at]

    def collect(w, s, total):
        return lax.fori_loop(w * KEYS, w * KEYS + groups_of(s), each, total)

    n_arrived = LINE + groups_of(seg_a) + jnp.where(two, groups_of(seg_b), 0)
    all_landed(arrived, n_arrived, 2 * KEYS + LINE, arrive_recv)

    def put(total):
        for t in range(SHARE):
            image_ref[t] = total[t * VEC:(t + 1) * VEC]

    total = collect(0, seg_a, jnp.zeros((ROWS, WIDTH), jnp.float32))
    put(lax.fori_loop(2 * KEYS, 2 * KEYS + LINE, each, total))

    @pl.when(two)
    def _():
        put(collect(1, seg_b, jnp.concatenate([image_ref[t] for t in range(SHARE)], axis=0)))

    def flat(ref):
        return jnp.concatenate([ref[t] for t in range(SHARE)], axis=1)

    image = flat(image_ref)
    both = lax.dot_general(
        jnp.concatenate([flat(x_ref), image], axis=0), image, NT_DIMS,
        precision=lax.Precision.HIGHEST, preferred_element_type=jnp.float32,
    )
    gram_tile[...] = jnp.zeros((VEC, WIDTH), jnp.float32)
    gram_tile[:, 0:VEC] = both[:VEC]
    gram_tile[:, VEC:2 * VEC] = both[VEC:]
    moved = pltpu.roll(gram_tile[...], 0, 1, stride=2 * VEC, stride_axis=0)
    gram_own[0] = jnp.sum(moved, axis=0, keepdims=True)

    rank = rank_of(me)
    circles = (
        (gram_a, z, LINE, [line((z + dz) & 7) for dz in (4, 3, 5, 2, 6, 1, 7)]),
        (gram_b, rank, PLANE, [plane(rank ^ m) for m in far_first]),
    )
    for n, (buf, rank, size, partners) in enumerate(circles):
        for dev in partners:
            pltpu.make_async_remote_copy(
                src_ref=gram_own.at[n], dst_ref=buf.at[rank], send_sem=gram_send.at[n],
                recv_sem=gram_recv.at[n], device_id=(dev,), device_id_type=MESH,
            ).start()

        buf[rank] = gram_own[n]
        if n == 0:
            relayed(add_parts(False))

            @pl.when(off_diagonal)
            def _():
                all_sent(0, row, False, part_send)

            @pl.when(works)
            def _():
                all_sent(1, col, True, col_send)

            landed(col_sum.at[pl.ds(0, LINE - 1)], back_send)

        landed(buf.at[pl.ds(0, size - 1)], gram_recv.at[n])
        terms = [buf[q] for q in range(size)]
        while len(terms) > 1:
            terms = [a + b for a, b in zip(terms[::2], terms[1::2])]
        if n == 0:
            gram_own[1] = terms[0]
        else:
            out = jnp.broadcast_to(terms[0] * (1.0 / (TILES * WIDTH)), (VEC, WIDTH))
            block = lax.broadcasted_iota(jnp.int32, (VEC, WIDTH), 1) >> 4
            out = jnp.where(block == lax.broadcasted_iota(jnp.int32, (VEC, WIDTH), 0), out, 0.0)
            for shift in (64, 32, 16):
                out = out + pltpu.roll(out, shift, 1)
            grams_ref[...] = out

    for n, (buf, _rank, size, _partners) in enumerate(circles):
        landed(buf.at[pl.ds(0, size - 1)], gram_send.at[n])


def per_device(tiles, tile_rows, tile_cols, counts, block_vectors):
    f32, i32 = jnp.float32, jnp.int32
    vmem = pl.BlockSpec(memory_space=pltpu.VMEM)
    dma = pltpu.SemaphoreType.DMA
    image, grams = pl.pallas_call(
        kernel,
        out_shape=(
            pltpu.VMEM((SHARE, VEC, WIDTH), f32),
            pltpu.VMEM((VEC, WIDTH), f32),
        ),
        in_specs=[pl.BlockSpec(memory_space=pl.ANY)] * 7,
        out_specs=(vmem, vmem),
        scratch_shapes=[
            pltpu.VMEM((SLOTS, WIDTH, WIDTH), f32),
            pltpu.VMEM((SLOTS, WIDTH, WIDTH), jnp.bfloat16),
            pltpu.VMEM((SLOTS, WIDTH, WIDTH), jnp.bfloat16),
            pltpu.VMEM((SHARE, VEC, WIDTH), f32),
            pltpu.SMEM((SLOTS,), i32),
            pltpu.SMEM((SLOTS,), i32),
            pltpu.VMEM((1, SLOTS), i32),
            pltpu.VMEM((1, SLOTS), i32),
            pltpu.SMEM((1,), i32),
            pltpu.VMEM((WINDOW * SHARE, VEC, WIDTH), f32),
            pltpu.VMEM((WINDOW * SHARE, VEC, WIDTH), f32),
            pltpu.VMEM((KEYS, 2, SHARE, VEC, WIDTH), f32),
            pltpu.VMEM((LINE, SHARE, VEC, WIDTH), f32),
            pltpu.VMEM((2 * PLANE, ROWS, WIDTH), f32),
            pltpu.VMEM((LINE, ROWS, WIDTH), f32),
            pltpu.VMEM((SLOTS * VEC, WIDTH), f32),
            pltpu.VMEM((SLOTS * VEC, WIDTH), f32),
            pltpu.VMEM((2, PAD * VEC, WIDTH), f32),
            pltpu.VMEM((2 * GROUP, ROWS, WIDTH), f32),
            pltpu.VMEM((KEYS, 2, ROWS, WIDTH), f32),
            pltpu.VMEM((2 * KEYS + LINE, ROWS, WIDTH), f32),
            pltpu.VMEM((VEC, WIDTH), f32),
            pltpu.VMEM((2, 1, WIDTH), f32),
            pltpu.VMEM((LINE, 1, WIDTH), f32),
            pltpu.VMEM((PLANE, 1, WIDTH), f32),
            dma((7,)),
            dma,
            dma((KEYS, 2)),
            dma,
            dma,
            dma((LINE,)),
            dma,
            dma((2,)),
            dma,
            dma,
            dma,
            dma,
            dma,
            dma,
            dma,
            dma((2,)),
            dma((2,)),
        ],
        compiler_params=pltpu.CompilerParams(
            collective_id=0, has_side_effects=True, vmem_limit_bytes=60 * 1024 * 1024
        ),
    )(
        tiles, tile_rows, tile_cols, tile_rows.reshape(1, SLOTS), tile_cols.reshape(1, SLOTS),
        counts, block_vectors,
    )
    return image, grams[:, :VEC], grams[:, VEC:2 * VEC]


def solution(mesh):
    placed = (P("tri", None, None), P("tri"), P("tri"), P("tri"), P("tri", None, None))
    return jax.shard_map(
        per_device,
        mesh=mesh,
        in_specs=placed,
        out_specs=(P("tri", None, None), P(), P()),
        check_vma=False,
    )
```

```python
import jax
import jax.numpy as jnp
from jax import lax
from jax.experimental import pallas as pl
from jax.experimental.pallas import tpu as pltpu
from jax.sharding import PartitionSpec as P

MESH = pl.DeviceIdType.MESH
SEGS = 22
TILES = 1024
SHARE = 4
VEC = 8
WIDTH = 128
ROWS = SHARE * VEC
SLOTS = 32
WINDOW = 13
PAD = 64
BLOCKS = SEGS * (SEGS + 1) // 2
DEVICES = 256
LOW_SCALE, LOW_SHIFT = 2979, 6
GROUP = 8
LINE = 8
PLANE = 32
ROWS_AT = (4, 2, 2, 2)
KEYS = 4
NT_DIMS = (((1,), (1,)), ((), ()))
NN_DIMS = (((1,), (0,)), ((), ()))


def seg_low(s):
    return (s * LOW_SCALE) >> LOW_SHIFT


def seg_of(t):
    return ((t + 1) * SEGS - 1) >> 10


def first_share(s):
    return seg_low(s) >> 2


def shares(s):
    return ((seg_low(s + 1) - 1) >> 2) - first_share(s) + 1


def tri(s):
    return (s * (s + 1)) >> 1


def row_of(d, low=0, high=DEVICES):
    marks = [m * (m + 1) // 2 for m in range(1, SEGS)]
    row = sum(m <= low for m in marks)
    for m in marks:
        if low < m < high:
            row = row + (d >= m).astype(jnp.int32)
    return row


def first_group(s):
    return tri(s) >> 3


def groups_of(s):
    return ((tri(s) + s - 1) >> 3) - first_group(s) + 1


def split(a):
    hi = a.astype(jnp.bfloat16)
    lo = (a - hi.astype(jnp.float32)).astype(jnp.bfloat16)
    return hi, lo


def kernel(
    tiles_ref, rows_hbm, cols_hbm, rows_hbm2, cols_hbm2, count_hbm, x_hbm,
    image_ref, grams_ref,
    tile_buf, hi_buf, lo_buf, x_ref, rows_ref, cols_ref, rows_vec, cols_vec, count_ref,
    x_row, x_col, relay_buf, line_buf, col_buf, col_sum, row_terms, col_terms, contrib, part_buf, part_sum, arrived,
    gram_tile, gram_own, gram_a, gram_b,
    in_sem, relay_send, relay_recv, pass_send, line_send, line_recv, spread_send, gather_recv,
    part_send, part_recv, sum_send, col_send, col_recv, back_send, arrive_recv, gram_send, gram_recv,
):
    me = lax.axis_index("tri")
    residue = me & 7
    group = me >> 3
    base = group * GROUP
    works = me < BLOCKS
    row = row_of(me)
    col = jnp.minimum(me - tri(row), row)
    off_diagonal = jnp.logical_and(works, row > col)
    on_diagonal = jnp.logical_and(works, row == col)
    top = row_of(base)
    rows_here = row_of(jnp.minimum(base + GROUP - 1, BLOCKS - 1)) - top + 1
    seg_a = seg_of(SHARE * me)
    seg_b = seg_of(SHARE * me + SHARE - 1)
    two = seg_b > seg_a

    loads = [
        pltpu.make_async_copy(src, dst, in_sem.at[n])
        for n, (src, dst) in enumerate((
            (x_hbm, x_ref), (tiles_ref, tile_buf), (rows_hbm, rows_ref), (cols_hbm, cols_ref),
            (rows_hbm2, rows_vec), (cols_hbm2, cols_vec), (count_hbm, count_ref),
        ))
    ]
    def loop(n, body):
        def step(i, _):
            body(i)
            return 0

        lax.fori_loop(0, n, step, 0)

    def owned(body):
        body(seg_a, 0)

        @pl.when(two)
        def _():
            body(seg_b, 1)

    def span(s):
        low = jnp.maximum(tri(s), base)
        return low, jnp.minimum(tri(s) + s, base + GROUP) - low

    def relayed(body):
        def each(n):
            s = top + n
            start = (residue - first_share(s)) & 7
            for turn in range(2):
                p = start + GROUP * turn

                @pl.when(jnp.logical_and(p < shares(s), span(s)[1] > 0))
                def _():
                    body(s, p, s & 3, turn)

        loop(rows_here, each)

    def members(s, body):
        low, count = span(s)
        loop(count, lambda i: body(low + i))

    def send(src, dst, send_sem, recv_sem, dev):
        def remote():
            pltpu.make_async_remote_copy(
                src_ref=src, dst_ref=dst, send_sem=send_sem, recv_sem=recv_sem,
                device_id=(dev,), device_id_type=MESH,
            ).start()

        def local():
            pltpu.make_async_copy(src, dst, recv_sem).start()

        lax.cond(dev != me, remote, local)

    def sent(src, send_sem, dev):
        @pl.when(dev != me)
        def _():
            pltpu.make_async_copy(src, src, send_sem).wait()

    def landed(dst, recv_sem):
        pltpu.make_async_copy(dst, dst, recv_sem).wait()

    def all_landed(held, n, limit, recv_sem):
        def narrow(low, high):
            if high - low > 1:
                mid = (low + high) // 2
                lax.cond(n < mid, lambda: narrow(low, mid), lambda: narrow(mid, high))
            elif low:
                landed(held.at[pl.ds(0, low)], recv_sem)

        narrow(0, limit + 1)

    barrier = pltpu.get_barrier_semaphore()

    def greet(dev):
        @pl.when(dev != me)
        def _():
            pl.semaphore_signal(barrier, inc=1, device_id=(dev,), device_id_type=MESH)

    z, y = group & 7, me >> 6

    def rank_of(dev):
        return ((dev >> 6) << 3) + (dev & 7)

    def line(zz):
        return (y * LINE + zz) * GROUP + residue

    def plane(q):
        return ((q >> 3) * LINE + z) * GROUP + (q & 7)

    relayed(lambda s, p, key, turn: greet(first_share(s) + p))
    for dz in (4, 3, 5, 2, 6, 1, 7):
        pl.semaphore_signal(barrier, inc=1, device_id=(line((z + dz) & 7),), device_id_type=MESH)
    def hops(m):
        return [0, 1, 2, 1][m >> 3] + [0, 1, 2, 1][(m >> 1) & 3]

    far_first = sorted(range(1, PLANE), key=hops, reverse=True)
    for m in far_first:
        pl.semaphore_signal(
            barrier, inc=1, device_id=(plane(rank_of(me) ^ m),), device_id_type=MESH
        )
    def greeters(s):
        mine = jnp.logical_and(group >= first_group(s), group < first_group(s) + groups_of(s))
        return groups_of(s) - jnp.where(mine, 1, 0)

    pl.semaphore_wait(barrier, LINE + PLANE - 2 + greeters(seg_a) + jnp.where(two, greeters(seg_b), 0))

    def near_first(n):
        return (z + jnp.where((n & 1) == 1, (n + 1) >> 1, LINE - (n >> 1))) & 7

    def at_my_z(s, k, first, low):
        return jnp.logical_and(((first + s - low) >> 3) == 0, s <= k)

    def owned_by(zz):
        owner = line(zz)
        a = seg_of(SHARE * owner)
        return owner, a, seg_of(SHARE * owner + SHARE - 1) - a + 1

    def targets(zz, body):
        owner, a, count = owned_by(zz)

        def one(w):
            s = a + w
            p = owner - first_share(s)
            for k, first, low in here:
                @pl.when(at_my_z(s, k, first, low))
                def _(first=first):
                    body(first + s, s, p)

        loop(count, one)

    def count_targets(zz, total):
        _owner, a, count = owned_by(zz)

        def one(w, total):
            for k, first, low in here:
                total = total + at_my_z(a + w, k, first, low).astype(jnp.int32)
            return total

        return lax.fori_loop(0, count, one, total)

    def to_line(n):
        zz = near_first(n)
        send(x_hbm, line_buf.at[z], line_send, line_recv.at[z], line(zz))

    def spread(start):
        def each(n):
            zz = near_first(n)
            src = line_buf.at[zz]
            if start:
                landed(src, line_recv.at[zz])

            def body(dev, s, p):
                if start:
                    dst = x_col.at[pl.ds(p * SHARE, SHARE)]
                    send(src, dst, spread_send, gather_recv.at[1], dev)
                else:
                    sent(src, spread_send, dev)

            targets(zz, body)

        loop(LINE, each)

    def to_relays(start):
        def body(s, w):
            turn = (me - first_share(s)) >> 3
            dst, sem = relay_buf.at[s & 3, turn], relay_recv.at[s & 3, turn]

            def each(n):
                dev = (first_group(s) + n) * GROUP + residue
                if start:
                    send(x_hbm, dst, relay_send, sem, dev)
                else:
                    sent(x_hbm, relay_send, dev)

            loop(groups_of(s), each)

        return body

    loop(LINE, to_line)
    owned(to_relays(True))

    for load in loads:
        load.start()

    here = []
    for yy in (2, 1, 3, 0):
        low = yy * 64 + z * GROUP
        first_row = row_of(low, yy * 64, yy * 64 + 64)
        for k in [first_row + i for i in range(ROWS_AT[yy])]:
            here.append((k, jnp.where(k < SEGS, tri(k), 2 * DEVICES), low))

    for load in loads:
        load.wait()

    def split_tile(k):
        hi, lo = split(tile_buf[k])
        hi_buf[k] = hi
        lo_buf[k] = lo

    loop(SLOTS, split_tile)

    def pass_on(start):
        def body(s, p, key, turn):
            src = relay_buf.at[key, turn]
            dst = x_row.at[pl.ds(p * SHARE, SHARE)]
            if start:
                landed(src, relay_recv.at[key, turn])

            def each(dev):
                if start:
                    send(src, dst, pass_send, gather_recv.at[0], dev)
                else:
                    sent(src, pass_send, dev)

            members(s, each)

        return body

    spread(True)
    relayed(pass_on(True))

    def wait_rows(s, held, recv_sem):
        for n in (WINDOW - 1, WINDOW):
            @pl.when(shares(s) == n)
            def _():
                landed(held.at[pl.ds(0, n * SHARE)], recv_sem)

    row_base = SHARE * first_share(row)
    col_base = SHARE * first_share(col)

    def multiply(held, ids, origin, terms, axis, dims):
        def one(k):
            hi, lo = split(held[jnp.clip(ids[k] - origin, 0, WINDOW * SHARE - 1)])
            both = jnp.concatenate([hi, lo], axis=0)
            out = lax.dot_general(
                jnp.concatenate([both, both], axis=1),
                jnp.concatenate([hi_buf[k], lo_buf[k]], axis=axis), dims,
                preferred_element_type=jnp.float32,
            )
            terms[pl.ds(pl.multiple_of(k * VEC, VEC), VEC), :] = out[:VEC] + out[VEC:]

        def several(n):
            for u in range(8):
                one(8 * n + u)

        loop(SLOTS // 8, several)

    def reduce(vec, origin, terms, which):
        live = lax.broadcasted_iota(jnp.int32, (PAD, SLOTS), 1) < count_ref[0]
        place = lax.broadcasted_iota(jnp.int32, (PAD, SLOTS), 0)
        hit = jnp.logical_and(place == vec[...] - origin, live)
        hot = hit.astype(jnp.float32).astype(jnp.bfloat16)
        hot = jnp.concatenate([hot, hot], axis=1)
        for v in range(VEC):
            hi, lo = split(terms[pl.ds(v, SLOTS, stride=VEC), :])
            contrib[which, pl.ds(v, PAD, stride=VEC), :] = lax.dot_general(
                hot, jnp.concatenate([hi, lo], axis=0), NN_DIMS,
                preferred_element_type=jnp.float32,
            )

    def chunk(which, p):
        return contrib.at[which, pl.ds(pl.multiple_of(p * ROWS, ROWS), ROWS), :]

    def row_parts(p):
        turn = p >> 3
        send(
            chunk(0, p), part_buf.at[turn * GROUP + residue], part_send, part_recv,
            base + ((first_share(row) + p) & 7),
        )

    def all_sent(which, s, same_y, sem):
        n = shares(s)
        for turn in range(2):
            p = ((residue - first_share(s)) & 7) + GROUP * turn
            mine = p < shares(s)
            if same_y:
                mine = jnp.logical_and(mine, ((first_share(s) + p) >> 6) == y)
            n = n - mine.astype(jnp.int32)
        for count in range(WINDOW - 3, WINDOW + 1):
            @pl.when(n == count)
            def _():
                landed(contrib.at[which, pl.ds(0, count * ROWS), :], sem)

    def place_of(owner, s):
        return jnp.where(seg_of(SHARE * owner) == s, 0, 1)

    def col_parts(p):
        owner = first_share(col) + p
        at = rank_of(me) * 2 + (p >> 3)
        dev = (((owner >> 6) << 3) + z) * GROUP + (owner & 7)
        send(chunk(1, p), col_buf.at[at], col_send, col_recv, dev)

    @pl.when(works)
    def _():
        wait_rows(col, x_col, gather_recv.at[1])
        multiply(x_col, cols_ref, col_base, row_terms, 1, NT_DIMS)
        reduce(rows_vec, row_base, row_terms, 0)

        @pl.when(off_diagonal)
        def _():
            loop(shares(row), row_parts)
            wait_rows(row, x_row, gather_recv.at[0])
            multiply(x_row, rows_ref, row_base, col_terms, 0, NN_DIMS)

        @pl.when(on_diagonal)
        def _():
            multiply(x_col, rows_ref, row_base, col_terms, 0, NN_DIMS)

        reduce(cols_vec, col_base, col_terms, 1)

        @pl.when(on_diagonal)
        def _():
            contrib[1] = contrib[0] + contrib[1]

        loop(shares(col), col_parts)

    landed(line_buf.at[pl.ds(0, LINE - 1)], line_send)
    owned(to_relays(False))
    spread(False)
    relayed(pass_on(False))

    def add_parts(start):
        def body(s, p, key, turn):
            owner = first_share(s) + p
            src = part_sum.at[key, turn]
            if start:
                low, count = span(s)

                def each(i, total):
                    rank = (low + i) & 7
                    return total + part_buf[turn * GROUP + rank]

                part_sum[key, turn] = lax.fori_loop(
                    0, count, each, jnp.zeros((ROWS, WIDTH), jnp.float32)
                )
                at = place_of(owner, s) * KEYS + group - first_group(s)
                send(src, arrived.at[at], sum_send, arrive_recv, owner)
            else:
                sent(src, sum_send, owner)

        return body

    def add_cols(n):
        zz = near_first(LINE - 1 - n)
        col_sum[zz] = jnp.zeros((ROWS, WIDTH), jnp.float32)

        def body(dev, s, p):
            at = rank_of(dev) * 2 + (p >> 3)
            col_sum[zz] = col_sum[zz] + col_buf[at]

        targets(zz, body)
        at = 2 * KEYS + z
        send(col_sum.at[zz], arrived.at[at], back_send, arrive_recv, line(zz))

    def parts_of(n, total):
        s = top + n
        start = (residue - first_share(s)) & 7
        turns = (start < shares(s)).astype(jnp.int32) + (start + GROUP < shares(s)).astype(jnp.int32)
        return total + turns * jnp.maximum(span(s)[1], 0)

    n_parts = lax.fori_loop(0, rows_here, parts_of, 0)
    n_cols = lax.fori_loop(0, LINE, count_targets, 0)
    all_landed(part_buf, n_parts, 2 * GROUP, part_recv)
    relayed(add_parts(True))
    all_landed(col_buf, n_cols, 2 * PLANE, col_recv)
    loop(LINE, add_cols)

    def each(at, total):
        return total + arrived[at]

    def collect(w, s, total):
        return lax.fori_loop(w * KEYS, w * KEYS + groups_of(s), each, total)

    n_arrived = LINE + groups_of(seg_a) + jnp.where(two, groups_of(seg_b), 0)
    all_landed(arrived, n_arrived, 2 * KEYS + LINE, arrive_recv)

    def put(total):
        for t in range(SHARE):
            image_ref[t] = total[t * VEC:(t + 1) * VEC]

    total = collect(0, seg_a, jnp.zeros((ROWS, WIDTH), jnp.float32))
    put(lax.fori_loop(2 * KEYS, 2 * KEYS + LINE, each, total))

    @pl.when(two)
    def _():
        put(collect(1, seg_b, jnp.concatenate([image_ref[t] for t in range(SHARE)], axis=0)))

    def flat(ref):
        return jnp.concatenate([ref[t] for t in range(SHARE)], axis=1)

    image = flat(image_ref)
    left = jnp.concatenate(split(jnp.concatenate([flat(x_ref), image], axis=0)), axis=0)
    both = lax.dot_general(
        jnp.concatenate([left, left], axis=1), jnp.concatenate(split(image), axis=1), NT_DIMS,
        preferred_element_type=jnp.float32,
    )
    both = both[:2 * VEC] + both[2 * VEC:]
    gram_tile[...] = jnp.zeros((VEC, WIDTH), jnp.float32)
    gram_tile[:, 0:VEC] = both[:VEC]
    gram_tile[:, VEC:2 * VEC] = both[VEC:]
    moved = pltpu.roll(gram_tile[...], 0, 1, stride=2 * VEC, stride_axis=0)
    gram_own[0] = jnp.sum(moved, axis=0, keepdims=True)

    rank = rank_of(me)
    circles = (
        (gram_a, z, LINE, [line((z + dz) & 7) for dz in (4, 3, 5, 2, 6, 1, 7)]),
        (gram_b, rank, PLANE, [plane(rank ^ m) for m in far_first]),
    )
    for n, (buf, rank, size, partners) in enumerate(circles):
        for dev in partners:
            pltpu.make_async_remote_copy(
                src_ref=gram_own.at[n], dst_ref=buf.at[rank], send_sem=gram_send.at[n],
                recv_sem=gram_recv.at[n], device_id=(dev,), device_id_type=MESH,
            ).start()

        buf[rank] = gram_own[n]
        if n == 0:
            relayed(add_parts(False))

            @pl.when(off_diagonal)
            def _():
                all_sent(0, row, False, part_send)

            @pl.when(works)
            def _():
                all_sent(1, col, True, col_send)

            landed(col_sum.at[pl.ds(0, LINE - 1)], back_send)

        landed(buf.at[pl.ds(0, size - 1)], gram_recv.at[n])
        terms = [buf[q] for q in range(size)]
        while len(terms) > 1:
            terms = [a + b for a, b in zip(terms[::2], terms[1::2])]
        if n == 0:
            gram_own[1] = terms[0]
        else:
            out = jnp.broadcast_to(terms[0] * (1.0 / (TILES * WIDTH)), (VEC, WIDTH))
            block = lax.broadcasted_iota(jnp.int32, (VEC, WIDTH), 1) >> 4
            out = jnp.where(block == lax.broadcasted_iota(jnp.int32, (VEC, WIDTH), 0), out, 0.0)
            for shift in (64, 32, 16):
                out = out + pltpu.roll(out, shift, 1)
            grams_ref[...] = out

    for n, (buf, _rank, size, _partners) in enumerate(circles):
        landed(buf.at[pl.ds(0, size - 1)], gram_send.at[n])


def per_device(tiles, tile_rows, tile_cols, counts, block_vectors):
    f32, i32 = jnp.float32, jnp.int32
    vmem = pl.BlockSpec(memory_space=pltpu.VMEM)
    dma = pltpu.SemaphoreType.DMA
    image, grams = pl.pallas_call(
        kernel,
        out_shape=(
            pltpu.VMEM((SHARE, VEC, WIDTH), f32),
            pltpu.VMEM((VEC, WIDTH), f32),
        ),
        in_specs=[pl.BlockSpec(memory_space=pl.ANY)] * 7,
        out_specs=(vmem, vmem),
        scratch_shapes=[
            pltpu.VMEM((SLOTS, WIDTH, WIDTH), f32),
            pltpu.VMEM((SLOTS, WIDTH, WIDTH), jnp.bfloat16),
            pltpu.VMEM((SLOTS, WIDTH, WIDTH), jnp.bfloat16),
            pltpu.VMEM((SHARE, VEC, WIDTH), f32),
            pltpu.SMEM((SLOTS,), i32),
            pltpu.SMEM((SLOTS,), i32),
            pltpu.VMEM((1, SLOTS), i32),
            pltpu.VMEM((1, SLOTS), i32),
            pltpu.SMEM((1,), i32),
            pltpu.VMEM((WINDOW * SHARE, VEC, WIDTH), f32),
            pltpu.VMEM((WINDOW * SHARE, VEC, WIDTH), f32),
            pltpu.VMEM((KEYS, 2, SHARE, VEC, WIDTH), f32),
            pltpu.VMEM((LINE, SHARE, VEC, WIDTH), f32),
            pltpu.VMEM((2 * PLANE, ROWS, WIDTH), f32),
            pltpu.VMEM((LINE, ROWS, WIDTH), f32),
            pltpu.VMEM((SLOTS * VEC, WIDTH), f32),
            pltpu.VMEM((SLOTS * VEC, WIDTH), f32),
            pltpu.VMEM((2, PAD * VEC, WIDTH), f32),
            pltpu.VMEM((2 * GROUP, ROWS, WIDTH), f32),
            pltpu.VMEM((KEYS, 2, ROWS, WIDTH), f32),
            pltpu.VMEM((2 * KEYS + LINE, ROWS, WIDTH), f32),
            pltpu.VMEM((VEC, WIDTH), f32),
            pltpu.VMEM((2, 1, WIDTH), f32),
            pltpu.VMEM((LINE, 1, WIDTH), f32),
            pltpu.VMEM((PLANE, 1, WIDTH), f32),
            dma((7,)),
            dma,
            dma((KEYS, 2)),
            dma,
            dma,
            dma((LINE,)),
            dma,
            dma((2,)),
            dma,
            dma,
            dma,
            dma,
            dma,
            dma,
            dma,
            dma((2,)),
            dma((2,)),
        ],
        compiler_params=pltpu.CompilerParams(
            collective_id=0, has_side_effects=True, vmem_limit_bytes=60 * 1024 * 1024
        ),
    )(
        tiles, tile_rows, tile_cols, tile_rows.reshape(1, SLOTS), tile_cols.reshape(1, SLOTS),
        counts, block_vectors,
    )
    return image, grams[:, :VEC], grams[:, VEC:2 * VEC]


def solution(mesh):
    placed = (P("tri", None, None), P("tri"), P("tri"), P("tri"), P("tri", None, None))
    return jax.shard_map(
        per_device,
        mesh=mesh,
        in_specs=placed,
        out_specs=(P("tri", None, None), P(), P()),
        check_vma=False,
    )
```

```python
import jax
import jax.numpy as jnp
from jax import lax
from jax.experimental import pallas as pl
from jax.experimental.pallas import tpu as pltpu
from jax.sharding import PartitionSpec as P

MESH = pl.DeviceIdType.MESH
SEGS = 22
TILES = 1024
SHARE = 4
VEC = 8
WIDTH = 128
ROWS = SHARE * VEC
SLOTS = 32
WINDOW = 13
PAD = 64
BLOCKS = SEGS * (SEGS + 1) // 2
DEVICES = 256
LOW_SCALE, LOW_SHIFT = 2979, 6
GROUP = 8
LINE = 8
PLANE = 32
ROWS_AT = (4, 2, 2, 2)
KEYS = 4
NT_DIMS = (((1,), (1,)), ((), ()))
NN_DIMS = (((1,), (0,)), ((), ()))


def seg_low(s):
    return (s * LOW_SCALE) >> LOW_SHIFT


def seg_of(t):
    return ((t + 1) * SEGS - 1) >> 10


def first_share(s):
    return seg_low(s) >> 2


def shares(s):
    return ((seg_low(s + 1) - 1) >> 2) - first_share(s) + 1


def tri(s):
    return (s * (s + 1)) >> 1


def row_of(d, low=0, high=DEVICES):
    marks = [m * (m + 1) // 2 for m in range(1, SEGS)]
    row = sum(m <= low for m in marks)
    for m in marks:
        if low < m < high:
            row = row + (d >= m).astype(jnp.int32)
    return row


def first_group(s):
    return tri(s) >> 3


def groups_of(s):
    return ((tri(s) + s - 1) >> 3) - first_group(s) + 1


def split(a):
    hi = a.astype(jnp.bfloat16)
    lo = (a - hi.astype(jnp.float32)).astype(jnp.bfloat16)
    return hi, lo


def kernel(
    tiles_ref, rows_hbm, cols_hbm, rows_hbm2, cols_hbm2, count_hbm, x_hbm,
    image_ref, grams_ref,
    tile_buf, hi_buf, lo_buf, x_ref, rows_ref, cols_ref, rows_vec, cols_vec, count_ref,
    x_row, x_col, relay_buf, line_buf, col_buf, col_sum, row_terms, col_terms, contrib, part_buf, part_sum, arrived,
    gram_tile, gram_own, gram_a, gram_b,
    in_sem, relay_send, relay_recv, pass_send, line_send, line_recv, spread_send, gather_recv,
    part_send, part_recv, sum_send, col_send, col_recv, back_send, arrive_recv, gram_send, gram_recv,
):
    me = lax.axis_index("tri")
    residue = me & 7
    group = me >> 3
    base = group * GROUP
    works = me < BLOCKS
    row = row_of(me)
    col = jnp.minimum(me - tri(row), row)
    off_diagonal = jnp.logical_and(works, row > col)
    on_diagonal = jnp.logical_and(works, row == col)
    top = row_of(base)
    rows_here = row_of(jnp.minimum(base + GROUP - 1, BLOCKS - 1)) - top + 1
    seg_a = seg_of(SHARE * me)
    seg_b = seg_of(SHARE * me + SHARE - 1)
    two = seg_b > seg_a

    loads = [
        pltpu.make_async_copy(src, dst, in_sem.at[n])
        for n, (src, dst) in enumerate((
            (x_hbm, x_ref), (tiles_ref, tile_buf), (rows_hbm, rows_ref), (cols_hbm, cols_ref),
            (rows_hbm2, rows_vec), (cols_hbm2, cols_vec), (count_hbm, count_ref),
        ))
    ]
    def loop(n, body):
        def step(i, _):
            body(i)
            return 0

        lax.fori_loop(0, n, step, 0)

    def owned(body):
        body(seg_a, 0)

        @pl.when(two)
        def _():
            body(seg_b, 1)

    def span(s):
        low = jnp.maximum(tri(s), base)
        return low, jnp.minimum(tri(s) + s, base + GROUP) - low

    def relayed(body):
        def each(n):
            s = top + n
            start = (residue - first_share(s)) & 7
            for turn in range(2):
                p = start + GROUP * turn

                @pl.when(jnp.logical_and(p < shares(s), span(s)[1] > 0))
                def _():
                    body(s, p, s & 3, turn)

        loop(rows_here, each)

    def members(s, body):
        low, count = span(s)
        loop(count, lambda i: body(low + i))

    def send(src, dst, send_sem, recv_sem, dev):
        def remote():
            pltpu.make_async_remote_copy(
                src_ref=src, dst_ref=dst, send_sem=send_sem, recv_sem=recv_sem,
                device_id=(dev,), device_id_type=MESH,
            ).start()

        def local():
            pltpu.make_async_copy(src, dst, recv_sem).start()

        lax.cond(dev != me, remote, local)

    def sent(src, send_sem, dev):
        @pl.when(dev != me)
        def _():
            pltpu.make_async_copy(src, src, send_sem).wait()

    def landed(dst, recv_sem):
        pltpu.make_async_copy(dst, dst, recv_sem).wait()

    def all_landed(held, n, limit, recv_sem):
        def narrow(low, high):
            if high - low > 1:
                mid = (low + high) // 2
                lax.cond(n < mid, lambda: narrow(low, mid), lambda: narrow(mid, high))
            elif low:
                landed(held.at[pl.ds(0, low)], recv_sem)

        narrow(0, limit + 1)

    barrier = pltpu.get_barrier_semaphore()

    def greet(dev):
        @pl.when(dev != me)
        def _():
            pl.semaphore_signal(barrier, inc=1, device_id=(dev,), device_id_type=MESH)

    z, y = group & 7, me >> 6

    def rank_of(dev):
        return ((dev >> 6) << 3) + (dev & 7)

    def line(zz):
        return (y * LINE + zz) * GROUP + residue

    def plane(q):
        return ((q >> 3) * LINE + z) * GROUP + (q & 7)

    relayed(lambda s, p, key, turn: greet(first_share(s) + p))
    for dz in (4, 3, 5, 2, 6, 1, 7):
        pl.semaphore_signal(barrier, inc=1, device_id=(line((z + dz) & 7),), device_id_type=MESH)
    def hops(m):
        return [0, 1, 2, 1][m >> 3] + [0, 1, 2, 1][(m >> 1) & 3]

    far_first = sorted(range(1, PLANE), key=hops, reverse=True)
    for m in far_first:
        pl.semaphore_signal(
            barrier, inc=1, device_id=(plane(rank_of(me) ^ m),), device_id_type=MESH
        )
    def greeters(s):
        mine = jnp.logical_and(group >= first_group(s), group < first_group(s) + groups_of(s))
        return groups_of(s) - jnp.where(mine, 1, 0)

    pl.semaphore_wait(barrier, LINE + PLANE - 2 + greeters(seg_a) + jnp.where(two, greeters(seg_b), 0))

    def near_first(n):
        return (z + jnp.where((n & 1) == 1, (n + 1) >> 1, LINE - (n >> 1))) & 7

    def at_my_z(s, k, first, low):
        return jnp.logical_and(((first + s - low) >> 3) == 0, s <= k)

    def owned_by(zz):
        owner = line(zz)
        a = seg_of(SHARE * owner)
        return owner, a, seg_of(SHARE * owner + SHARE - 1) - a + 1

    def targets(zz, body):
        owner, a, count = owned_by(zz)

        def one(w):
            s = a + w
            p = owner - first_share(s)
            for k, first, low in here:
                @pl.when(at_my_z(s, k, first, low))
                def _(first=first):
                    body(first + s, s, p)

        loop(count, one)

    def count_targets(zz, total):
        _owner, a, count = owned_by(zz)

        def one(w, total):
            for k, first, low in here:
                total = total + at_my_z(a + w, k, first, low).astype(jnp.int32)
            return total

        return lax.fori_loop(0, count, one, total)

    def to_line(n):
        zz = near_first(n)
        send(x_hbm, line_buf.at[z], line_send, line_recv.at[z], line(zz))

    def spread(start):
        def each(n):
            zz = near_first(n)
            src = line_buf.at[zz]
            if start:
                landed(src, line_recv.at[zz])

            def body(dev, s, p):
                if start:
                    dst = x_col.at[pl.ds(p * SHARE, SHARE)]
                    send(src, dst, spread_send, gather_recv.at[1], dev)
                else:
                    sent(src, spread_send, dev)

            targets(zz, body)

        loop(LINE, each)

    def to_relays(start):
        def body(s, w):
            turn = (me - first_share(s)) >> 3
            dst, sem = relay_buf.at[s & 3, turn], relay_recv.at[s & 3, turn]

            def each(n):
                dev = (first_group(s) + n) * GROUP + residue
                if start:
                    send(x_hbm, dst, relay_send, sem, dev)
                else:
                    sent(x_hbm, relay_send, dev)

            loop(groups_of(s), each)

        return body

    loop(LINE, to_line)
    owned(to_relays(True))

    for load in loads:
        load.start()

    here = []
    for yy in (2, 1, 3, 0):
        low = yy * 64 + z * GROUP
        first_row = row_of(low, yy * 64, yy * 64 + 64)
        for k in [first_row + i for i in range(ROWS_AT[yy])]:
            here.append((k, jnp.where(k < SEGS, tri(k), 2 * DEVICES), low))

    for load in loads:
        load.wait()

    def split_tile(k):
        hi, lo = split(tile_buf[k])
        hi_buf[k] = hi
        lo_buf[k] = lo

    loop(SLOTS, split_tile)

    def pass_on(start):
        def body(s, p, key, turn):
            src = relay_buf.at[key, turn]
            dst = x_row.at[pl.ds(p * SHARE, SHARE)]
            if start:
                landed(src, relay_recv.at[key, turn])

            def each(dev):
                if start:
                    send(src, dst, pass_send, gather_recv.at[0], dev)
                else:
                    sent(src, pass_send, dev)

            members(s, each)

        return body

    spread(True)
    relayed(pass_on(True))

    def wait_rows(s, held, recv_sem):
        for n in (WINDOW - 1, WINDOW):
            @pl.when(shares(s) == n)
            def _():
                landed(held.at[pl.ds(0, n * SHARE)], recv_sem)

    row_base = SHARE * first_share(row)
    col_base = SHARE * first_share(col)

    def multiply(held, ids, origin, terms, axis, dims):
        def one(k):
            hi, lo = split(held[jnp.clip(ids[k] - origin, 0, WINDOW * SHARE - 1)])
            both = jnp.concatenate([hi, lo], axis=0)
            out = lax.dot_general(
                jnp.concatenate([both, both], axis=1),
                jnp.concatenate([hi_buf[k], lo_buf[k]], axis=axis), dims,
                preferred_element_type=jnp.float32,
            )
            terms[pl.ds(pl.multiple_of(k * VEC, VEC), VEC), :] = out[:VEC] + out[VEC:]

        def several(n):
            for u in range(8):
                one(8 * n + u)

        loop(SLOTS // 8, several)

    def reduce(vec, origin, terms, which):
        live = lax.broadcasted_iota(jnp.int32, (PAD, SLOTS), 1) < count_ref[0]
        place = lax.broadcasted_iota(jnp.int32, (PAD, SLOTS), 0)
        hit = jnp.logical_and(place == vec[...] - origin, live)
        hot = hit.astype(jnp.float32).astype(jnp.bfloat16)
        hot = jnp.concatenate([hot, hot], axis=1)
        for v in range(VEC):
            hi, lo = split(terms[pl.ds(v, SLOTS, stride=VEC), :])
            contrib[which, pl.ds(v, PAD, stride=VEC), :] = lax.dot_general(
                hot, jnp.concatenate([hi, lo], axis=0), NN_DIMS,
                preferred_element_type=jnp.float32,
            )

    def chunk(which, p):
        return contrib.at[which, pl.ds(pl.multiple_of(p * ROWS, ROWS), ROWS), :]

    def row_parts(p):
        turn = p >> 3
        send(
            chunk(0, p), part_buf.at[turn * GROUP + residue], part_send, part_recv,
            base + ((first_share(row) + p) & 7),
        )

    def all_sent(which, s, same_y, sem):
        n = shares(s)
        for turn in range(2):
            p = ((residue - first_share(s)) & 7) + GROUP * turn
            mine = p < shares(s)
            if same_y:
                mine = jnp.logical_and(mine, ((first_share(s) + p) >> 6) == y)
            n = n - mine.astype(jnp.int32)
        for count in range(WINDOW - 3, WINDOW + 1):
            @pl.when(n == count)
            def _():
                landed(contrib.at[which, pl.ds(0, count * ROWS), :], sem)

    def place_of(owner, s):
        return jnp.where(seg_of(SHARE * owner) == s, 0, 1)

    def col_parts(p):
        owner = first_share(col) + p
        at = rank_of(me) * 2 + (p >> 3)
        dev = (((owner >> 6) << 3) + z) * GROUP + (owner & 7)
        send(chunk(1, p), col_buf.at[at], col_send, col_recv, dev)

    @pl.when(works)
    def _():
        wait_rows(col, x_col, gather_recv.at[1])
        multiply(x_col, cols_ref, col_base, row_terms, 1, NT_DIMS)
        reduce(rows_vec, row_base, row_terms, 0)

        @pl.when(off_diagonal)
        def _():
            loop(shares(row), row_parts)
            wait_rows(row, x_row, gather_recv.at[0])
            multiply(x_row, rows_ref, row_base, col_terms, 0, NN_DIMS)

        @pl.when(on_diagonal)
        def _():
            multiply(x_col, rows_ref, row_base, col_terms, 0, NN_DIMS)

        reduce(cols_vec, col_base, col_terms, 1)

        @pl.when(on_diagonal)
        def _():
            contrib[1] = contrib[0] + contrib[1]

        loop(shares(col), col_parts)


    def add_parts(start):
        def body(s, p, key, turn):
            owner = first_share(s) + p
            src = part_sum.at[key, turn]
            if start:
                low, count = span(s)

                def each(i, total):
                    rank = (low + i) & 7
                    return total + part_buf[turn * GROUP + rank]

                part_sum[key, turn] = lax.fori_loop(
                    0, count, each, jnp.zeros((ROWS, WIDTH), jnp.float32)
                )
                at = place_of(owner, s) * KEYS + group - first_group(s)
                send(src, arrived.at[at], sum_send, arrive_recv, owner)
            else:
                sent(src, sum_send, owner)

        return body

    def add_cols(n):
        zz = near_first(LINE - 1 - n)
        col_sum[zz] = jnp.zeros((ROWS, WIDTH), jnp.float32)

        def body(dev, s, p):
            at = rank_of(dev) * 2 + (p >> 3)
            col_sum[zz] = col_sum[zz] + col_buf[at]

        targets(zz, body)
        at = 2 * KEYS + z
        send(col_sum.at[zz], arrived.at[at], back_send, arrive_recv, line(zz))

    def parts_of(n, total):
        s = top + n
        start = (residue - first_share(s)) & 7
        turns = (start < shares(s)).astype(jnp.int32) + (start + GROUP < shares(s)).astype(jnp.int32)
        return total + turns * jnp.maximum(span(s)[1], 0)

    n_parts = lax.fori_loop(0, rows_here, parts_of, 0)
    n_cols = lax.fori_loop(0, LINE, count_targets, 0)
    all_landed(part_buf, n_parts, 2 * GROUP, part_recv)
    relayed(add_parts(True))
    all_landed(col_buf, n_cols, 2 * PLANE, col_recv)
    loop(LINE, add_cols)

    def each(at, total):
        return total + arrived[at]

    def collect(w, s, total):
        return lax.fori_loop(w * KEYS, w * KEYS + groups_of(s), each, total)

    n_arrived = LINE + groups_of(seg_a) + jnp.where(two, groups_of(seg_b), 0)
    all_landed(arrived, n_arrived, 2 * KEYS + LINE, arrive_recv)

    def put(total):
        for t in range(SHARE):
            image_ref[t] = total[t * VEC:(t + 1) * VEC]

    total = collect(0, seg_a, jnp.zeros((ROWS, WIDTH), jnp.float32))
    put(lax.fori_loop(2 * KEYS, 2 * KEYS + LINE, each, total))

    @pl.when(two)
    def _():
        put(collect(1, seg_b, jnp.concatenate([image_ref[t] for t in range(SHARE)], axis=0)))

    def flat(ref):
        return jnp.concatenate([ref[t] for t in range(SHARE)], axis=1)

    image = flat(image_ref)
    both = lax.dot_general(
        jnp.concatenate([flat(x_ref), image], axis=0), image, NT_DIMS,
        precision=lax.Precision.HIGHEST, preferred_element_type=jnp.float32,
    )
    gram_tile[...] = jnp.zeros((VEC, WIDTH), jnp.float32)
    gram_tile[:, 0:VEC] = both[:VEC]
    gram_tile[:, VEC:2 * VEC] = both[VEC:]
    moved = pltpu.roll(gram_tile[...], 0, 1, stride=2 * VEC, stride_axis=0)
    gram_own[0] = jnp.sum(moved, axis=0, keepdims=True)

    rank = rank_of(me)
    circles = (
        (gram_a, z, LINE, [line((z + dz) & 7) for dz in (4, 3, 5, 2, 6, 1, 7)]),
        (gram_b, rank, PLANE, [plane(rank ^ m) for m in far_first]),
    )
    for n, (buf, rank, size, partners) in enumerate(circles):
        for dev in partners:
            pltpu.make_async_remote_copy(
                src_ref=gram_own.at[n], dst_ref=buf.at[rank], send_sem=gram_send.at[n],
                recv_sem=gram_recv.at[n], device_id=(dev,), device_id_type=MESH,
            ).start()

        buf[rank] = gram_own[n]
        if n == 0:
            landed(line_buf.at[pl.ds(0, LINE - 1)], line_send)
            owned(to_relays(False))
            spread(False)
            relayed(pass_on(False))
            relayed(add_parts(False))

            @pl.when(off_diagonal)
            def _():
                all_sent(0, row, False, part_send)

            @pl.when(works)
            def _():
                all_sent(1, col, True, col_send)

            landed(col_sum.at[pl.ds(0, LINE - 1)], back_send)

        landed(buf.at[pl.ds(0, size - 1)], gram_recv.at[n])
        terms = [buf[q] for q in range(size)]
        while len(terms) > 1:
            terms = [a + b for a, b in zip(terms[::2], terms[1::2])]
        if n == 0:
            gram_own[1] = terms[0]
        else:
            out = jnp.broadcast_to(terms[0] * (1.0 / (TILES * WIDTH)), (VEC, WIDTH))
            block = lax.broadcasted_iota(jnp.int32, (VEC, WIDTH), 1) >> 4
            out = jnp.where(block == lax.broadcasted_iota(jnp.int32, (VEC, WIDTH), 0), out, 0.0)
            for shift in (64, 32, 16):
                out = out + pltpu.roll(out, shift, 1)
            grams_ref[...] = out

    for n, (buf, _rank, size, _partners) in enumerate(circles):
        landed(buf.at[pl.ds(0, size - 1)], gram_send.at[n])


def per_device(tiles, tile_rows, tile_cols, counts, block_vectors):
    f32, i32 = jnp.float32, jnp.int32
    vmem = pl.BlockSpec(memory_space=pltpu.VMEM)
    dma = pltpu.SemaphoreType.DMA
    image, grams = pl.pallas_call(
        kernel,
        out_shape=(
            pltpu.VMEM((SHARE, VEC, WIDTH), f32),
            pltpu.VMEM((VEC, WIDTH), f32),
        ),
        in_specs=[pl.BlockSpec(memory_space=pl.ANY)] * 7,
        out_specs=(vmem, vmem),
        scratch_shapes=[
            pltpu.VMEM((SLOTS, WIDTH, WIDTH), f32),
            pltpu.VMEM((SLOTS, WIDTH, WIDTH), jnp.bfloat16),
            pltpu.VMEM((SLOTS, WIDTH, WIDTH), jnp.bfloat16),
            pltpu.VMEM((SHARE, VEC, WIDTH), f32),
            pltpu.SMEM((SLOTS,), i32),
            pltpu.SMEM((SLOTS,), i32),
            pltpu.VMEM((1, SLOTS), i32),
            pltpu.VMEM((1, SLOTS), i32),
            pltpu.SMEM((1,), i32),
            pltpu.VMEM((WINDOW * SHARE, VEC, WIDTH), f32),
            pltpu.VMEM((WINDOW * SHARE, VEC, WIDTH), f32),
            pltpu.VMEM((KEYS, 2, SHARE, VEC, WIDTH), f32),
            pltpu.VMEM((LINE, SHARE, VEC, WIDTH), f32),
            pltpu.VMEM((2 * PLANE, ROWS, WIDTH), f32),
            pltpu.VMEM((LINE, ROWS, WIDTH), f32),
            pltpu.VMEM((SLOTS * VEC, WIDTH), f32),
            pltpu.VMEM((SLOTS * VEC, WIDTH), f32),
            pltpu.VMEM((2, PAD * VEC, WIDTH), f32),
            pltpu.VMEM((2 * GROUP, ROWS, WIDTH), f32),
            pltpu.VMEM((KEYS, 2, ROWS, WIDTH), f32),
            pltpu.VMEM((2 * KEYS + LINE, ROWS, WIDTH), f32),
            pltpu.VMEM((VEC, WIDTH), f32),
            pltpu.VMEM((2, 1, WIDTH), f32),
            pltpu.VMEM((LINE, 1, WIDTH), f32),
            pltpu.VMEM((PLANE, 1, WIDTH), f32),
            dma((7,)),
            dma,
            dma((KEYS, 2)),
            dma,
            dma,
            dma((LINE,)),
            dma,
            dma((2,)),
            dma,
            dma,
            dma,
            dma,
            dma,
            dma,
            dma,
            dma((2,)),
            dma((2,)),
        ],
        compiler_params=pltpu.CompilerParams(
            collective_id=0, has_side_effects=True, vmem_limit_bytes=60 * 1024 * 1024
        ),
    )(
        tiles, tile_rows, tile_cols, tile_rows.reshape(1, SLOTS), tile_cols.reshape(1, SLOTS),
        counts, block_vectors,
    )
    return image, grams[:, :VEC], grams[:, VEC:2 * VEC]


def solution(mesh):
    placed = (P("tri", None, None), P("tri"), P("tri"), P("tri"), P("tri", None, None))
    return jax.shard_map(
        per_device,
        mesh=mesh,
        in_specs=placed,
        out_specs=(P("tri", None, None), P(), P()),
        check_vma=False,
    )
```
